32 devices in a mesh: cases: 2 (over y), runs: 16 (over z, x, core).
Axes of the slice: x: 2, y: 2, z: 4, core: 2. Of those that a mesh axis runs over, the one named last changes fastest.
Arguments:
- run_inputs: float32 [2048, 24], P(('cases', 'runs')), parts along dimension 0, may hold values from -3 to 3
- term_codes: int32 [4096, 4], replicated, may hold values from 0 to 119
- weight_levels: int32 [4096], replicated, may hold values from 0 to 3
- correlations: bfloat16 [8192, 1024], P(('cases', 'runs')), parts along dimension 0, may hold values from -32 to 32
- slab_modes: bfloat16 [4096, 1024], P('cases'), parts along dimension 0, may hold values from -0.1875 to 0.1875
- cell_map: int32 [2048], replicated, may hold values from 0 to 2047, each once
Outputs:
- coefficients: float32 [8192, 1024], P(('cases', 'runs')), parts along dimension 0
- lifted: bfloat16 [8192, 2048], P(('cases', 'runs')), parts along dimension 0
The draws below stay inside these ranges and needn't reach their ends.
There are 2 independent parts, one for each index of `cases`. The reference program is written for one: setup_inputs(seed, part) draws one part's arguments, and reference() takes and returns one part's arrays. A program takes and returns all parts, laid end to end along the dimension named above; an argument that names none is the same for every part. Nothing has to cross between parts.
All inputs are finite; a program needn't handle non-finite values.
Results may differ from the reference program's by a relative error of at most 0.0067.
Values may be sent and summed in bfloat16 or wider, within the bound.
No kernel may reach another device: no remote copies, remote signals or barrier semaphores. Data moves between devices by JAX's collectives and lax.ppermute only.
A program may use at most 64 MiB of HBM per device.

```python
import math
import jax
import jax.numpy as jnp
from jax import lax

P_SIZE = 4096
M = 1024
DIM = 24
SLOTS = 4
RUN_DEV = 64
CELLS = 2048
RUNS = 1024
CODES = 120
N_RUNS = 16


def draw_correlations(key, part):
    keys = jax.random.split(key, 3)
    row_scale = jnp.exp(jax.random.uniform(keys[0], (P_SIZE, 1), minval=jnp.log(0.3), maxval=jnp.log(3.0)))
    column_scale = jnp.exp(jax.random.uniform(keys[2], (1, M), minval=jnp.log(0.5), maxval=jnp.log(2.0)))
    noise = jnp.clip(jax.random.normal(keys[1], (P_SIZE, M)), -4.0, 4.0)
    values = row_scale * column_scale * noise
    return values.astype(jnp.float32).astype(jnp.bfloat16)


def set_ends(entries, key, smallest, top_value):
    longest = entries.shape.index(max(entries.shape))
    spots = []
    for shift in (0, 1):
        where = [jax.random.randint(jax.random.fold_in(key, axis), (), 0, length) for axis, length in enumerate(entries.shape)]
        where[longest] = (where[longest] + shift) % entries.shape[longest]
        spots.append(tuple(where))
    return entries.at[spots[0]].set(smallest).at[spots[1]].set(top_value)


def shard_levels(rng, dims, cuts, low, largest):
    level = 1.0
    for position, shards_of in cuts:
        draws = jax.random.uniform(jax.random.fold_in(jax.random.fold_in(rng, 6), position), (shards_of,), jnp.float32, low / len(cuts), largest / len(cuts))
        level = level * jnp.repeat(jnp.exp(draws), dims[position] // shards_of).reshape((-1,) + (1,) * (len(dims) - 1 - position))
    return level


def gaussian(key, shape, spread, most, shards=(), dtype=jnp.bfloat16):
    drawn = spread * jax.random.normal(key, shape, jnp.float32)
    if shards:
        drawn = drawn * shard_levels(key, shape, shards, -0.22, 0.18)
    return jnp.clip(drawn, -most, most).astype(dtype)


def setup_inputs(seed: int = 0, part: int = 0) -> dict:
    key_list = jax.random.split(jax.random.key(seed), 7)
    own_keys = jax.random.split(jax.random.fold_in(key_list[6], part), 7)
    run_inputs = gaussian(own_keys[0], (RUNS, DIM), 1.0, 3.0, ((0, 16),), jnp.float32)
    term_codes = set_ends(jax.random.randint(key_list[1], (P_SIZE, SLOTS), 0, CODES), jax.random.fold_in(key_list[1], 1), 0, CODES - 1).astype(jnp.int32)
    weight_levels = set_ends(jax.random.randint(key_list[2], (P_SIZE,), 0, 4), jax.random.fold_in(key_list[2], 1), 0, 3).astype(jnp.int32)
    correlations = draw_correlations(jax.random.fold_in(jax.random.fold_in(key_list[6], part), 71), part)
    slab_modes = gaussian(own_keys[4], (CELLS, M), M ** -0.5, 0.1875)
    cell_map = jax.random.permutation(key_list[5], CELLS).astype(jnp.int32)
    return {"run_inputs": run_inputs, "term_codes": term_codes, "weight_levels": weight_levels, "correlations": correlations, "slab_modes": slab_modes, "cell_map": cell_map}


STEP = 0.5
LAMBDA_FRACTION = 0.05
EPSILON = 1e-06
ROOT_TWO = math.sqrt(2.0)
ROOT_SIX = math.sqrt(6.0)
ROOT_TWENTYFOUR = math.sqrt(24.0)

def hermite_table(points):
    squared = points * points
    columns = [jnp.ones_like(points), points, (squared - 1.0) / ROOT_TWO, points * (squared - 3.0) / ROOT_SIX, (squared * squared - 6.0 * squared + 3.0) / ROOT_TWENTYFOUR]
    return jnp.stack(columns, axis=-1).reshape(points.shape[0], -1)

def basis(points, codes):
    hermite = hermite_table(points)
    product = jnp.take(hermite, codes[:, 0], axis=1)
    for column in range(1, codes.shape[1]):
        product = product * jnp.take(hermite, codes[:, column], axis=1)
    return product.astype(jnp.bfloat16)

def shrink(values, limits):
    length = jnp.sqrt(lax.optimization_barrier(jnp.sum(values * values, axis=1, keepdims=True)) + EPSILON)
    return values * jnp.maximum(0.0, 1.0 - limits[:, None] / length)

def reference(run_inputs, term_codes, weight_levels, correlations, slab_modes, cell_map):
    weights = jnp.exp2(weight_levels.astype(jnp.float32))
    corr = correlations.astype(jnp.float32)
    penalty = LAMBDA_FRACTION * jnp.max(jnp.sqrt(lax.optimization_barrier(jnp.sum(corr * corr, axis=1))) / weights)
    first = shrink(STEP * corr, STEP * penalty * weights)
    first_wide = first.astype(jnp.bfloat16).astype(jnp.float32)
    blocks = run_inputs.reshape(N_RUNS, RUN_DEV, DIM)

    def accumulate(running, points):
        design = basis(points, term_codes).astype(jnp.float32)
        fitted = jnp.dot(design, first_wide, preferred_element_type=jnp.float32).astype(jnp.bfloat16)
        return (running + jnp.dot(design.T, fitted.astype(jnp.float32), preferred_element_type=jnp.float32), None)
    summed, _ = lax.scan(accumulate, jnp.zeros((P_SIZE, M), jnp.float32), blocks)
    gradient = summed / RUNS - corr
    coefficients = shrink(first - STEP * gradient, STEP * penalty * weights)
    modes = jnp.take(slab_modes, cell_map, axis=0).astype(jnp.float32)
    coeff_wide = coefficients.astype(jnp.bfloat16).astype(jnp.float32)
    lifted = jnp.dot(coeff_wide, modes.T, preferred_element_type=jnp.float32).astype(jnp.bfloat16)
    return (coefficients, lifted)
```

```python
import functools
import math

import jax
import jax.numpy as jnp
from jax import lax
from jax.experimental import pallas as pl
from jax.experimental.pallas import tpu as pltpu
from jax.sharding import PartitionSpec as P

STEP = 0.5
LAMBDA_FRACTION = 0.05
EPSILON = 1e-06
DEGREES = 5
LANES = 128
ROOT_TWO = math.sqrt(2.0)
ROOT_SIX = math.sqrt(6.0)
ROOT_TWENTYFOUR = math.sqrt(24.0)
MIB = 1 << 20


def round_up(value, multiple):
    return -(-value // multiple) * multiple


def prepare_kernel(corr_ref, points_ref, turned_ref, packet_ref):
    turned = corr_ref[...].astype(jnp.float32).T
    turned_ref[...] = turned.astype(jnp.bfloat16)
    squares = jnp.sum(turned * turned, axis=0, keepdims=True)
    dim, runs = points_ref.shape
    packet_ref[...] = jnp.zeros_like(packet_ref)
    packet_ref[0:dim, 0:runs] = points_ref[...]
    for part in range(squares.shape[1] // LANES):
        packet_ref[dim + part : dim + part + 1, :] = squares[
            :, part * LANES : (part + 1) * LANES
        ]


def hermite_columns(points):
    squared = points * points
    return jnp.concatenate(
        [
            jnp.ones_like(points),
            points,
            (squared - 1.0) / ROOT_TWO,
            points * (squared - 3.0) / ROOT_SIX,
            (squared * squared - 6.0 * squared + 3.0) / ROOT_TWENTYFOUR,
        ],
        axis=0,
    )


def design_kernel(dim, run_count, packets_ref, codes_ref, design_ref, table):
    devices = packets_ref.shape[0]
    half = table.shape[1] // 2

    @pl.when(pl.program_id(0) == 0)
    def _():
        per = LANES // run_count
        for group in range(devices // per):
            points = jnp.concatenate(
                [
                    packets_ref[group * per + i, 0:dim, 0:run_count]
                    for i in range(per)
                ],
                axis=1,
            )
            columns = hermite_columns(points)
            columns = jnp.concatenate(
                [
                    columns,
                    jnp.zeros((half - columns.shape[0], LANES), jnp.float32),
                ],
                axis=0,
            ).T
            high = columns.astype(jnp.bfloat16)
            low = (columns - high.astype(jnp.float32)).astype(jnp.bfloat16)
            rows = slice(group * LANES, (group + 1) * LANES)
            table[rows, 0:half] = high
            table[rows, half : 2 * half] = low

    codes = codes_ref[...]
    spots = (codes % DEGREES) * dim + codes // DEGREES
    terms = codes.shape[1]
    row = lax.broadcasted_iota(jnp.int32, (half, terms), 0)
    product = None
    for slot in range(codes.shape[0]):
        chosen = jnp.where(row == spots[slot : slot + 1, :], 1.0, 0.0).astype(
            jnp.bfloat16
        )
        chosen = jnp.concatenate([chosen, chosen], axis=0)
        factor = jnp.dot(table[...], chosen, preferred_element_type=jnp.float32)
        product = factor if product is None else product * factor
    design_ref[...] = product.astype(jnp.bfloat16)


def penalty_rows(dim, term_count, packets_ref, levels_ref):
    squares = jnp.concatenate(
        [
            packets_ref[i, dim + part : dim + part + 1, :]
            for i in range(packets_ref.shape[0])
            for part in range(term_count // LANES)
        ],
        axis=1,
    )
    weights = jnp.exp2(levels_ref[...].astype(jnp.float32))
    ratio = jnp.max(jnp.sqrt(squares) / weights, axis=1, keepdims=True)
    return squares, weights, LAMBDA_FRACTION * ratio


def shrink_factor(squares, limits):
    return jnp.maximum(0.0, 1.0 - limits / jnp.sqrt(squares + EPSILON))


def fit_kernel(
    dim, total_runs, packets_ref, levels_ref, corr_ref, design_ref, summed_ref, scale_ref
):
    devices, _, term_count = corr_ref.shape
    squares, weights, penalty = penalty_rows(dim, term_count, packets_ref, levels_ref)
    limits = STEP * penalty * weights
    factor = shrink_factor(STEP * STEP * squares, limits)
    scale_ref[0:1, :] = factor
    scale_ref[1:2, :] = limits
    fitted = None
    for i in range(devices):
        terms = slice(i * term_count, (i + 1) * term_count)
        first = STEP * corr_ref[i].astype(jnp.float32) * factor[:, terms]
        part = lax.dot_general(
            first.astype(jnp.bfloat16),
            design_ref[:, terms],
            (((1,), (1,)), ((), ())),
            preferred_element_type=jnp.float32,
        )
        fitted = part if fitted is None else fitted + part
    fitted = fitted.astype(jnp.bfloat16)
    for i in range(devices):
        terms = slice(i * term_count, (i + 1) * term_count)
        summed = jnp.dot(
            fitted, design_ref[:, terms], preferred_element_type=jnp.float32
        )
        summed_ref[i] = (summed / total_runs).astype(jnp.bfloat16)


def finish_kernel(summed_ref, corr_ref, scale_ref, out_ref, half_ref):
    corr = corr_ref[...].astype(jnp.float32)
    first = STEP * corr * scale_ref[0:1, :]
    gradient = summed_ref[...].astype(jnp.float32) - corr
    moved = first - STEP * gradient
    squares = jnp.sum(moved * moved, axis=0, keepdims=True)
    values = (moved * shrink_factor(squares, scale_ref[1:2, :])).T
    out_ref[...] = values
    half_ref[...] = values.astype(jnp.bfloat16)


def reorder_kernel(map_ref, slab_ref, modes_ref):
    cells = slab_ref.shape[0]
    block = modes_ref.shape[0]
    row = lax.broadcasted_iota(jnp.int32, (cells, block), 0)
    chosen = jnp.where(row == map_ref[...], 1.0, 0.0).astype(jnp.bfloat16)
    modes_ref[...] = lax.dot_general(
        chosen,
        slab_ref[...],
        (((0,), (0,)), ((), ())),
        preferred_element_type=jnp.float32,
    ).astype(jnp.bfloat16)


def lift_kernel(half_ref, modes_ref, lifted_ref):
    lifted_ref[...] = lax.dot_general(
        half_ref[...],
        modes_ref[...],
        (((1,), (1,)), ((), ())),
        preferred_element_type=jnp.float32,
    ).astype(jnp.bfloat16)


def split_by_modes(
    run_inputs, term_codes, weight_levels, correlations, slab_modes, cell_map
):
    run_count, dim = run_inputs.shape
    term_count, modes = correlations.shape
    terms, slots = term_codes.shape
    cells = slab_modes.shape[0]
    slab_cells = cell_map.shape[0]
    devices = lax.axis_size("runs")
    total_runs = run_count * devices
    own_modes = modes // devices
    offset = lax.axis_index("runs") * term_count
    packet_rows = round_up(dim + term_count // LANES, 8)
    params = pltpu.CompilerParams(vmem_limit_bytes=48 * MIB)

    turned, packet = pl.pallas_call(
        prepare_kernel,
        out_shape=(
            jax.ShapeDtypeStruct((modes, term_count), jnp.bfloat16),
            jax.ShapeDtypeStruct((packet_rows, LANES), jnp.float32),
        ),
        compiler_params=params,
        name="prepare",
    )(correlations, run_inputs.T)
    packets = lax.all_gather(packet, "runs", axis=0, tiled=False)
    blocks = lax.all_to_all(
        turned.reshape(devices, own_modes, term_count), "runs", 0, 0, tiled=False
    )

    tile = term_count
    half = round_up(DEGREES * dim, LANES)
    design = pl.pallas_call(
        functools.partial(design_kernel, dim, run_count),
        grid=(terms // tile,),
        in_specs=[
            pl.BlockSpec((devices, packet_rows, LANES), lambda i: (0, 0, 0)),
            pl.BlockSpec((slots, tile), lambda i: (0, i)),
        ],
        out_specs=pl.BlockSpec((total_runs, tile), lambda i: (0, i)),
        out_shape=jax.ShapeDtypeStruct((total_runs, terms), jnp.bfloat16),
        scratch_shapes=[pltpu.VMEM((total_runs, 2 * half), jnp.bfloat16)],
        compiler_params=params,
        name="design",
    )(packets, term_codes.T)

    summed, scale = pl.pallas_call(
        functools.partial(fit_kernel, dim, float(total_runs)),
        out_shape=(
            jax.ShapeDtypeStruct((devices, own_modes, term_count), jnp.bfloat16),
            jax.ShapeDtypeStruct((8, terms), jnp.float32),
        ),
        compiler_params=params,
        name="fit",
    )(packets, weight_levels[None, :], blocks, design)
    own_scale = lax.dynamic_slice_in_dim(scale, offset, term_count, 1)
    returned = lax.all_to_all(summed, "runs", 0, 0, tiled=False).reshape(
        modes, term_count
    )

    block = min(512, slab_cells)
    ordered = pl.pallas_call(
        reorder_kernel,
        grid=(slab_cells // block,),
        in_specs=[
            pl.BlockSpec((1, block), lambda i: (0, i)),
            pl.BlockSpec((cells, modes), lambda i: (0, 0)),
        ],
        out_specs=pl.BlockSpec((block, modes), lambda i: (i, 0)),
        out_shape=jax.ShapeDtypeStruct((slab_cells, modes), jnp.bfloat16),
        compiler_params=params,
        name="reorder",
    )(cell_map[None, :], slab_modes)

    coefficients, half_width = pl.pallas_call(
        finish_kernel,
        out_shape=(
            jax.ShapeDtypeStruct((term_count, modes), jnp.float32),
            jax.ShapeDtypeStruct((term_count, modes), jnp.bfloat16),
        ),
        compiler_params=params,
        name="finish",
    )(returned, turned, own_scale)
    lifted = pl.pallas_call(
        lift_kernel,
        grid=(slab_cells // block,),
        in_specs=[
            pl.BlockSpec((term_count, modes), lambda i: (0, 0)),
            pl.BlockSpec((block, modes), lambda i: (i, 0)),
        ],
        out_specs=pl.BlockSpec((term_count, block), lambda i: (0, i)),
        out_shape=jax.ShapeDtypeStruct((term_count, slab_cells), jnp.bfloat16),
        compiler_params=params,
        name="lift",
    )(half_width, ordered)
    return (coefficients, lifted)


def hermite_table(points):
    squared = points * points
    columns = [
        jnp.ones_like(points),
        points,
        (squared - 1.0) / ROOT_TWO,
        points * (squared - 3.0) / ROOT_SIX,
        (squared * squared - 6.0 * squared + 3.0) / ROOT_TWENTYFOUR,
    ]
    return jnp.stack(columns, axis=-1).reshape(points.shape[0], -1)


def basis(points, codes):
    hermite = hermite_table(points)
    product = jnp.take(hermite, codes[:, 0], axis=1)
    for column in range(1, codes.shape[1]):
        product = product * jnp.take(hermite, codes[:, column], axis=1)
    return product.astype(jnp.bfloat16)


def shrink(values, limits):
    length = jnp.sqrt(jnp.sum(values * values, axis=1, keepdims=True) + EPSILON)
    return values * jnp.maximum(0.0, 1.0 - limits[:, None] / length)


def transposed_product(left, right):
    return lax.dot_general(
        left, right, (((0,), (0,)), ((), ())), preferred_element_type=jnp.float32
    )


def split_by_runs(
    run_inputs, term_codes, weight_levels, correlations, slab_modes, cell_map
):
    run_count = run_inputs.shape[0]
    term_count = correlations.shape[0]
    devices = lax.axis_size("runs")
    offset = lax.axis_index("runs") * term_count
    total_runs = run_count * devices
    weights_all = jnp.exp2(weight_levels.astype(jnp.float32))
    own_weights = lax.dynamic_slice_in_dim(weights_all, offset, term_count)
    own_corr = correlations.astype(jnp.float32)
    ratio = jnp.max(jnp.sqrt(jnp.sum(own_corr * own_corr, axis=1)) / own_weights)
    penalty = LAMBDA_FRACTION * lax.pmax(ratio, "runs")
    first = shrink(STEP * own_corr, STEP * penalty * own_weights)
    design = basis(run_inputs, term_codes)
    fitted = jnp.dot(
        design,
        lax.all_gather(first.astype(jnp.bfloat16), "runs", axis=0, tiled=True),
        preferred_element_type=jnp.float32,
    )
    fitted_half = fitted.astype(jnp.bfloat16)
    all_points = lax.all_gather(run_inputs, "runs", axis=0, tiled=True)
    own_codes = lax.dynamic_slice_in_dim(term_codes, offset, term_count, 0)
    owned_design = basis(all_points, own_codes)
    summed = transposed_product(
        owned_design, lax.all_gather(fitted_half, "runs", axis=0, tiled=True)
    )
    gradient = summed / total_runs - own_corr
    coefficients = shrink(first - STEP * gradient, STEP * penalty * own_weights)
    modes = jnp.take(slab_modes, cell_map, axis=0)
    lifted = lax.dot_general(
        coefficients.astype(jnp.bfloat16),
        modes,
        (((1,), (1,)), ((), ())),
        preferred_element_type=jnp.float32,
    ).astype(jnp.bfloat16)
    return (coefficients, lifted)


def on_device(
    run_inputs, term_codes, weight_levels, correlations, slab_modes, cell_map
):
    devices = lax.axis_size("runs")
    run_count = run_inputs.shape[0]
    term_count, modes = correlations.shape
    whole_tiles = (
        modes % (16 * devices) == 0
        and term_count % LANES == 0
        and LANES % run_count == 0
        and devices % (LANES // run_count) == 0
    )
    plan = split_by_modes if whole_tiles else split_by_runs
    return plan(
        run_inputs, term_codes, weight_levels, correlations, slab_modes, cell_map
    )


def solution(mesh):
    return jax.shard_map(
        on_device,
        mesh=mesh,
        in_specs=(
            P(("cases", "runs"), None),
            P(),
            P(),
            P(("cases", "runs"), None),
            P("cases", None),
            P(),
        ),
        out_specs=(P(("cases", "runs"), None), P(("cases", "runs"), None)),
        check_vma=False,
    )
```

```python
import functools
import math

import jax
import jax.numpy as jnp
from jax import lax
from jax.experimental import pallas as pl
from jax.experimental.pallas import tpu as pltpu
from jax.sharding import PartitionSpec as P

STEP = 0.5
LAMBDA_FRACTION = 0.05
EPSILON = 1e-06
DEGREES = 5
LANES = 128
ROOT_TWO = math.sqrt(2.0)
ROOT_SIX = math.sqrt(6.0)
ROOT_TWENTYFOUR = math.sqrt(24.0)
MIB = 1 << 20


def round_up(value, multiple):
    return -(-value // multiple) * multiple


def prepare_kernel(parts, corr_ref, points_ref, turned_ref, packets_ref):
    turned = corr_ref[...].astype(jnp.float32).T
    turned_ref[...] = turned.astype(jnp.bfloat16)
    squares = jnp.sum(turned * turned, axis=0, keepdims=True)
    rows = points_ref.shape[0] // parts
    pieces = [
        jnp.concatenate(
            [points_ref[part * rows : (part + 1) * rows, :] for part in range(parts)],
            axis=1,
        )
    ]
    pieces += [
        squares[:, part * LANES : (part + 1) * LANES]
        for part in range(squares.shape[1] // LANES)
    ]
    used = rows + len(pieces) - 1
    if packets_ref.shape[1] > used:
        pieces.append(jnp.zeros((packets_ref.shape[1] - used, LANES), jnp.float32))
    packet = jnp.concatenate(pieces, axis=0)
    for i in range(packets_ref.shape[0]):
        packets_ref[i] = packet


def hermite_columns(points):
    squared = points * points
    return jnp.concatenate(
        [
            jnp.ones_like(points),
            points,
            (squared - 1.0) / ROOT_TWO,
            points * (squared - 3.0) / ROOT_SIX,
            (squared * squared - 6.0 * squared + 3.0) / ROOT_TWENTYFOUR,
        ],
        axis=0,
    )


def design_kernel(dim, run_count, packets_ref, codes_ref, design_ref, table, chosen):
    devices = packets_ref.shape[0]
    half = table.shape[1] // 2
    parts = LANES // run_count
    rows = dim // parts

    @pl.when(pl.program_id(0) == 0)
    def _():
        for group in range(devices // parts):
            points = jnp.concatenate(
                [
                    jnp.concatenate(
                        [
                            packets_ref[
                                group * parts + i,
                                0:rows,
                                part * run_count : (part + 1) * run_count,
                            ]
                            for i in range(parts)
                        ],
                        axis=1,
                    )
                    for part in range(parts)
                ],
                axis=0,
            )
            columns = hermite_columns(points)
            columns = jnp.concatenate(
                [
                    columns,
                    jnp.zeros((half - columns.shape[0], LANES), jnp.float32),
                ],
                axis=0,
            ).T
            high = columns.astype(jnp.bfloat16)
            low = (columns - high.astype(jnp.float32)).astype(jnp.bfloat16)
            block = slice(group * LANES, (group + 1) * LANES)
            table[block, 0:half] = high
            table[block, half : 2 * half] = low

    codes = codes_ref[...]
    spots = (codes % DEGREES) * dim + codes // DEGREES
    slots, terms = codes.shape
    row = lax.broadcasted_iota(jnp.int32, (half, terms), 0)
    for slot in range(slots):
        picked = jnp.where(row == spots[slot : slot + 1, :], 1.0, 0.0).astype(
            jnp.bfloat16
        )
        chosen[slot, 0:half, :] = picked
        chosen[slot, half : 2 * half, :] = picked
    for start in range(0, table.shape[0], LANES):
        block = slice(start, start + LANES)
        product = None
        for slot in range(slots):
            factor = jnp.dot(
                table[block, :], chosen[slot], preferred_element_type=jnp.float32
            )
            product = factor if product is None else product * factor
        design_ref[block, :] = product.astype(jnp.bfloat16)


def penalty_rows(first_row, term_count, packets_ref, levels_ref):
    squares = jnp.concatenate(
        [
            packets_ref[i, first_row + part : first_row + part + 1, :]
            for i in range(packets_ref.shape[0])
            for part in range(term_count // LANES)
        ],
        axis=1,
    )
    weights = jnp.exp2(levels_ref[...].astype(jnp.float32))
    ratio = jnp.max(jnp.sqrt(squares) / weights, axis=1, keepdims=True)
    return squares, weights, LAMBDA_FRACTION * ratio


def shrink_factor(squares, limits):
    return jnp.maximum(0.0, 1.0 - limits / jnp.sqrt(squares + EPSILON))


def fit_kernel(
    first_row,
    total_runs,
    packets_ref,
    levels_ref,
    corr_ref,
    design_ref,
    summed_ref,
    scale_ref,
    first_ref,
):
    devices, _, term_count = corr_ref.shape
    squares, weights, penalty = penalty_rows(
        first_row, term_count, packets_ref, levels_ref
    )
    limits = STEP * penalty * weights
    factor = shrink_factor(STEP * STEP * squares, limits)
    scale_ref[0:1, :] = factor
    scale_ref[1:2, :] = limits
    for i in range(devices):
        terms = slice(i * term_count, (i + 1) * term_count)
        first = STEP * corr_ref[i].astype(jnp.float32) * factor[:, terms]
        first_ref[:, terms] = first.astype(jnp.bfloat16)
    fitted = lax.dot_general(
        first_ref[...],
        design_ref[...],
        (((1,), (1,)), ((), ())),
        preferred_element_type=jnp.float32,
    ).astype(jnp.bfloat16)
    for i in range(devices):
        terms = slice(i * term_count, (i + 1) * term_count)
        summed = jnp.dot(
            fitted, design_ref[:, terms], preferred_element_type=jnp.float32
        )
        summed_ref[i] = (summed / total_runs).astype(jnp.bfloat16)


def reorder_kernel(map_ref, slab_ref, modes_ref, turned):
    cells, block = slab_ref.shape[0], modes_ref.shape[1]

    @pl.when(pl.program_id(0) == 0)
    def _():
        for start in range(0, cells, LANES):
            rows = slice(start, start + LANES)
            turned[:, rows] = slab_ref[rows, :].T

    row = lax.broadcasted_iota(jnp.int32, (cells, block), 0)
    chosen = jnp.where(row == map_ref[...], 1.0, 0.0).astype(jnp.bfloat16)
    modes_ref[...] = jnp.dot(
        turned[...], chosen, preferred_element_type=jnp.float32
    ).astype(jnp.bfloat16)


def finish_kernel(
    summed_ref,
    corr_ref,
    scale_ref,
    modes_ref,
    out_ref,
    lifted_ref,
    moved,
    values,
    half,
    lifted,
    out_sem,
    lifted_sem,
):
    modes, terms = corr_ref.shape
    squares = jnp.zeros((1, terms), jnp.float32)
    for start in range(0, modes, LANES):
        block = slice(start, start + LANES)
        corr = corr_ref[block, :].astype(jnp.float32)
        first = STEP * corr * scale_ref[0:1, :]
        gradient = summed_ref[block, :].astype(jnp.float32) - corr
        step = first - STEP * gradient
        moved[block, :] = step
        squares = squares + jnp.sum(step * step, axis=0, keepdims=True)
    factor = shrink_factor(squares, scale_ref[1:2, :])
    for start in range(0, modes, LANES):
        block = slice(start, start + LANES)
        turned = (moved[block, :] * factor).T
        values[:, block] = turned
        half[:, block] = turned.astype(jnp.bfloat16)
    copies = [pltpu.make_async_copy(values, out_ref, out_sem)]
    copies[0].start()
    width = lifted.shape[2]
    for i in range(lifted.shape[0]):
        block = slice(i * width, (i + 1) * width)
        lifted[i] = jnp.dot(
            half[...], modes_ref[:, block], preferred_element_type=jnp.float32
        ).astype(jnp.bfloat16)
        copies.append(
            pltpu.make_async_copy(
                lifted.at[i], lifted_ref.at[:, block], lifted_sem.at[i]
            )
        )
        copies[-1].start()
    for copy in copies:
        copy.wait()


def params(limit):
    return pltpu.CompilerParams(vmem_limit_bytes=limit * MIB)


def split_by_modes(
    run_inputs, term_codes, weight_levels, correlations, slab_modes, cell_map
):
    run_count, dim = run_inputs.shape
    term_count, modes = correlations.shape
    terms, slots = term_codes.shape
    cells = slab_modes.shape[0]
    slab_cells = cell_map.shape[0]
    devices = lax.axis_size("runs")
    total_runs = run_count * devices
    own_modes = modes // devices
    offset = lax.axis_index("runs") * term_count
    parts = LANES // run_count
    first_row = dim // parts
    packet_rows = round_up(first_row + term_count // LANES, 8)

    turned, packets = pl.pallas_call(
        functools.partial(prepare_kernel, parts),
        out_shape=(
            jax.ShapeDtypeStruct((modes, term_count), jnp.bfloat16),
            jax.ShapeDtypeStruct((devices, packet_rows, LANES), jnp.float32),
        ),
        compiler_params=params(16),
        name="prepare",
    )(correlations, run_inputs.T)
    packets = lax.all_to_all(packets, "runs", 0, 0, tiled=False)
    blocks = lax.all_to_all(
        turned.reshape(devices, own_modes, term_count), "runs", 0, 0, tiled=False
    )

    tile = term_count
    half = round_up(DEGREES * dim, LANES)
    design = pl.pallas_call(
        functools.partial(design_kernel, dim, run_count),
        grid=(terms // tile,),
        in_specs=[
            pl.BlockSpec((devices, packet_rows, LANES), lambda i: (0, 0, 0)),
            pl.BlockSpec((slots, tile), lambda i: (0, i)),
        ],
        out_specs=pl.BlockSpec((total_runs, tile), lambda i: (0, i)),
        out_shape=jax.ShapeDtypeStruct((total_runs, terms), jnp.bfloat16),
        scratch_shapes=[
            pltpu.VMEM((total_runs, 2 * half), jnp.bfloat16),
            pltpu.VMEM((slots, 2 * half, tile), jnp.bfloat16),
        ],
        compiler_params=params(16),
        name="design",
    )(packets, term_codes.T)

    summed, scale = pl.pallas_call(
        functools.partial(fit_kernel, first_row, float(total_runs)),
        out_shape=(
            jax.ShapeDtypeStruct((devices, own_modes, term_count), jnp.bfloat16),
            jax.ShapeDtypeStruct((8, terms), jnp.float32),
        ),
        scratch_shapes=[pltpu.VMEM((own_modes, terms), jnp.bfloat16)],
        compiler_params=params(20),
        name="fit",
    )(packets, weight_levels[None, :], blocks, design)
    own_scale = lax.dynamic_slice_in_dim(scale, offset, term_count, 1)
    returned = lax.all_to_all(summed, "runs", 0, 0, tiled=False).reshape(
        modes, term_count
    )

    block = math.gcd(512, slab_cells)
    ordered = pl.pallas_call(
        reorder_kernel,
        grid=(slab_cells // block,),
        in_specs=[
            pl.BlockSpec((1, block), lambda i: (0, i)),
            pl.BlockSpec((cells, modes), lambda i: (0, 0)),
        ],
        out_specs=pl.BlockSpec((modes, block), lambda i: (0, i)),
        out_shape=jax.ShapeDtypeStruct((modes, slab_cells), jnp.bfloat16),
        scratch_shapes=[pltpu.VMEM((modes, cells), jnp.bfloat16)],
        compiler_params=params(24),
        name="reorder",
    )(cell_map[None, :], slab_modes)

    vmem = pl.BlockSpec(memory_space=pltpu.VMEM)
    anywhere = pl.BlockSpec(memory_space=pl.ANY)
    return pl.pallas_call(
        finish_kernel,
        in_specs=[vmem, vmem, vmem, vmem],
        out_specs=(anywhere, anywhere),
        out_shape=(
            jax.ShapeDtypeStruct((term_count, modes), jnp.float32),
            jax.ShapeDtypeStruct((term_count, slab_cells), jnp.bfloat16),
        ),
        scratch_shapes=[
            pltpu.VMEM((modes, term_count), jnp.float32),
            pltpu.VMEM((term_count, modes), jnp.float32),
            pltpu.VMEM((term_count, modes), jnp.bfloat16),
            pltpu.VMEM((slab_cells // block, term_count, block), jnp.bfloat16),
            pltpu.SemaphoreType.DMA,
            pltpu.SemaphoreType.DMA((slab_cells // block,)),
        ],
        compiler_params=params(20),
        name="finish",
    )(returned, turned, own_scale, ordered)


def hermite_table(points):
    squared = points * points
    columns = [
        jnp.ones_like(points),
        points,
        (squared - 1.0) / ROOT_TWO,
        points * (squared - 3.0) / ROOT_SIX,
        (squared * squared - 6.0 * squared + 3.0) / ROOT_TWENTYFOUR,
    ]
    return jnp.stack(columns, axis=-1).reshape(points.shape[0], -1)


def basis(points, codes):
    hermite = hermite_table(points)
    product = jnp.take(hermite, codes[:, 0], axis=1)
    for column in range(1, codes.shape[1]):
        product = product * jnp.take(hermite, codes[:, column], axis=1)
    return product.astype(jnp.bfloat16)


def shrink(values, limits):
    length = jnp.sqrt(jnp.sum(values * values, axis=1, keepdims=True) + EPSILON)
    return values * jnp.maximum(0.0, 1.0 - limits[:, None] / length)


def transposed_product(left, right):
    return lax.dot_general(
        left, right, (((0,), (0,)), ((), ())), preferred_element_type=jnp.float32
    )


def split_by_runs(
    run_inputs, term_codes, weight_levels, correlations, slab_modes, cell_map
):
    run_count = run_inputs.shape[0]
    term_count = correlations.shape[0]
    devices = lax.axis_size("runs")
    offset = lax.axis_index("runs") * term_count
    total_runs = run_count * devices
    weights_all = jnp.exp2(weight_levels.astype(jnp.float32))
    own_weights = lax.dynamic_slice_in_dim(weights_all, offset, term_count)
    own_corr = correlations.astype(jnp.float32)
    ratio = jnp.max(jnp.sqrt(jnp.sum(own_corr * own_corr, axis=1)) / own_weights)
    penalty = LAMBDA_FRACTION * lax.pmax(ratio, "runs")
    first = shrink(STEP * own_corr, STEP * penalty * own_weights)
    design = basis(run_inputs, term_codes)
    fitted = jnp.dot(
        design,
        lax.all_gather(first.astype(jnp.bfloat16), "runs", axis=0, tiled=True),
        preferred_element_type=jnp.float32,
    )
    fitted_half = fitted.astype(jnp.bfloat16)
    all_points = lax.all_gather(run_inputs, "runs", axis=0, tiled=True)
    own_codes = lax.dynamic_slice_in_dim(term_codes, offset, term_count, 0)
    owned_design = basis(all_points, own_codes)
    summed = transposed_product(
        owned_design, lax.all_gather(fitted_half, "runs", axis=0, tiled=True)
    )
    gradient = summed / total_runs - own_corr
    coefficients = shrink(first - STEP * gradient, STEP * penalty * own_weights)
    modes = jnp.take(slab_modes, cell_map, axis=0)
    lifted = lax.dot_general(
        coefficients.astype(jnp.bfloat16),
        modes,
        (((1,), (1,)), ((), ())),
        preferred_element_type=jnp.float32,
    ).astype(jnp.bfloat16)
    return (coefficients, lifted)


def on_device(
    run_inputs, term_codes, weight_levels, correlations, slab_modes, cell_map
):
    devices = lax.axis_size("runs")
    run_count = run_inputs.shape[0]
    term_count, modes = correlations.shape
    whole_tiles = (
        modes % (16 * devices) == 0
        and term_count % LANES == 0
        and LANES % run_count == 0
        and devices % (LANES // run_count) == 0
        and run_inputs.shape[1] % (LANES // run_count) == 0
        and slab_modes.shape[0] % LANES == 0
        and cell_map.shape[0] % LANES == 0
    )
    plan = split_by_modes if whole_tiles else split_by_runs
    return plan(
        run_inputs, term_codes, weight_levels, correlations, slab_modes, cell_map
    )


def solution(mesh):
    return jax.shard_map(
        on_device,
        mesh=mesh,
        in_specs=(
            P(("cases", "runs"), None),
            P(),
            P(),
            P(("cases", "runs"), None),
            P("cases", None),
            P(),
        ),
        out_specs=(P(("cases", "runs"), None), P(("cases", "runs"), None)),
        check_vma=False,
    )
```

```python
import functools
import math

import jax
import jax.numpy as jnp
from jax import lax
from jax.experimental import pallas as pl
from jax.experimental.pallas import tpu as pltpu
from jax.sharding import PartitionSpec as P

STEP = 0.5
LAMBDA_FRACTION = 0.05
EPSILON = 1e-06
DEGREES = 5
LANES = 128
ROOT_TWO = math.sqrt(2.0)
ROOT_SIX = math.sqrt(6.0)
ROOT_TWENTYFOUR = math.sqrt(24.0)
MIB = 1 << 20


def round_up(value, multiple):
    return -(-value // multiple) * multiple


def prepare_kernel(parts, corr_ref, points_ref, turned_ref, packets_ref):
    turned = corr_ref[...].astype(jnp.float32).T
    turned_ref[...] = turned.astype(jnp.bfloat16)
    squares = jnp.sum(turned * turned, axis=0, keepdims=True)
    rows = points_ref.shape[0] // parts
    pieces = [
        jnp.concatenate(
            [points_ref[part * rows : (part + 1) * rows, :] for part in range(parts)],
            axis=1,
        )
    ]
    pieces += [
        squares[:, part * LANES : (part + 1) * LANES]
        for part in range(squares.shape[1] // LANES)
    ]
    used = rows + len(pieces) - 1
    if packets_ref.shape[1] > used:
        pieces.append(jnp.zeros((packets_ref.shape[1] - used, LANES), jnp.float32))
    packet = jnp.concatenate(pieces, axis=0)
    for i in range(packets_ref.shape[0]):
        packets_ref[i] = packet


def hermite_columns(points):
    squared = points * points
    return jnp.concatenate(
        [
            jnp.ones_like(points),
            points,
            (squared - 1.0) / ROOT_TWO,
            points * (squared - 3.0) / ROOT_SIX,
            (squared * squared - 6.0 * squared + 3.0) / ROOT_TWENTYFOUR,
        ],
        axis=0,
    )


def design_kernel(
    dim, run_count, packets_ref, codes_ref, design_ref, exact, table, chosen
):
    devices = packets_ref.shape[0]
    half = exact.shape[1]
    parts = LANES // run_count
    rows = dim // parts

    @pl.when(pl.program_id(0) == 0)
    def _():
        for group in range(devices // parts):
            points = jnp.concatenate(
                [
                    jnp.concatenate(
                        [
                            packets_ref[
                                group * parts + i,
                                0:rows,
                                part * run_count : (part + 1) * run_count,
                            ]
                            for i in range(parts)
                        ],
                        axis=1,
                    )
                    for part in range(parts)
                ],
                axis=0,
            )
            columns = hermite_columns(points)
            columns = jnp.concatenate(
                [
                    columns,
                    jnp.zeros((half - columns.shape[0], LANES), jnp.float32),
                ],
                axis=0,
            ).T
            high = columns.astype(jnp.bfloat16)
            low = (columns - high.astype(jnp.float32)).astype(jnp.bfloat16)
            block = slice(group * LANES, (group + 1) * LANES)
            exact[block, :] = columns
            table[block, 0:half] = high
            table[block, half : 2 * half] = low

    codes = codes_ref[...]
    spots = (codes % DEGREES) * dim + codes // DEGREES
    slots, terms = codes.shape
    row = lax.broadcasted_iota(jnp.int32, (half, terms), 0)
    matmuls = chosen.shape[0]
    for slot in range(matmuls):
        picked = jnp.where(row == spots[slot : slot + 1, :], 1.0, 0.0).astype(
            jnp.bfloat16
        )
        chosen[slot, 0:half, :] = picked
        chosen[slot, half : 2 * half, :] = picked
    for start in range(0, table.shape[0], LANES):
        block = slice(start, start + LANES)
        rows = exact[block, :]
        product = None
        for slot in range(matmuls):
            factor = jnp.dot(
                table[block, :], chosen[slot], preferred_element_type=jnp.float32
            )
            product = factor if product is None else product * factor
        for part in range(0, terms, half):
            lanes = slice(part, part + half)
            factor = product[:, lanes]
            for slot in range(matmuls, slots):
                spot = jnp.broadcast_to(spots[slot : slot + 1, lanes], rows.shape)
                factor = factor * jnp.take_along_axis(rows, spot, axis=1)
            design_ref[block, lanes] = factor.astype(jnp.bfloat16)


def penalty_rows(first_row, term_count, packets_ref, levels_ref):
    squares = jnp.concatenate(
        [
            packets_ref[i, first_row + part : first_row + part + 1, :]
            for i in range(packets_ref.shape[0])
            for part in range(term_count // LANES)
        ],
        axis=1,
    )
    weights = jnp.exp2(levels_ref[...].astype(jnp.float32))
    ratio = jnp.max(jnp.sqrt(squares) / weights, axis=1, keepdims=True)
    return squares, weights, LAMBDA_FRACTION * ratio


def shrink_factor(squares, limits):
    return jnp.maximum(0.0, 1.0 - limits / jnp.sqrt(squares + EPSILON))


def fit_kernel(
    first_row,
    total_runs,
    packets_ref,
    levels_ref,
    corr_ref,
    design_ref,
    summed_ref,
    scale_ref,
    first_ref,
    held,
    sems,
):
    devices, _, term_count = corr_ref.shape
    width = held.shape[1] // sems.shape[0]
    copies = []
    for i in range(sems.shape[0]):
        chunk = slice(i * width, (i + 1) * width)
        copies.append(
            pltpu.make_async_copy(design_ref.at[:, chunk], held.at[:, chunk], sems.at[i])
        )
        copies[-1].start()
    squares, weights, penalty = penalty_rows(
        first_row, term_count, packets_ref, levels_ref
    )
    limits = STEP * penalty * weights
    factor = shrink_factor(STEP * STEP * squares, limits)
    scale_ref[0:1, :] = factor
    scale_ref[1:2, :] = limits
    for i in range(devices):
        terms = slice(i * term_count, (i + 1) * term_count)
        first = STEP * corr_ref[i].astype(jnp.float32) * factor[:, terms]
        first_ref[:, terms] = first.astype(jnp.bfloat16)
    fitted = None
    for i in range(sems.shape[0]):
        chunk = slice(i * width, (i + 1) * width)
        copies[i].wait()
        part = lax.dot_general(
            first_ref[:, chunk],
            held[:, chunk],
            (((1,), (1,)), ((), ())),
            preferred_element_type=jnp.float32,
        )
        fitted = part if fitted is None else fitted + part
    fitted = fitted.astype(jnp.bfloat16)
    for i in range(devices):
        terms = slice(i * term_count, (i + 1) * term_count)
        summed = jnp.dot(fitted, held[:, terms], preferred_element_type=jnp.float32)
        summed_ref[i] = (summed / total_runs).astype(jnp.bfloat16)


def reorder_kernel(map_ref, slab_ref, modes_ref, turned):
    cells, block = slab_ref.shape[0], modes_ref.shape[1]

    @pl.when(pl.program_id(0) == 0)
    def _():
        for start in range(0, cells, LANES):
            rows = slice(start, start + LANES)
            turned[:, rows] = slab_ref[rows, :].T

    row = lax.broadcasted_iota(jnp.int32, (cells, block), 0)
    chosen = jnp.where(row == map_ref[...], 1.0, 0.0).astype(jnp.bfloat16)
    modes_ref[...] = jnp.dot(
        turned[...], chosen, preferred_element_type=jnp.float32
    ).astype(jnp.bfloat16)


def finish_kernel(
    summed_ref,
    corr_ref,
    scale_ref,
    modes_ref,
    out_ref,
    lifted_ref,
    moved,
    values,
    half,
    lifted,
    held,
    held_sem,
    out_sem,
    lifted_sem,
):
    load = pltpu.make_async_copy(modes_ref, held, held_sem)
    load.start()
    modes, terms = corr_ref.shape
    squares = jnp.zeros((1, terms), jnp.float32)
    for start in range(0, modes, LANES):
        block = slice(start, start + LANES)
        corr = corr_ref[block, :].astype(jnp.float32)
        first = STEP * corr * scale_ref[0:1, :]
        gradient = summed_ref[block, :].astype(jnp.float32) - corr
        step = first - STEP * gradient
        moved[block, :] = step
        squares = squares + jnp.sum(step * step, axis=0, keepdims=True)
    factor = shrink_factor(squares, scale_ref[1:2, :])
    for start in range(0, modes, LANES):
        block = slice(start, start + LANES)
        turned = (moved[block, :] * factor).T
        values[:, block] = turned
        half[:, block] = turned.astype(jnp.bfloat16)
    copies = [pltpu.make_async_copy(values, out_ref, out_sem)]
    copies[0].start()
    width = lifted.shape[2]
    load.wait()
    for i in range(lifted.shape[0]):
        block = slice(i * width, (i + 1) * width)
        lifted[i] = jnp.dot(
            half[...], held[:, block], preferred_element_type=jnp.float32
        ).astype(jnp.bfloat16)
        copies.append(
            pltpu.make_async_copy(
                lifted.at[i], lifted_ref.at[:, block], lifted_sem.at[i]
            )
        )
        copies[-1].start()
    for copy in copies:
        copy.wait()


def in_hbm(array):
    return pltpu.with_memory_space_constraint(array, pltpu.HBM)


def params(limit):
    return pltpu.CompilerParams(vmem_limit_bytes=limit * MIB)


def split_by_modes(
    run_inputs, term_codes, weight_levels, correlations, slab_modes, cell_map
):
    run_count, dim = run_inputs.shape
    term_count, modes = correlations.shape
    terms, slots = term_codes.shape
    cells = slab_modes.shape[0]
    slab_cells = cell_map.shape[0]
    devices = lax.axis_size("runs")
    total_runs = run_count * devices
    own_modes = modes // devices
    offset = lax.axis_index("runs") * term_count
    parts = LANES // run_count
    first_row = dim // parts
    packet_rows = round_up(first_row + term_count // LANES, 8)

    turned, packets = pl.pallas_call(
        functools.partial(prepare_kernel, parts),
        out_shape=(
            jax.ShapeDtypeStruct((modes, term_count), jnp.bfloat16),
            jax.ShapeDtypeStruct((devices, packet_rows, LANES), jnp.float32),
        ),
        compiler_params=params(16),
        name="prepare",
    )(in_hbm(correlations), in_hbm(run_inputs.T))
    packets = lax.all_to_all(packets, "runs", 0, 0, tiled=False)
    blocks = lax.all_to_all(
        turned.reshape(devices, own_modes, term_count), "runs", 0, 0, tiled=False
    )

    tile = term_count
    half = round_up(DEGREES * dim, LANES)
    design = pl.pallas_call(
        functools.partial(design_kernel, dim, run_count),
        grid=(terms // tile,),
        in_specs=[
            pl.BlockSpec((devices, packet_rows, LANES), lambda i: (0, 0, 0)),
            pl.BlockSpec((slots, tile), lambda i: (0, i)),
        ],
        out_specs=pl.BlockSpec((total_runs, tile), lambda i: (0, i)),
        out_shape=pltpu.HBM((total_runs, terms), jnp.bfloat16),
        scratch_shapes=[
            pltpu.VMEM((total_runs, half), jnp.float32),
            pltpu.VMEM((total_runs, 2 * half), jnp.bfloat16),
            pltpu.VMEM((slots - slots // 2, 2 * half, tile), jnp.bfloat16),
        ],
        compiler_params=params(16),
        name="design",
    )(packets, in_hbm(term_codes.T))

    vmem = pl.BlockSpec(memory_space=pltpu.VMEM)
    anywhere = pl.BlockSpec(memory_space=pl.ANY)
    chunks = math.gcd(8, terms // LANES)
    summed, scale = pl.pallas_call(
        functools.partial(fit_kernel, first_row, float(total_runs)),
        in_specs=[vmem, vmem, vmem, anywhere],
        out_shape=(
            jax.ShapeDtypeStruct((devices, own_modes, term_count), jnp.bfloat16),
            jax.ShapeDtypeStruct((8, terms), jnp.float32),
        ),
        scratch_shapes=[
            pltpu.VMEM((own_modes, terms), jnp.bfloat16),
            pltpu.VMEM((total_runs, terms), jnp.bfloat16),
            pltpu.SemaphoreType.DMA((chunks,)),
        ],
        compiler_params=params(24),
        name="fit",
    )(packets, weight_levels[None, :], blocks, in_hbm(design))
    own_scale = lax.dynamic_slice_in_dim(scale, offset, term_count, 1)
    returned = lax.all_to_all(summed, "runs", 0, 0, tiled=False).reshape(
        modes, term_count
    )

    block = math.gcd(512, slab_cells)
    ordered = pl.pallas_call(
        reorder_kernel,
        grid=(slab_cells // block,),
        in_specs=[
            pl.BlockSpec((1, block), lambda i: (0, i)),
            pl.BlockSpec((cells, modes), lambda i: (0, 0)),
        ],
        out_specs=pl.BlockSpec((modes, block), lambda i: (0, i)),
        out_shape=pltpu.HBM((modes, slab_cells), jnp.bfloat16),
        scratch_shapes=[pltpu.VMEM((modes, cells), jnp.bfloat16)],
        compiler_params=params(24),
        name="reorder",
    )(cell_map[None, :], in_hbm(slab_modes))

    return pl.pallas_call(
        finish_kernel,
        in_specs=[vmem, vmem, vmem, anywhere],
        out_specs=(anywhere, anywhere),
        out_shape=(
            jax.ShapeDtypeStruct((term_count, modes), jnp.float32),
            jax.ShapeDtypeStruct((term_count, slab_cells), jnp.bfloat16),
        ),
        scratch_shapes=[
            pltpu.VMEM((modes, term_count), jnp.float32),
            pltpu.VMEM((term_count, modes), jnp.float32),
            pltpu.VMEM((term_count, modes), jnp.bfloat16),
            pltpu.VMEM((slab_cells // block, term_count, block), jnp.bfloat16),
            pltpu.VMEM((modes, slab_cells), jnp.bfloat16),
            pltpu.SemaphoreType.DMA,
            pltpu.SemaphoreType.DMA,
            pltpu.SemaphoreType.DMA((slab_cells // block,)),
        ],
        compiler_params=params(20),
        name="finish",
    )(returned, turned, own_scale, in_hbm(ordered))


def hermite_table(points):
    squared = points * points
    columns = [
        jnp.ones_like(points),
        points,
        (squared - 1.0) / ROOT_TWO,
        points * (squared - 3.0) / ROOT_SIX,
        (squared * squared - 6.0 * squared + 3.0) / ROOT_TWENTYFOUR,
    ]
    return jnp.stack(columns, axis=-1).reshape(points.shape[0], -1)


def basis(points, codes):
    hermite = hermite_table(points)
    product = jnp.take(hermite, codes[:, 0], axis=1)
    for column in range(1, codes.shape[1]):
        product = product * jnp.take(hermite, codes[:, column], axis=1)
    return product.astype(jnp.bfloat16)


def shrink(values, limits):
    length = jnp.sqrt(jnp.sum(values * values, axis=1, keepdims=True) + EPSILON)
    return values * jnp.maximum(0.0, 1.0 - limits[:, None] / length)


def transposed_product(left, right):
    return lax.dot_general(
        left, right, (((0,), (0,)), ((), ())), preferred_element_type=jnp.float32
    )


def split_by_runs(
    run_inputs, term_codes, weight_levels, correlations, slab_modes, cell_map
):
    run_count = run_inputs.shape[0]
    term_count = correlations.shape[0]
    devices = lax.axis_size("runs")
    offset = lax.axis_index("runs") * term_count
    total_runs = run_count * devices
    weights_all = jnp.exp2(weight_levels.astype(jnp.float32))
    own_weights = lax.dynamic_slice_in_dim(weights_all, offset, term_count)
    own_corr = correlations.astype(jnp.float32)
    ratio = jnp.max(jnp.sqrt(jnp.sum(own_corr * own_corr, axis=1)) / own_weights)
    penalty = LAMBDA_FRACTION * lax.pmax(ratio, "runs")
    first = shrink(STEP * own_corr, STEP * penalty * own_weights)
    design = basis(run_inputs, term_codes)
    fitted = jnp.dot(
        design,
        lax.all_gather(first.astype(jnp.bfloat16), "runs", axis=0, tiled=True),
        preferred_element_type=jnp.float32,
    )
    fitted_half = fitted.astype(jnp.bfloat16)
    all_points = lax.all_gather(run_inputs, "runs", axis=0, tiled=True)
    own_codes = lax.dynamic_slice_in_dim(term_codes, offset, term_count, 0)
    owned_design = basis(all_points, own_codes)
    summed = transposed_product(
        owned_design, lax.all_gather(fitted_half, "runs", axis=0, tiled=True)
    )
    gradient = summed / total_runs - own_corr
    coefficients = shrink(first - STEP * gradient, STEP * penalty * own_weights)
    modes = jnp.take(slab_modes, cell_map, axis=0)
    lifted = lax.dot_general(
        coefficients.astype(jnp.bfloat16),
        modes,
        (((1,), (1,)), ((), ())),
        preferred_element_type=jnp.float32,
    ).astype(jnp.bfloat16)
    return (coefficients, lifted)


def on_device(
    run_inputs, term_codes, weight_levels, correlations, slab_modes, cell_map
):
    devices = lax.axis_size("runs")
    run_count = run_inputs.shape[0]
    term_count, modes = correlations.shape
    whole_tiles = (
        modes % (16 * devices) == 0
        and DEGREES * run_inputs.shape[1] <= LANES
        and term_count % LANES == 0
        and LANES % run_count == 0
        and devices % (LANES // run_count) == 0
        and run_inputs.shape[1] % (LANES // run_count) == 0
        and slab_modes.shape[0] % LANES == 0
        and cell_map.shape[0] % LANES == 0
    )
    plan = split_by_modes if whole_tiles else split_by_runs
    return plan(
        run_inputs, term_codes, weight_levels, correlations, slab_modes, cell_map
    )


def solution(mesh):
    return jax.shard_map(
        on_device,
        mesh=mesh,
        in_specs=(
            P(("cases", "runs"), None),
            P(),
            P(),
            P(("cases", "runs"), None),
            P("cases", None),
            P(),
        ),
        out_specs=(P(("cases", "runs"), None), P(("cases", "runs"), None)),
        check_vma=False,
    )
```

```python
import functools
import math

import jax
import jax.numpy as jnp
from jax import lax
from jax.experimental import pallas as pl
from jax.experimental.pallas import tpu as pltpu
from jax.sharding import PartitionSpec as P

STEP = 0.5
LAMBDA_FRACTION = 0.05
EPSILON = 1e-06
DEGREES = 5
LANES = 128
ROOT_TWO = math.sqrt(2.0)
ROOT_SIX = math.sqrt(6.0)
ROOT_TWENTYFOUR = math.sqrt(24.0)
MIB = 1 << 20


def round_up(value, multiple):
    return -(-value // multiple) * multiple


def prepare_kernel(parts, me_ref, corr_ref, points_ref, turned_ref, packet_ref, *sent):
    turned = corr_ref[...].astype(jnp.float32).T
    turned_ref[...] = turned.astype(jnp.bfloat16)
    squares = jnp.sum(turned * turned, axis=0, keepdims=True)
    rows = points_ref.shape[0] // parts
    pieces = [
        jnp.concatenate(
            [points_ref[part * rows : (part + 1) * rows, :] for part in range(parts)],
            axis=1,
        )
    ]
    pieces += [
        squares[:, part * LANES : (part + 1) * LANES]
        for part in range(squares.shape[1] // LANES)
    ]
    used = rows + len(pieces) - 1
    if packet_ref.shape[0] > used:
        pieces.append(jnp.zeros((packet_ref.shape[0] - used, LANES), jnp.float32))
    packet_ref[...] = jnp.concatenate(pieces, axis=0)
    for k, block_ref in enumerate(sent):
        block_ref[...] = turned_ref[own_rows(me_ref, k, block_ref.shape[0]), :]


def own_rows(me_ref, k, count):
    return pl.ds(pl.multiple_of((me_ref[0] ^ k) * count, count), count)


def hermite_columns(points):
    squared = points * points
    return jnp.concatenate(
        [
            jnp.ones_like(points),
            points,
            (squared - 1.0) / ROOT_TWO,
            points * (squared - 3.0) / ROOT_SIX,
            (squared * squared - 6.0 * squared + 3.0) / ROOT_TWENTYFOUR,
        ],
        axis=0,
    )


def design_kernel(dim, run_count, me_ref, codes_ref, *refs):
    *packet_refs, design_ref, exact, table, chosen = refs
    half = exact.shape[1]
    parts = LANES // run_count
    rows = dim // parts

    @pl.when(pl.program_id(0) == 0)
    def _():
        for group in range(len(packet_refs) // parts):
            points = jnp.concatenate(
                [
                    jnp.concatenate(
                        [
                            packet_refs[group * parts + i][
                                0:rows, part * run_count : (part + 1) * run_count
                            ]
                            for i in range(parts)
                        ],
                        axis=1,
                    )
                    for part in range(parts)
                ],
                axis=0,
            )
            columns = hermite_columns(points)
            columns = jnp.concatenate(
                [
                    columns,
                    jnp.zeros((half - columns.shape[0], LANES), jnp.float32),
                ],
                axis=0,
            ).T
            high = columns.astype(jnp.bfloat16)
            low = (columns - high.astype(jnp.float32)).astype(jnp.bfloat16)
            block = slice(group * LANES, (group + 1) * LANES)
            exact[block, :] = columns
            table[block, 0:half] = high
            table[block, half : 2 * half] = low

    codes = codes_ref[...]
    spots = (codes % DEGREES) * dim + codes // DEGREES
    slots, terms = codes.shape
    row = lax.broadcasted_iota(jnp.int32, (half, terms), 0)
    matmuls = chosen.shape[0]
    for slot in range(matmuls):
        picked = jnp.where(row == spots[slot : slot + 1, :], 1.0, 0.0).astype(
            jnp.bfloat16
        )
        chosen[slot, 0:half, :] = picked
        chosen[slot, half : 2 * half, :] = picked
    for start in range(0, table.shape[0], LANES):
        block = slice(start, start + LANES)
        rows = exact[block, :]
        product = None
        for slot in range(matmuls):
            factor = jnp.dot(
                table[block, :], chosen[slot], preferred_element_type=jnp.float32
            )
            product = factor if product is None else product * factor
        for part in range(0, terms, half):
            lanes = slice(part, part + half)
            factor = product[:, lanes]
            for slot in range(matmuls, slots):
                spot = jnp.broadcast_to(spots[slot : slot + 1, lanes], rows.shape)
                factor = factor * jnp.take_along_axis(rows, spot, axis=1)
            design_ref[block, lanes] = factor.astype(jnp.bfloat16)


def shrink_factor(squares, limits):
    return jnp.maximum(0.0, 1.0 - limits / jnp.sqrt(squares + EPSILON))


def fit_kernel(first_row, total_runs, me_ref, levels_ref, design_ref, *refs):
    devices = (len(refs) - 2) // 3
    packet_refs, corr_refs = refs[:devices], refs[devices : 2 * devices]
    summed_refs = refs[2 * devices : 3 * devices]
    scale_ref, first_ref = refs[3 * devices :]
    term_count = corr_refs[0].shape[1]
    squares = jnp.concatenate(
        [
            packet_ref[first_row + part : first_row + part + 1, :]
            for packet_ref in packet_refs
            for part in range(term_count // LANES)
        ],
        axis=1,
    )
    levels = jnp.concatenate(
        [levels_ref[:, own_rows(me_ref, k, term_count)] for k in range(devices)],
        axis=1,
    )
    weights = jnp.exp2(levels.astype(jnp.float32))
    ratio = jnp.max(jnp.sqrt(squares) / weights, axis=1, keepdims=True)
    limits = STEP * (LAMBDA_FRACTION * ratio) * weights
    factor = shrink_factor(STEP * STEP * squares, limits)
    scale_ref[0:1, :] = factor[:, 0:term_count]
    scale_ref[1:2, :] = limits[:, 0:term_count]
    for k in range(devices):
        terms = slice(k * term_count, (k + 1) * term_count)
        first = STEP * corr_refs[k][...].astype(jnp.float32) * factor[:, terms]
        first_ref[:, terms] = first.astype(jnp.bfloat16)
    fitted = lax.dot_general(
        first_ref[...],
        design_ref[...],
        (((1,), (1,)), ((), ())),
        preferred_element_type=jnp.float32,
    ).astype(jnp.bfloat16)
    for k in range(devices):
        terms = slice(k * term_count, (k + 1) * term_count)
        summed = jnp.dot(
            fitted, design_ref[:, terms], preferred_element_type=jnp.float32
        )
        summed_refs[k][...] = (summed / total_runs).astype(jnp.bfloat16)


def reorder_kernel(map_ref, slab_ref, modes_ref, turned):
    cells, block = slab_ref.shape[0], modes_ref.shape[1]

    @pl.when(pl.program_id(0) == 0)
    def _():
        for start in range(0, cells, LANES):
            rows = slice(start, start + LANES)
            turned[:, rows] = slab_ref[rows, :].T

    row = lax.broadcasted_iota(jnp.int32, (cells, block), 0)
    chosen = jnp.where(row == map_ref[...], 1.0, 0.0).astype(jnp.bfloat16)
    modes_ref[...] = jnp.dot(
        turned[...], chosen, preferred_element_type=jnp.float32
    ).astype(jnp.bfloat16)


def finish_kernel(me_ref, corr_ref, scale_ref, modes_ref, *refs):
    *summed_refs, out_ref, lifted_ref, moved, values, half, lifted, out_sem, lifted_sem = refs
    modes, terms = corr_ref.shape
    count = summed_refs[0].shape[0]
    squares = jnp.zeros((1, terms), jnp.float32)
    for k, summed_ref in enumerate(summed_refs):
        rows = own_rows(me_ref, k, count)
        corr = corr_ref[rows, :].astype(jnp.float32)
        first = STEP * corr * scale_ref[0:1, :]
        gradient = summed_ref[...].astype(jnp.float32) - corr
        step = first - STEP * gradient
        moved[rows, :] = step
        squares = squares + jnp.sum(step * step, axis=0, keepdims=True)
    factor = shrink_factor(squares, scale_ref[1:2, :])
    for start in range(0, modes, LANES):
        block = slice(start, start + LANES)
        turned = (moved[block, :] * factor).T
        values[:, block] = turned
        half[:, block] = turned.astype(jnp.bfloat16)
    copies = [pltpu.make_async_copy(values, out_ref, out_sem)]
    copies[0].start()
    width = lifted.shape[2]
    for i in range(lifted.shape[0]):
        block = slice(i * width, (i + 1) * width)
        lifted[i] = jnp.dot(
            half[...], modes_ref[:, block], preferred_element_type=jnp.float32
        ).astype(jnp.bfloat16)
        copies.append(
            pltpu.make_async_copy(
                lifted.at[i], lifted_ref.at[:, block], lifted_sem.at[i]
            )
        )
        copies[-1].start()
    for copy in copies:
        copy.wait()


def in_hbm(array):
    return pltpu.with_memory_space_constraint(array, pltpu.HBM)


def params(limit):
    return pltpu.CompilerParams(vmem_limit_bytes=limit * MIB)


def cost(flops, moved):
    return pl.CostEstimate(flops=flops, bytes_accessed=moved, transcendentals=0)


def to_partner(array, k):
    devices = lax.axis_size("runs")
    return lax.ppermute(array, "runs", [(i, i ^ k) for i in range(devices)])


def split_by_modes(
    run_inputs, term_codes, weight_levels, correlations, slab_modes, cell_map
):
    run_count, dim = run_inputs.shape
    term_count, modes = correlations.shape
    terms, slots = term_codes.shape
    cells = slab_modes.shape[0]
    slab_cells = cell_map.shape[0]
    devices = lax.axis_size("runs")
    total_runs = run_count * devices
    own_modes = modes // devices
    parts = LANES // run_count
    first_row = dim // parts
    packet_rows = round_up(first_row + term_count // LANES, 8)
    me = lax.axis_index("runs").astype(jnp.int32).reshape(1)
    smem = pl.BlockSpec(memory_space=pltpu.SMEM)
    vmem = pl.BlockSpec(memory_space=pltpu.VMEM)
    anywhere = pl.BlockSpec(memory_space=pl.ANY)
    block_type = jax.ShapeDtypeStruct((own_modes, term_count), jnp.bfloat16)

    turned, packet, *sent = pl.pallas_call(
        functools.partial(prepare_kernel, parts),
        in_specs=[smem, vmem, vmem],
        out_specs=[vmem] * (2 + devices),
        out_shape=[
            jax.ShapeDtypeStruct((modes, term_count), jnp.bfloat16),
            jax.ShapeDtypeStruct((packet_rows, LANES), jnp.float32),
        ]
        + [block_type] * devices,
        compiler_params=params(16),
        name="prepare",
    )(me, in_hbm(correlations), in_hbm(run_inputs.T))
    packets = [packet] + [to_partner(packet, k) for k in range(1, devices)]
    blocks = sent[:1] + [to_partner(sent[k], k) for k in range(1, devices)]

    tile = term_count
    half = round_up(DEGREES * dim, LANES)
    design = pl.pallas_call(
        functools.partial(design_kernel, dim, run_count),
        grid_spec=pltpu.PrefetchScalarGridSpec(
            num_scalar_prefetch=1,
            grid=(terms // tile,),
            in_specs=[pl.BlockSpec((slots, tile), lambda i, me: (0, me[0] ^ i))]
            + [pl.BlockSpec((packet_rows, LANES), lambda i, me: (0, 0))] * devices,
            out_specs=pl.BlockSpec((total_runs, tile), lambda i, me: (0, i)),
            scratch_shapes=[
                pltpu.VMEM((total_runs, half), jnp.float32),
                pltpu.VMEM((total_runs, 2 * half), jnp.bfloat16),
                pltpu.VMEM((slots - slots // 4, 2 * half, tile), jnp.bfloat16),
            ],
        ),
        out_shape=jax.ShapeDtypeStruct((total_runs, terms), jnp.bfloat16),
        compiler_params=params(16),
        cost_estimate=cost(
            4 * total_runs * terms * slots * half, 2 * total_runs * terms
        ),
        name="design",
    )(me, in_hbm(term_codes.T), *packets)

    *summed, scale = pl.pallas_call(
        functools.partial(fit_kernel, first_row, float(total_runs)),
        in_specs=[smem] + [vmem] * (2 + 2 * devices),
        out_specs=[vmem] * (devices + 1),
        out_shape=[block_type] * devices
        + [jax.ShapeDtypeStruct((8, term_count), jnp.float32)],
        scratch_shapes=[pltpu.VMEM((own_modes, terms), jnp.bfloat16)],
        compiler_params=params(24),
        cost_estimate=cost(4 * total_runs * terms * own_modes, 2 * total_runs * terms),
        name="fit",
    )(me, weight_levels[None, :], design, *packets, *blocks)
    returned = summed[:1] + [to_partner(summed[k], k) for k in range(1, devices)]

    block = math.gcd(512, slab_cells)
    ordered = pl.pallas_call(
        reorder_kernel,
        grid=(slab_cells // block,),
        in_specs=[
            pl.BlockSpec((1, block), lambda i: (0, i)),
            pl.BlockSpec((cells, modes), lambda i: (0, 0)),
        ],
        out_specs=pl.BlockSpec((modes, block), lambda i: (0, i)),
        out_shape=jax.ShapeDtypeStruct((modes, slab_cells), jnp.bfloat16),
        scratch_shapes=[pltpu.VMEM((modes, cells), jnp.bfloat16)],
        compiler_params=params(24),
        cost_estimate=cost(2 * cells * slab_cells * modes, 4 * cells * modes),
        name="reorder",
    )(cell_map[None, :], in_hbm(slab_modes))

    return pl.pallas_call(
        finish_kernel,
        in_specs=[smem] + [vmem] * (3 + devices),
        out_specs=(anywhere, anywhere),
        out_shape=(
            jax.ShapeDtypeStruct((term_count, modes), jnp.float32),
            jax.ShapeDtypeStruct((term_count, slab_cells), jnp.bfloat16),
        ),
        scratch_shapes=[
            pltpu.VMEM((modes, term_count), jnp.float32),
            pltpu.VMEM((term_count, modes), jnp.float32),
            pltpu.VMEM((term_count, modes), jnp.bfloat16),
            pltpu.VMEM((slab_cells // block, term_count, block), jnp.bfloat16),
            pltpu.SemaphoreType.DMA,
            pltpu.SemaphoreType.DMA((slab_cells // block,)),
        ],
        compiler_params=params(20),
        name="finish",
    )(me, turned, scale, ordered, *returned)


def hermite_table(points):
    squared = points * points
    columns = [
        jnp.ones_like(points),
        points,
        (squared - 1.0) / ROOT_TWO,
        points * (squared - 3.0) / ROOT_SIX,
        (squared * squared - 6.0 * squared + 3.0) / ROOT_TWENTYFOUR,
    ]
    return jnp.stack(columns, axis=-1).reshape(points.shape[0], -1)


def basis(points, codes):
    hermite = hermite_table(points)
    product = jnp.take(hermite, codes[:, 0], axis=1)
    for column in range(1, codes.shape[1]):
        product = product * jnp.take(hermite, codes[:, column], axis=1)
    return product.astype(jnp.bfloat16)


def shrink(values, limits):
    length = jnp.sqrt(jnp.sum(values * values, axis=1, keepdims=True) + EPSILON)
    return values * jnp.maximum(0.0, 1.0 - limits[:, None] / length)


def transposed_product(left, right):
    return lax.dot_general(
        left, right, (((0,), (0,)), ((), ())), preferred_element_type=jnp.float32
    )


def split_by_runs(
    run_inputs, term_codes, weight_levels, correlations, slab_modes, cell_map
):
    run_count = run_inputs.shape[0]
    term_count = correlations.shape[0]
    devices = lax.axis_size("runs")
    offset = lax.axis_index("runs") * term_count
    total_runs = run_count * devices
    weights_all = jnp.exp2(weight_levels.astype(jnp.float32))
    own_weights = lax.dynamic_slice_in_dim(weights_all, offset, term_count)
    own_corr = correlations.astype(jnp.float32)
    ratio = jnp.max(jnp.sqrt(jnp.sum(own_corr * own_corr, axis=1)) / own_weights)
    penalty = LAMBDA_FRACTION * lax.pmax(ratio, "runs")
    first = shrink(STEP * own_corr, STEP * penalty * own_weights)
    design = basis(run_inputs, term_codes)
    fitted = jnp.dot(
        design,
        lax.all_gather(first.astype(jnp.bfloat16), "runs", axis=0, tiled=True),
        preferred_element_type=jnp.float32,
    )
    fitted_half = fitted.astype(jnp.bfloat16)
    all_points = lax.all_gather(run_inputs, "runs", axis=0, tiled=True)
    own_codes = lax.dynamic_slice_in_dim(term_codes, offset, term_count, 0)
    owned_design = basis(all_points, own_codes)
    summed = transposed_product(
        owned_design, lax.all_gather(fitted_half, "runs", axis=0, tiled=True)
    )
    gradient = summed / total_runs - own_corr
    coefficients = shrink(first - STEP * gradient, STEP * penalty * own_weights)
    modes = jnp.take(slab_modes, cell_map, axis=0)
    lifted = lax.dot_general(
        coefficients.astype(jnp.bfloat16),
        modes,
        (((1,), (1,)), ((), ())),
        preferred_element_type=jnp.float32,
    ).astype(jnp.bfloat16)
    return (coefficients, lifted)


def on_device(
    run_inputs, term_codes, weight_levels, correlations, slab_modes, cell_map
):
    devices = lax.axis_size("runs")
    run_count = run_inputs.shape[0]
    term_count, modes = correlations.shape
    whole_tiles = (
        devices & (devices - 1) == 0
        and modes % (16 * devices) == 0
        and DEGREES * run_inputs.shape[1] <= LANES
        and term_count % LANES == 0
        and LANES % run_count == 0
        and devices % (LANES // run_count) == 0
        and run_inputs.shape[1] % (LANES // run_count) == 0
        and slab_modes.shape[0] % LANES == 0
        and cell_map.shape[0] % LANES == 0
    )
    plan = split_by_modes if whole_tiles else split_by_runs
    return plan(
        run_inputs, term_codes, weight_levels, correlations, slab_modes, cell_map
    )


def solution(mesh):
    return jax.shard_map(
        on_device,
        mesh=mesh,
        in_specs=(
            P(("cases", "runs"), None),
            P(),
            P(),
            P(("cases", "runs"), None),
            P("cases", None),
            P(),
        ),
        out_specs=(P(("cases", "runs"), None), P(("cases", "runs"), None)),
        check_vma=False,
    )
```

```python
import functools
import math

import jax
import jax.numpy as jnp
from jax import lax
from jax.experimental import pallas as pl
from jax.experimental.pallas import tpu as pltpu
from jax.sharding import PartitionSpec as P

STEP = 0.5
LAMBDA_FRACTION = 0.05
EPSILON = 1e-06
DEGREES = 5
LANES = 128
ROOT_TWO = math.sqrt(2.0)
ROOT_SIX = math.sqrt(6.0)
ROOT_TWENTYFOUR = math.sqrt(24.0)
MIB = 1 << 20


def round_up(value, multiple):
    return -(-value // multiple) * multiple


def split_in_two(values):
    high = values.astype(jnp.bfloat16).astype(jnp.float32)
    return [high, values - high]


def prepare_kernel(corr_ref, points_ref, turned_ref, sent_ref):
    turned = corr_ref[...].astype(jnp.float32).T
    squares = jnp.sum(turned * turned, axis=0, keepdims=True)
    devices, sent_rows, terms = sent_ref.shape
    count = turned.shape[0] // devices
    dim, runs = points_ref.shape
    rows = dim * runs // terms
    points = jnp.concatenate(
        [points_ref[start : start + rows, :] for start in range(0, dim, rows)], axis=1
    )
    pieces = split_in_two(points) + split_in_two(squares)
    used = 2 * rows + 2
    if sent_rows - count > used:
        pieces.append(jnp.zeros((sent_rows - count - used, terms), jnp.float32))
    packet = jnp.concatenate(pieces, axis=0).astype(jnp.bfloat16)
    for i in range(devices):
        block = turned[i * count : (i + 1) * count, :].astype(jnp.bfloat16)
        turned_ref[i * count : (i + 1) * count, :] = block
        sent_ref[i, 0:count, :] = block
        sent_ref[i, count:sent_rows, :] = packet


def hermite_columns(points):
    squared = points * points
    return jnp.concatenate(
        [
            jnp.ones_like(points),
            points,
            (squared - 1.0) / ROOT_TWO,
            points * (squared - 3.0) / ROOT_SIX,
            (squared * squared - 6.0 * squared + 3.0) / ROOT_TWENTYFOUR,
        ],
        axis=0,
    )


def design_kernel(
    dim, run_count, count, blocks_ref, codes_ref, design_ref, exact, table, chosen
):
    devices = blocks_ref.shape[0]
    half = exact.shape[1]
    rows = dim * run_count // blocks_ref.shape[2]

    @pl.when(pl.program_id(0) == 0)
    def _():
        per = LANES // run_count
        for group in range(devices // per):
            owned = []
            for i in range(per):
                packet = blocks_ref[
                    group * per + i, count : blocks_ref.shape[1], :
                ].astype(jnp.float32)
                owned.append(packet[0:rows, :] + packet[rows : 2 * rows, :])
            points = jnp.concatenate(
                [
                    jnp.concatenate(
                        [inputs[:, start : start + run_count] for inputs in owned],
                        axis=1,
                    )
                    for start in range(0, blocks_ref.shape[2], run_count)
                ],
                axis=0,
            )
            columns = hermite_columns(points)
            columns = jnp.concatenate(
                [
                    columns,
                    jnp.zeros((half - columns.shape[0], LANES), jnp.float32),
                ],
                axis=0,
            ).T
            high = columns.astype(jnp.bfloat16)
            low = (columns - high.astype(jnp.float32)).astype(jnp.bfloat16)
            block = slice(group * LANES, (group + 1) * LANES)
            exact[block, :] = columns
            table[block, 0:half] = high
            table[block, half : 2 * half] = low

    codes = codes_ref[...]
    spots = (codes % DEGREES) * dim + codes // DEGREES
    slots, terms = codes.shape
    row = lax.broadcasted_iota(jnp.int32, (half, terms), 0)
    matmuls = chosen.shape[0]
    for slot in range(matmuls):
        picked = jnp.where(row == spots[slot : slot + 1, :], 1.0, 0.0).astype(
            jnp.bfloat16
        )
        chosen[slot, 0:half, :] = picked
        chosen[slot, half : 2 * half, :] = picked
    for start in range(0, table.shape[0], LANES):
        block = slice(start, start + LANES)
        rows = exact[block, :]
        product = None
        for slot in range(matmuls):
            factor = jnp.dot(
                table[block, :], chosen[slot], preferred_element_type=jnp.float32
            )
            product = factor if product is None else product * factor
        for part in range(0, terms, half):
            lanes = slice(part, part + half)
            factor = product[:, lanes]
            for slot in range(matmuls, slots):
                spot = jnp.broadcast_to(spots[slot : slot + 1, lanes], rows.shape)
                factor = factor * jnp.take_along_axis(rows, spot, axis=1)
            design_ref[block, lanes] = factor.astype(jnp.bfloat16)


def penalty_rows(count, row, blocks_ref, levels_ref):
    rows = []
    for i in range(blocks_ref.shape[0]):
        packet = blocks_ref[i, count : blocks_ref.shape[1], :].astype(jnp.float32)
        rows.append(packet[row : row + 1, :] + packet[row + 1 : row + 2, :])
    squares = jnp.concatenate(rows, axis=1)
    weights = jnp.exp2(levels_ref[...].astype(jnp.float32))
    ratio = jnp.max(jnp.sqrt(squares) / weights, axis=1, keepdims=True)
    return squares, weights, LAMBDA_FRACTION * ratio


def shrink_factor(squares, limits):
    return jnp.maximum(0.0, 1.0 - limits / jnp.sqrt(squares + EPSILON))


def fit_kernel(
    row, total_runs, levels_ref, blocks_ref, design_ref, summed_ref, scale_ref, first_ref
):
    devices, count, term_count = summed_ref.shape
    squares, weights, penalty = penalty_rows(count, row, blocks_ref, levels_ref)
    limits = STEP * penalty * weights
    factor = shrink_factor(STEP * STEP * squares, limits)
    scale_ref[0:1, :] = factor
    scale_ref[1:2, :] = limits
    for i in range(devices):
        terms = slice(i * term_count, (i + 1) * term_count)
        first = (
            STEP * blocks_ref[i, 0:count, :].astype(jnp.float32) * factor[:, terms]
        )
        first_ref[:, terms] = first.astype(jnp.bfloat16)
    fitted = lax.dot_general(
        first_ref[...],
        design_ref[...],
        (((1,), (1,)), ((), ())),
        preferred_element_type=jnp.float32,
    ).astype(jnp.bfloat16)
    for i in range(devices):
        terms = slice(i * term_count, (i + 1) * term_count)
        summed = jnp.dot(
            fitted, design_ref[:, terms], preferred_element_type=jnp.float32
        )
        summed_ref[i] = (summed / total_runs).astype(jnp.bfloat16)


def reorder_kernel(map_ref, slab_ref, modes_ref, turned):
    cells, block = slab_ref.shape[0], modes_ref.shape[1]

    @pl.when(pl.program_id(0) == 0)
    def _():
        for start in range(0, cells, LANES):
            rows = slice(start, start + LANES)
            turned[:, rows] = slab_ref[rows, :].T

    row = lax.broadcasted_iota(jnp.int32, (cells, block), 0)
    chosen = jnp.where(row == map_ref[...], 1.0, 0.0).astype(jnp.bfloat16)
    modes_ref[...] = jnp.dot(
        turned[...], chosen, preferred_element_type=jnp.float32
    ).astype(jnp.bfloat16)


def finish_kernel(
    summed_ref,
    corr_ref,
    scale_ref,
    modes_ref,
    out_ref,
    lifted_ref,
    moved,
    values,
    half,
    lifted,
    held,
    held_sem,
    out_sem,
    lifted_sem,
):
    width = lifted.shape[2]
    loads = []
    for i in range(lifted.shape[0]):
        block = slice(i * width, (i + 1) * width)
        loads.append(
            pltpu.make_async_copy(
                modes_ref.at[:, block], held.at[:, block], held_sem.at[i]
            )
        )
        loads[-1].start()
    modes, terms = corr_ref.shape
    squares = jnp.zeros((1, terms), jnp.float32)
    for start in range(0, modes, LANES):
        block = slice(start, start + LANES)
        corr = corr_ref[block, :].astype(jnp.float32)
        first = STEP * corr * scale_ref[0:1, :]
        gradient = summed_ref[block, :].astype(jnp.float32) - corr
        step = first - STEP * gradient
        moved[block, :] = step
        squares = squares + jnp.sum(step * step, axis=0, keepdims=True)
    factor = shrink_factor(squares, scale_ref[1:2, :])
    for start in range(0, modes, LANES):
        block = slice(start, start + LANES)
        turned = (moved[block, :] * factor).T
        values[:, block] = turned
        half[:, block] = turned.astype(jnp.bfloat16)
    copies = [pltpu.make_async_copy(values, out_ref, out_sem)]
    copies[0].start()
    for i in range(lifted.shape[0]):
        block = slice(i * width, (i + 1) * width)
        loads[i].wait()
        lifted[i] = jnp.dot(
            half[...], held[:, block], preferred_element_type=jnp.float32
        ).astype(jnp.bfloat16)
        copies.append(
            pltpu.make_async_copy(
                lifted.at[i], lifted_ref.at[:, block], lifted_sem.at[i]
            )
        )
        copies[-1].start()
    for copy in copies:
        copy.wait()


def in_hbm(array):
    return pltpu.with_memory_space_constraint(array, pltpu.HBM)


def params(limit):
    return pltpu.CompilerParams(vmem_limit_bytes=limit * MIB)


def split_by_modes(
    run_inputs, term_codes, weight_levels, correlations, slab_modes, cell_map
):
    run_count, dim = run_inputs.shape
    term_count, modes = correlations.shape
    terms, slots = term_codes.shape
    cells = slab_modes.shape[0]
    slab_cells = cell_map.shape[0]
    devices = lax.axis_size("runs")
    total_runs = run_count * devices
    own_modes = modes // devices
    offset = lax.axis_index("runs") * term_count
    rows = dim * run_count // term_count
    sent_rows = round_up(own_modes + 2 * rows + 2, 16)
    vmem = pl.BlockSpec(memory_space=pltpu.VMEM)
    anywhere = pl.BlockSpec(memory_space=pl.ANY)

    turned, sent = pl.pallas_call(
        prepare_kernel,
        out_shape=(
            jax.ShapeDtypeStruct((modes, term_count), jnp.bfloat16),
            jax.ShapeDtypeStruct((devices, sent_rows, term_count), jnp.bfloat16),
        ),
        compiler_params=params(16),
        name="prepare",
    )(in_hbm(correlations), in_hbm(run_inputs.T))
    blocks = lax.all_to_all(sent, "runs", 0, 0, tiled=False)

    tile = term_count
    half = round_up(DEGREES * dim, LANES)
    design = pl.pallas_call(
        functools.partial(design_kernel, dim, run_count, own_modes),
        grid=(terms // tile,),
        in_specs=[
            pl.BlockSpec((devices, sent_rows, term_count), lambda i: (0, 0, 0)),
            pl.BlockSpec((slots, tile), lambda i: (0, i)),
        ],
        out_specs=pl.BlockSpec((total_runs, tile), lambda i: (0, i)),
        out_shape=jax.ShapeDtypeStruct((total_runs, terms), jnp.bfloat16),
        scratch_shapes=[
            pltpu.VMEM((total_runs, half), jnp.float32),
            pltpu.VMEM((total_runs, 2 * half), jnp.bfloat16),
            pltpu.VMEM((slots - slots // 4, 2 * half, tile), jnp.bfloat16),
        ],
        compiler_params=params(16),
        name="design",
    )(blocks, in_hbm(term_codes.T))

    summed, scale = pl.pallas_call(
        functools.partial(fit_kernel, 2 * rows, float(total_runs)),
        in_specs=[vmem, vmem, vmem],
        out_shape=(
            jax.ShapeDtypeStruct((devices, own_modes, term_count), jnp.bfloat16),
            jax.ShapeDtypeStruct((8, terms), jnp.float32),
        ),
        scratch_shapes=[pltpu.VMEM((own_modes, terms), jnp.bfloat16)],
        compiler_params=params(24),
        name="fit",
    )(weight_levels[None, :], blocks, design)
    own_scale = lax.dynamic_slice_in_dim(scale, offset, term_count, 1)
    returned = lax.all_to_all(summed, "runs", 0, 0, tiled=False).reshape(
        modes, term_count
    )

    block = math.gcd(512, slab_cells)
    ordered = pl.pallas_call(
        reorder_kernel,
        grid=(slab_cells // block,),
        in_specs=[
            pl.BlockSpec((1, block), lambda i: (0, i)),
            pl.BlockSpec((cells, modes), lambda i: (0, 0)),
        ],
        out_specs=pl.BlockSpec((modes, block), lambda i: (0, i)),
        out_shape=pltpu.HBM((modes, slab_cells), jnp.bfloat16),
        scratch_shapes=[pltpu.VMEM((modes, cells), jnp.bfloat16)],
        compiler_params=params(24),
        name="reorder",
    )(cell_map[None, :], in_hbm(slab_modes))

    return pl.pallas_call(
        finish_kernel,
        in_specs=[vmem, vmem, vmem, anywhere],
        out_specs=(anywhere, anywhere),
        out_shape=(
            jax.ShapeDtypeStruct((term_count, modes), jnp.float32),
            jax.ShapeDtypeStruct((term_count, slab_cells), jnp.bfloat16),
        ),
        scratch_shapes=[
            pltpu.VMEM((modes, term_count), jnp.float32),
            pltpu.VMEM((term_count, modes), jnp.float32),
            pltpu.VMEM((term_count, modes), jnp.bfloat16),
            pltpu.VMEM((slab_cells // block, term_count, block), jnp.bfloat16),
            pltpu.VMEM((modes, slab_cells), jnp.bfloat16),
            pltpu.SemaphoreType.DMA((slab_cells // block,)),
            pltpu.SemaphoreType.DMA,
            pltpu.SemaphoreType.DMA((slab_cells // block,)),
        ],
        compiler_params=params(20),
        name="finish",
    )(returned, turned, own_scale, in_hbm(ordered))


def hermite_table(points):
    squared = points * points
    columns = [
        jnp.ones_like(points),
        points,
        (squared - 1.0) / ROOT_TWO,
        points * (squared - 3.0) / ROOT_SIX,
        (squared * squared - 6.0 * squared + 3.0) / ROOT_TWENTYFOUR,
    ]
    return jnp.stack(columns, axis=-1).reshape(points.shape[0], -1)


def basis(points, codes):
    hermite = hermite_table(points)
    product = jnp.take(hermite, codes[:, 0], axis=1)
    for column in range(1, codes.shape[1]):
        product = product * jnp.take(hermite, codes[:, column], axis=1)
    return product.astype(jnp.bfloat16)


def shrink(values, limits):
    length = jnp.sqrt(jnp.sum(values * values, axis=1, keepdims=True) + EPSILON)
    return values * jnp.maximum(0.0, 1.0 - limits[:, None] / length)


def transposed_product(left, right):
    return lax.dot_general(
        left, right, (((0,), (0,)), ((), ())), preferred_element_type=jnp.float32
    )


def split_by_runs(
    run_inputs, term_codes, weight_levels, correlations, slab_modes, cell_map
):
    run_count = run_inputs.shape[0]
    term_count = correlations.shape[0]
    devices = lax.axis_size("runs")
    offset = lax.axis_index("runs") * term_count
    total_runs = run_count * devices
    weights_all = jnp.exp2(weight_levels.astype(jnp.float32))
    own_weights = lax.dynamic_slice_in_dim(weights_all, offset, term_count)
    own_corr = correlations.astype(jnp.float32)
    ratio = jnp.max(jnp.sqrt(jnp.sum(own_corr * own_corr, axis=1)) / own_weights)
    penalty = LAMBDA_FRACTION * lax.pmax(ratio, "runs")
    first = shrink(STEP * own_corr, STEP * penalty * own_weights)
    design = basis(run_inputs, term_codes)
    fitted = jnp.dot(
        design,
        lax.all_gather(first.astype(jnp.bfloat16), "runs", axis=0, tiled=True),
        preferred_element_type=jnp.float32,
    )
    fitted_half = fitted.astype(jnp.bfloat16)
    all_points = lax.all_gather(run_inputs, "runs", axis=0, tiled=True)
    own_codes = lax.dynamic_slice_in_dim(term_codes, offset, term_count, 0)
    owned_design = basis(all_points, own_codes)
    summed = transposed_product(
        owned_design, lax.all_gather(fitted_half, "runs", axis=0, tiled=True)
    )
    gradient = summed / total_runs - own_corr
    coefficients = shrink(first - STEP * gradient, STEP * penalty * own_weights)
    modes = jnp.take(slab_modes, cell_map, axis=0)
    lifted = lax.dot_general(
        coefficients.astype(jnp.bfloat16),
        modes,
        (((1,), (1,)), ((), ())),
        preferred_element_type=jnp.float32,
    ).astype(jnp.bfloat16)
    return (coefficients, lifted)


def on_device(
    run_inputs, term_codes, weight_levels, correlations, slab_modes, cell_map
):
    devices = lax.axis_size("runs")
    run_count = run_inputs.shape[0]
    term_count, modes = correlations.shape
    whole_tiles = (
        modes % (16 * devices) == 0
        and DEGREES * run_inputs.shape[1] <= LANES
        and term_count % LANES == 0
        and LANES % run_count == 0
        and devices % (LANES // run_count) == 0
        and term_count % run_count == 0
        and run_inputs.shape[1] % (term_count // run_count) == 0
        and slab_modes.shape[0] % LANES == 0
        and cell_map.shape[0] % LANES == 0
    )
    plan = split_by_modes if whole_tiles else split_by_runs
    return plan(
        run_inputs, term_codes, weight_levels, correlations, slab_modes, cell_map
    )


def solution(mesh):
    return jax.shard_map(
        on_device,
        mesh=mesh,
        in_specs=(
            P(("cases", "runs"), None),
            P(),
            P(),
            P(("cases", "runs"), None),
            P("cases", None),
            P(),
        ),
        out_specs=(P(("cases", "runs"), None), P(("cases", "runs"), None)),
        check_vma=False,
    )
```

```python
import functools
import math

import jax
import jax.numpy as jnp
from jax import lax
from jax.experimental import pallas as pl
from jax.experimental.pallas import tpu as pltpu
from jax.sharding import PartitionSpec as P

STEP = 0.5
LAMBDA_FRACTION = 0.05
EPSILON = 1e-06
DEGREES = 5
LANES = 128
CORES = 2
ROOT_TWO = math.sqrt(2.0)
ROOT_SIX = math.sqrt(6.0)
ROOT_TWENTYFOUR = math.sqrt(24.0)
MIB = 1 << 20


def round_up(value, multiple):
    return -(-value // multiple) * multiple


def split_in_two(values):
    high = values.astype(jnp.bfloat16).astype(jnp.float32)
    return [high, values - high]


def rows_of(index, count):
    return pl.ds(pl.multiple_of(index * count, count), count)


def prepare_kernel(me_ref, corr_ref, points_ref, turned_ref, *sent_refs):
    turned = corr_ref[...].astype(jnp.float32).T
    turned_ref[...] = turned.astype(jnp.bfloat16)
    squares = jnp.sum(turned * turned, axis=0, keepdims=True)
    sent_rows, terms = sent_refs[0].shape
    count = turned.shape[0] // len(sent_refs)
    dim, runs = points_ref.shape
    rows = dim * runs // terms
    points = jnp.concatenate(
        [points_ref[start : start + rows, :] for start in range(0, dim, rows)], axis=1
    )
    pieces = split_in_two(points) + split_in_two(squares)
    used = 2 * rows + 2
    if sent_rows - count > used:
        pieces.append(jnp.zeros((sent_rows - count - used, terms), jnp.float32))
    packet = jnp.concatenate(pieces, axis=0).astype(jnp.bfloat16)
    for k, sent_ref in enumerate(sent_refs):
        chip = (me_ref[0] // CORES) ^ k
        sent_ref[0:count, :] = turned_ref[rows_of(chip, count), :]
        sent_ref[count:sent_rows, :] = packet


def split_in_two(values):
    high = values.astype(jnp.bfloat16).astype(jnp.float32)
    return [high, values - high]


def hermite_columns(points):
    squared = points * points
    return jnp.concatenate(
        [
            jnp.ones_like(points),
            points,
            (squared - 1.0) / ROOT_TWO,
            points * (squared - 3.0) / ROOT_SIX,
            (squared * squared - 6.0 * squared + 3.0) / ROOT_TWENTYFOUR,
        ],
        axis=0,
    )


def design_kernel(dim, run_count, me_ref, codes_ref, own_ref, other_ref, *refs):
    design_ref, exact, table, chosen = refs[-4:]
    chips, _, terms = own_ref.shape
    half = exact.shape[1]
    rows = dim * run_count // terms
    core = me_ref[0] % CORES

    @pl.when(pl.program_id(0) == 0)
    def _():
        per = LANES // run_count
        sources = [
            (packets_ref, group, base)
            for packets_ref, base in ((own_ref, core), (other_ref, 1 - core))
            for group in range(chips // per)
        ]
        for packets_ref, group, base in sources:
            owned = []
            for i in range(per):
                packet = packets_ref[group * per + i].astype(jnp.float32)
                owned.append(packet[0:rows, :] + packet[rows : 2 * rows, :])
            points = jnp.concatenate(
                [
                    jnp.concatenate(
                        [inputs[:, start : start + run_count] for inputs in owned],
                        axis=1,
                    )
                    for start in range(0, terms, run_count)
                ],
                axis=0,
            )
            columns = hermite_columns(points)
            columns = jnp.concatenate(
                [
                    columns,
                    jnp.zeros((half - columns.shape[0], LANES), jnp.float32),
                ],
                axis=0,
            ).T
            high = columns.astype(jnp.bfloat16)
            low = (columns - high.astype(jnp.float32)).astype(jnp.bfloat16)
            block = rows_of(base * (chips // per) + group, LANES)
            exact[block, :] = columns
            table[block, 0:half] = high
            table[block, half : 2 * half] = low

    codes = codes_ref[...]
    spots = (codes % DEGREES) * dim + codes // DEGREES
    slots, terms = codes.shape
    row = lax.broadcasted_iota(jnp.int32, (half, terms), 0)
    matmuls = chosen.shape[0]
    for slot in range(matmuls):
        picked = jnp.where(row == spots[slot : slot + 1, :], 1.0, 0.0).astype(
            jnp.bfloat16
        )
        chosen[slot, 0:half, :] = picked
        chosen[slot, half : 2 * half, :] = picked
    for start in range(0, table.shape[0], LANES):
        block = slice(start, start + LANES)
        rows = exact[block, :]
        product = None
        for slot in range(matmuls):
            factor = jnp.dot(
                table[block, :], chosen[slot], preferred_element_type=jnp.float32
            )
            product = factor if product is None else product * factor
        for part in range(0, terms, half):
            lanes = slice(part, part + half)
            factor = product[:, lanes]
            for slot in range(matmuls, slots):
                spot = jnp.broadcast_to(spots[slot : slot + 1, lanes], rows.shape)
                factor = factor * jnp.take_along_axis(rows, spot, axis=1)
            design_ref[block, lanes] = factor.astype(jnp.bfloat16)


def shrink_factor(squares, limits):
    return jnp.maximum(0.0, 1.0 - limits / jnp.sqrt(squares + EPSILON))


def rows_and_weights(row, first, packets_ref, levels_ref):
    squares, levels = [], []
    for k in range(packets_ref.shape[0]):
        packet = packets_ref[k].astype(jnp.float32)
        squares.append(packet[row : row + 1, :] + packet[row + 1 : row + 2, :])
        device = first ^ (CORES * k)
        levels.append(levels_ref[:, rows_of(device, packets_ref.shape[2])])
    weights = jnp.exp2(jnp.concatenate(levels, axis=1).astype(jnp.float32))
    return jnp.concatenate(squares, axis=1), weights


def fit_kernel(row, me_ref, levels_ref, own_ref, other_ref, design_ref, *refs):
    *block_refs, fitted_ref, scale_ref, first_ref = refs
    count = fitted_ref.shape[0]
    term_count = own_ref.shape[2]
    me = me_ref[0]
    squares, weights = rows_and_weights(row, me, own_ref, levels_ref)
    others, other_weights = rows_and_weights(row, me ^ 1, other_ref, levels_ref)
    ratio = jnp.maximum(
        jnp.max(jnp.sqrt(squares) / weights, axis=1, keepdims=True),
        jnp.max(jnp.sqrt(others) / other_weights, axis=1, keepdims=True),
    )
    limits = STEP * (LAMBDA_FRACTION * ratio) * weights
    factor = shrink_factor(STEP * STEP * squares, limits)
    scale_ref[0:1, :] = factor[:, 0:term_count]
    scale_ref[1:2, :] = limits[:, 0:term_count]
    for k, block_ref in enumerate(block_refs):
        terms = slice(k * term_count, (k + 1) * term_count)
        first = STEP * block_ref[0:count, :].astype(jnp.float32) * factor[:, terms]
        first_ref[:, terms] = first.astype(jnp.bfloat16)
    fitted_ref[...] = lax.dot_general(
        first_ref[...],
        design_ref[...],
        (((1,), (1,)), ((), ())),
        preferred_element_type=jnp.float32,
    )


def sum_kernel(total_runs, own_ref, other_ref, design_ref, *summed_refs):
    fitted = (own_ref[...] + other_ref[...]).astype(jnp.bfloat16)
    term_count = summed_refs[0].shape[1]
    for k, summed_ref in enumerate(summed_refs):
        terms = slice(k * term_count, (k + 1) * term_count)
        summed = jnp.dot(
            fitted, design_ref[:, terms], preferred_element_type=jnp.float32
        )
        summed_ref[...] = (summed / total_runs).astype(jnp.bfloat16)


def reorder_kernel(map_ref, slab_ref, *refs):
    modes_ref = refs[-1]
    cells, block = slab_ref.shape[0], modes_ref.shape[0]
    row = lax.broadcasted_iota(jnp.int32, (cells, block), 0)
    chosen = jnp.where(row == map_ref[...], 1.0, 0.0).astype(jnp.bfloat16)
    modes_ref[...] = lax.dot_general(
        chosen,
        slab_ref[...],
        (((0,), (0,)), ((), ())),
        preferred_element_type=jnp.float32,
    ).astype(jnp.bfloat16)


def finish_kernel(pieces, me_ref, corr_ref, scale_ref, *refs):
    modes_refs, refs = refs[:pieces], refs[pieces:]
    *summed_refs, out_ref, lifted_ref, moved, values, half, lifted, out_sem, sems = refs
    modes, terms = corr_ref.shape
    count = summed_refs[0].shape[0]
    squares = jnp.zeros((1, terms), jnp.float32)
    for k, summed_ref in enumerate(summed_refs):
        rows = rows_of((me_ref[0] // CORES) ^ k, count)
        corr = corr_ref[rows, :].astype(jnp.float32)
        first = STEP * corr * scale_ref[0:1, :]
        gradient = summed_ref[...].astype(jnp.float32) - corr
        step = first - STEP * gradient
        moved[rows, :] = step
        squares = squares + jnp.sum(step * step, axis=0, keepdims=True)
    factor = shrink_factor(squares, scale_ref[1:2, :])
    for start in range(0, modes, LANES):
        block = slice(start, start + LANES)
        turned = (moved[block, :] * factor).T
        values[:, block] = turned
        half[:, block] = turned.astype(jnp.bfloat16)
    copies = [pltpu.make_async_copy(values, out_ref, out_sem)]
    copies[0].start()
    width = lifted.shape[2]
    for i, modes_ref in enumerate(modes_refs):
        block = slice(i * width, (i + 1) * width)
        lifted[i] = lax.dot_general(
            half[...],
            modes_ref[...],
            (((1,), (1,)), ((), ())),
            preferred_element_type=jnp.float32,
        ).astype(jnp.bfloat16)
        copies.append(
            pltpu.make_async_copy(lifted.at[i], lifted_ref.at[:, block], sems.at[i])
        )
        copies[-1].start()
    for copy in copies:
        copy.wait()


def in_hbm(array):
    return pltpu.with_memory_space_constraint(array, pltpu.HBM)


def params(limit):
    return pltpu.CompilerParams(vmem_limit_bytes=limit * MIB)


def cost(flops, moved):
    return pl.CostEstimate(flops=flops, bytes_accessed=moved, transcendentals=0)


def to_device(array, bits):
    devices = lax.axis_size("runs")
    return lax.ppermute(array, "runs", [(i, i ^ bits) for i in range(devices)])


def to_chips(arrays):
    moved = {0: arrays[0]}
    chips = len(arrays)
    for k in [*range(chips // 2, chips), *range(1, chips // 2)]:
        moved[k] = to_device(arrays[k], CORES * k)
    return [moved[k] for k in range(chips)]


def split_by_modes(
    run_inputs, term_codes, weight_levels, correlations, slab_modes, cell_map
):
    run_count, dim = run_inputs.shape
    term_count, modes = correlations.shape
    terms, slots = term_codes.shape
    cells = slab_modes.shape[0]
    slab_cells = cell_map.shape[0]
    chips = lax.axis_size("runs") // CORES
    total_runs = run_count * CORES * chips
    core_terms = terms // CORES
    own_modes = modes // chips
    rows = dim * run_count // term_count
    packet_rows = round_up(2 * rows + 2, 16)
    me = lax.axis_index("runs").astype(jnp.int32).reshape(1)
    smem = pl.BlockSpec(memory_space=pltpu.SMEM)
    vmem = pl.BlockSpec(memory_space=pltpu.VMEM)
    anywhere = pl.BlockSpec(memory_space=pl.ANY)

    turned, *sent = pl.pallas_call(
        prepare_kernel,
        in_specs=[smem, vmem, vmem],
        out_specs=[vmem] * (1 + chips),
        out_shape=[jax.ShapeDtypeStruct((modes, term_count), jnp.bfloat16)]
        + [jax.ShapeDtypeStruct((own_modes + packet_rows, term_count), jnp.bfloat16)]
        * chips,
        compiler_params=params(16),
        name="prepare",
    )(me, in_hbm(correlations), in_hbm(run_inputs.T))
    blocks = to_chips(sent)

    block = math.gcd(512, slab_cells)

    def reorder(start, *after):
        return pl.pallas_call(
            reorder_kernel,
            in_specs=[vmem, vmem] + [anywhere] * len(after),
            out_specs=vmem,
            out_shape=jax.ShapeDtypeStruct((block, modes), jnp.bfloat16),
            compiler_params=params(16),
            cost_estimate=cost(2 * cells * block * modes, 2 * cells * modes),
            name="reorder",
        )(cell_map[None, start : start + block], slab_modes, *after)

    starts = range(0, slab_cells, block)
    early = len(starts) // 2
    ordered = [reorder(start) for start in starts[:early]]
    packets = jnp.stack([block[own_modes:] for block in blocks])
    others = to_device(packets, 1)

    tile = term_count
    half = round_up(DEGREES * dim, LANES)
    packets_spec = pl.BlockSpec(
        (chips, packet_rows, term_count), lambda i, me: (0, 0, 0)
    )
    design = pl.pallas_call(
        functools.partial(design_kernel, dim, run_count),
        grid_spec=pltpu.PrefetchScalarGridSpec(
            num_scalar_prefetch=1,
            grid=(chips,),
            in_specs=[
                pl.BlockSpec((slots, tile), lambda i, me: (0, me[0] ^ (CORES * i))),
                packets_spec,
                packets_spec,
            ]
            + [anywhere] * early,
            out_specs=pl.BlockSpec((total_runs, tile), lambda i, me: (0, i)),
            scratch_shapes=[
                pltpu.VMEM((total_runs, half), jnp.float32),
                pltpu.VMEM((total_runs, 2 * half), jnp.bfloat16),
                pltpu.VMEM((slots - slots // 4, 2 * half, tile), jnp.bfloat16),
            ],
        ),
        out_shape=jax.ShapeDtypeStruct((total_runs, core_terms), jnp.bfloat16),
        compiler_params=params(16),
        cost_estimate=cost(
            4 * total_runs * core_terms * slots * half, 2 * total_runs * core_terms
        ),
        name="design",
    )(me, in_hbm(term_codes.T), packets, others, *ordered)

    fit_cost = cost(
        2 * total_runs * core_terms * own_modes, 2 * total_runs * core_terms
    )
    fitted, scale = pl.pallas_call(
        functools.partial(fit_kernel, 2 * rows),
        in_specs=[smem] + [vmem] * (4 + chips),
        out_specs=[vmem, vmem],
        out_shape=[
            jax.ShapeDtypeStruct((own_modes, total_runs), jnp.float32),
            jax.ShapeDtypeStruct((8, term_count), jnp.float32),
        ],
        scratch_shapes=[pltpu.VMEM((own_modes, core_terms), jnp.bfloat16)],
        compiler_params=params(16),
        cost_estimate=fit_cost,
        name="fit",
    )(me, weight_levels[None, :], packets, others, design, *blocks)
    summed = pl.pallas_call(
        functools.partial(sum_kernel, float(total_runs)),
        in_specs=[vmem] * 3,
        out_specs=[vmem] * chips,
        out_shape=[jax.ShapeDtypeStruct((own_modes, term_count), jnp.bfloat16)] * chips,
        compiler_params=params(16),
        cost_estimate=fit_cost,
        name="sum",
    )(fitted, to_device(fitted, 1), design)
    returned = to_chips(summed)
    ordered += [reorder(start, summed[0]) for start in starts[early:]]

    return pl.pallas_call(
        functools.partial(finish_kernel, len(ordered)),
        in_specs=[smem] + [vmem] * (2 + len(ordered) + chips),
        out_specs=(anywhere, anywhere),
        out_shape=(
            jax.ShapeDtypeStruct((term_count, modes), jnp.float32),
            jax.ShapeDtypeStruct((term_count, slab_cells), jnp.bfloat16),
        ),
        scratch_shapes=[
            pltpu.VMEM((modes, term_count), jnp.float32),
            pltpu.VMEM((term_count, modes), jnp.float32),
            pltpu.VMEM((term_count, modes), jnp.bfloat16),
            pltpu.VMEM((len(ordered), term_count, block), jnp.bfloat16),
            pltpu.SemaphoreType.DMA,
            pltpu.SemaphoreType.DMA((len(ordered),)),
        ],
        compiler_params=params(20),
        name="finish",
    )(me, turned, scale, *ordered, *returned)


def hermite_table(points):
    squared = points * points
    columns = [
        jnp.ones_like(points),
        points,
        (squared - 1.0) / ROOT_TWO,
        points * (squared - 3.0) / ROOT_SIX,
        (squared * squared - 6.0 * squared + 3.0) / ROOT_TWENTYFOUR,
    ]
    return jnp.stack(columns, axis=-1).reshape(points.shape[0], -1)


def basis(points, codes):
    hermite = hermite_table(points)
    product = jnp.take(hermite, codes[:, 0], axis=1)
    for column in range(1, codes.shape[1]):
        product = product * jnp.take(hermite, codes[:, column], axis=1)
    return product.astype(jnp.bfloat16)


def shrink(values, limits):
    length = jnp.sqrt(jnp.sum(values * values, axis=1, keepdims=True) + EPSILON)
    return values * jnp.maximum(0.0, 1.0 - limits[:, None] / length)


def transposed_product(left, right):
    return lax.dot_general(
        left, right, (((0,), (0,)), ((), ())), preferred_element_type=jnp.float32
    )


def split_by_runs(
    run_inputs, term_codes, weight_levels, correlations, slab_modes, cell_map
):
    run_count = run_inputs.shape[0]
    term_count = correlations.shape[0]
    devices = lax.axis_size("runs")
    offset = lax.axis_index("runs") * term_count
    total_runs = run_count * devices
    weights_all = jnp.exp2(weight_levels.astype(jnp.float32))
    own_weights = lax.dynamic_slice_in_dim(weights_all, offset, term_count)
    own_corr = correlations.astype(jnp.float32)
    ratio = jnp.max(jnp.sqrt(jnp.sum(own_corr * own_corr, axis=1)) / own_weights)
    penalty = LAMBDA_FRACTION * lax.pmax(ratio, "runs")
    first = shrink(STEP * own_corr, STEP * penalty * own_weights)
    design = basis(run_inputs, term_codes)
    fitted = jnp.dot(
        design,
        lax.all_gather(first.astype(jnp.bfloat16), "runs", axis=0, tiled=True),
        preferred_element_type=jnp.float32,
    )
    fitted_half = fitted.astype(jnp.bfloat16)
    all_points = lax.all_gather(run_inputs, "runs", axis=0, tiled=True)
    own_codes = lax.dynamic_slice_in_dim(term_codes, offset, term_count, 0)
    owned_design = basis(all_points, own_codes)
    summed = transposed_product(
        owned_design, lax.all_gather(fitted_half, "runs", axis=0, tiled=True)
    )
    gradient = summed / total_runs - own_corr
    coefficients = shrink(first - STEP * gradient, STEP * penalty * own_weights)
    modes = jnp.take(slab_modes, cell_map, axis=0)
    lifted = lax.dot_general(
        coefficients.astype(jnp.bfloat16),
        modes,
        (((1,), (1,)), ((), ())),
        preferred_element_type=jnp.float32,
    ).astype(jnp.bfloat16)
    return (coefficients, lifted)


def on_device(
    run_inputs, term_codes, weight_levels, correlations, slab_modes, cell_map
):
    devices = lax.axis_size("runs")
    run_count = run_inputs.shape[0]
    term_count, modes = correlations.shape
    chips = max(1, devices // CORES)
    whole_tiles = (
        devices >= CORES
        and devices & (devices - 1) == 0
        and modes % (LANES * chips) == 0
        and term_count % LANES == 0
        and DEGREES * run_inputs.shape[1] <= LANES
        and LANES % run_count == 0
        and chips % (LANES // run_count) == 0
        and term_count % run_count == 0
        and run_inputs.shape[1] % (term_count // run_count) == 0
        and slab_modes.shape[0] % LANES == 0
        and cell_map.shape[0] % LANES == 0
    )
    plan = split_by_modes if whole_tiles else split_by_runs
    return plan(
        run_inputs, term_codes, weight_levels, correlations, slab_modes, cell_map
    )


def solution(mesh):
    return jax.shard_map(
        on_device,
        mesh=mesh,
        in_specs=(
            P(("cases", "runs"), None),
            P(),
            P(),
            P(("cases", "runs"), None),
            P("cases", None),
            P(),
        ),
        out_specs=(P(("cases", "runs"), None), P(("cases", "runs"), None)),
        check_vma=False,
    )
```

```python
import functools
import math

import jax
import jax.numpy as jnp
from jax import lax
from jax.experimental import pallas as pl
from jax.experimental.pallas import tpu as pltpu
from jax.sharding import PartitionSpec as P

STEP = 0.5
LAMBDA_FRACTION = 0.05
EPSILON = 1e-06
DEGREES = 5
LANES = 128
CORES = 2
ROOT_TWO = math.sqrt(2.0)
ROOT_SIX = math.sqrt(6.0)
ROOT_TWENTYFOUR = math.sqrt(24.0)
MIB = 1 << 20


def round_up(value, multiple):
    return -(-value // multiple) * multiple


def split_in_two(values):
    high = values.astype(jnp.bfloat16).astype(jnp.float32)
    return [high, values - high]


def rows_of(index, count):
    return pl.ds(pl.multiple_of(index * count, count), count)


def prepare_kernel(me_ref, corr_ref, points_ref, turned_ref, *sent_refs):
    turned = corr_ref[...].astype(jnp.float32).T
    turned_ref[...] = turned.astype(jnp.bfloat16)
    squares = jnp.sum(turned * turned, axis=0, keepdims=True)
    sent_rows, terms = sent_refs[0].shape
    count = turned.shape[0] // len(sent_refs)
    dim, runs = points_ref.shape
    rows = dim * runs // terms
    points = jnp.concatenate(
        [points_ref[start : start + rows, :] for start in range(0, dim, rows)], axis=1
    )
    pieces = split_in_two(points) + split_in_two(squares)
    used = 2 * rows + 2
    if sent_rows - count > used:
        pieces.append(jnp.zeros((sent_rows - count - used, terms), jnp.float32))
    packet = jnp.concatenate(pieces, axis=0).astype(jnp.bfloat16)
    for k, sent_ref in enumerate(sent_refs):
        chip = (me_ref[0] // CORES) ^ k
        sent_ref[0:count, :] = turned_ref[rows_of(chip, count), :]
        sent_ref[count:sent_rows, :] = packet


def split_in_two(values):
    high = values.astype(jnp.bfloat16).astype(jnp.float32)
    return [high, values - high]


def hermite_columns(points):
    squared = points * points
    return jnp.concatenate(
        [
            jnp.ones_like(points),
            points,
            (squared - 1.0) / ROOT_TWO,
            points * (squared - 3.0) / ROOT_SIX,
            (squared * squared - 6.0 * squared + 3.0) / ROOT_TWENTYFOUR,
        ],
        axis=0,
    )


def collect_kernel(chips, *refs):
    packets_ref = refs[-1]
    rows = packets_ref.shape[1]
    for k, block_ref in enumerate(refs[:chips]):
        count = block_ref.shape[0]
        packets_ref[k] = block_ref[count - rows : count, :]


def design_kernel(
    dim, run_count, me_ref, codes_ref, packets_ref, design_ref, exact, table, chosen
):
    chips, _, terms = packets_ref.shape
    half = exact.shape[1]
    rows = dim * run_count // terms

    @pl.when(pl.program_id(0) == 0)
    def _():
        per = LANES // run_count
        for group in range(chips // per):
            owned = []
            for i in range(per):
                packet = packets_ref[group * per + i].astype(jnp.float32)
                owned.append(packet[0:rows, :] + packet[rows : 2 * rows, :])
            points = jnp.concatenate(
                [
                    jnp.concatenate(
                        [inputs[:, start : start + run_count] for inputs in owned],
                        axis=1,
                    )
                    for start in range(0, terms, run_count)
                ],
                axis=0,
            )
            columns = hermite_columns(points)
            columns = jnp.concatenate(
                [
                    columns,
                    jnp.zeros((half - columns.shape[0], LANES), jnp.float32),
                ],
                axis=0,
            ).T
            high = columns.astype(jnp.bfloat16)
            low = (columns - high.astype(jnp.float32)).astype(jnp.bfloat16)
            block = slice(group * LANES, (group + 1) * LANES)
            exact[block, :] = columns
            table[block, 0:half] = high
            table[block, half : 2 * half] = low

    codes = codes_ref[...]
    spots = (codes % DEGREES) * dim + codes // DEGREES
    slots, terms = codes.shape
    row = lax.broadcasted_iota(jnp.int32, (half, terms), 0)
    matmuls = chosen.shape[0]
    for slot in range(matmuls):
        picked = jnp.where(row == spots[slot : slot + 1, :], 1.0, 0.0).astype(
            jnp.bfloat16
        )
        chosen[slot, 0:half, :] = picked
        chosen[slot, half : 2 * half, :] = picked
    for start in range(0, table.shape[0], LANES):
        block = slice(start, start + LANES)
        rows = exact[block, :]
        product = None
        for slot in range(matmuls):
            factor = jnp.dot(
                table[block, :], chosen[slot], preferred_element_type=jnp.float32
            )
            product = factor if product is None else product * factor
        for part in range(0, terms, half):
            lanes = slice(part, part + half)
            factor = product[:, lanes]
            for slot in range(matmuls, slots):
                spot = jnp.broadcast_to(spots[slot : slot + 1, lanes], rows.shape)
                factor = factor * jnp.take_along_axis(rows, spot, axis=1)
            design_ref[block, lanes] = factor.astype(jnp.bfloat16)


def shrink_factor(squares, limits):
    return jnp.maximum(0.0, 1.0 - limits / jnp.sqrt(squares + EPSILON))


def rows_and_weights(row, first, packets_ref, levels_ref):
    squares, levels = [], []
    for k in range(packets_ref.shape[0]):
        packet = packets_ref[k].astype(jnp.float32)
        squares.append(packet[row : row + 1, :] + packet[row + 1 : row + 2, :])
        device = first ^ (CORES * k)
        levels.append(levels_ref[:, rows_of(device, packets_ref.shape[2])])
    weights = jnp.exp2(jnp.concatenate(levels, axis=1).astype(jnp.float32))
    return jnp.concatenate(squares, axis=1), weights


def fit_kernel(row, me_ref, levels_ref, own_ref, other_ref, *refs):
    *refs, fitted_ref, scale_ref, first_ref = refs
    block_refs, design_refs = refs[:-CORES], refs[-CORES:]
    count = fitted_ref.shape[0]
    term_count = own_ref.shape[2]
    me = me_ref[0]
    squares, weights = rows_and_weights(row, me, own_ref, levels_ref)
    others, other_weights = rows_and_weights(row, me ^ 1, other_ref, levels_ref)
    ratio = jnp.maximum(
        jnp.max(jnp.sqrt(squares) / weights, axis=1, keepdims=True),
        jnp.max(jnp.sqrt(others) / other_weights, axis=1, keepdims=True),
    )
    limits = STEP * (LAMBDA_FRACTION * ratio) * weights
    factor = shrink_factor(STEP * STEP * squares, limits)
    scale_ref[0:1, :] = factor[:, 0:term_count]
    scale_ref[1:2, :] = limits[:, 0:term_count]
    for k, block_ref in enumerate(block_refs):
        terms = slice(k * term_count, (k + 1) * term_count)
        first = STEP * block_ref[0:count, :].astype(jnp.float32) * factor[:, terms]
        first_ref[:, terms] = first.astype(jnp.bfloat16)
    runs = design_refs[0].shape[0]
    for i, design_ref in enumerate(design_refs):
        fitted_ref[:, i * runs : (i + 1) * runs] = lax.dot_general(
            first_ref[...],
            design_ref[...],
            (((1,), (1,)), ((), ())),
            preferred_element_type=jnp.float32,
        )


def sum_kernel(total_runs, own_ref, other_ref, *refs):
    design_refs, summed_refs = refs[:CORES], refs[CORES:]
    runs = design_refs[0].shape[0]
    near = own_ref[:, 0:runs] + other_ref[:, runs : 2 * runs]
    far = own_ref[:, runs : 2 * runs] + other_ref[:, 0:runs]
    near, far = near.astype(jnp.bfloat16), far.astype(jnp.bfloat16)
    term_count = summed_refs[0].shape[1]
    for k, summed_ref in enumerate(summed_refs):
        terms = slice(k * term_count, (k + 1) * term_count)
        summed = jnp.dot(
            near, design_refs[0][:, terms], preferred_element_type=jnp.float32
        ) + jnp.dot(far, design_refs[1][:, terms], preferred_element_type=jnp.float32)
        summed_ref[...] = (summed / total_runs).astype(jnp.bfloat16)


def reorder_kernel(map_ref, slab_ref, *refs):
    modes_ref = refs[-1]
    cells, block = slab_ref.shape[0], modes_ref.shape[0]
    row = lax.broadcasted_iota(jnp.int32, (cells, block), 0)
    chosen = jnp.where(row == map_ref[...], 1.0, 0.0).astype(jnp.bfloat16)
    modes_ref[...] = lax.dot_general(
        chosen,
        slab_ref[...],
        (((0,), (0,)), ((), ())),
        preferred_element_type=jnp.float32,
    ).astype(jnp.bfloat16)


def finish_kernel(pieces, me_ref, corr_ref, scale_ref, *refs):
    modes_refs, refs = refs[:pieces], refs[pieces:]
    *summed_refs, out_ref, lifted_ref, moved, values, half, lifted, out_sem, sems = refs
    modes, terms = corr_ref.shape
    count = summed_refs[0].shape[0]
    squares = jnp.zeros((1, terms), jnp.float32)
    for k, summed_ref in enumerate(summed_refs):
        rows = rows_of((me_ref[0] // CORES) ^ k, count)
        corr = corr_ref[rows, :].astype(jnp.float32)
        first = STEP * corr * scale_ref[0:1, :]
        gradient = summed_ref[...].astype(jnp.float32) - corr
        step = first - STEP * gradient
        moved[rows, :] = step
        squares = squares + jnp.sum(step * step, axis=0, keepdims=True)
    factor = shrink_factor(squares, scale_ref[1:2, :])
    for start in range(0, modes, LANES):
        block = slice(start, start + LANES)
        turned = (moved[block, :] * factor).T
        values[:, block] = turned
        half[:, block] = turned.astype(jnp.bfloat16)
    copies = [pltpu.make_async_copy(values, out_ref, out_sem)]
    copies[0].start()
    width = lifted.shape[2]
    for i, modes_ref in enumerate(modes_refs):
        block = slice(i * width, (i + 1) * width)
        lifted[i] = lax.dot_general(
            half[...],
            modes_ref[...],
            (((1,), (1,)), ((), ())),
            preferred_element_type=jnp.float32,
        ).astype(jnp.bfloat16)
        copies.append(
            pltpu.make_async_copy(lifted.at[i], lifted_ref.at[:, block], sems.at[i])
        )
        copies[-1].start()
    for copy in copies:
        copy.wait()


def in_hbm(array):
    return pltpu.with_memory_space_constraint(array, pltpu.HBM)


def params(limit):
    return pltpu.CompilerParams(vmem_limit_bytes=limit * MIB)


def cost(flops, moved):
    return pl.CostEstimate(flops=flops, bytes_accessed=moved, transcendentals=0)


def to_device(array, bits):
    devices = lax.axis_size("runs")
    return lax.ppermute(array, "runs", [(i, i ^ bits) for i in range(devices)])


def to_chips(arrays):
    return [arrays[0]] + [
        to_device(arrays[k], CORES * k) for k in range(1, len(arrays))
    ]


def split_by_modes(
    run_inputs, term_codes, weight_levels, correlations, slab_modes, cell_map
):
    run_count, dim = run_inputs.shape
    term_count, modes = correlations.shape
    terms, slots = term_codes.shape
    cells = slab_modes.shape[0]
    slab_cells = cell_map.shape[0]
    chips = lax.axis_size("runs") // CORES
    total_runs = run_count * CORES * chips
    core_terms = terms // CORES
    own_modes = modes // chips
    rows = dim * run_count // term_count
    packet_rows = round_up(2 * rows + 2, 16)
    me = lax.axis_index("runs").astype(jnp.int32).reshape(1)
    smem = pl.BlockSpec(memory_space=pltpu.SMEM)
    vmem = pl.BlockSpec(memory_space=pltpu.VMEM)
    anywhere = pl.BlockSpec(memory_space=pl.ANY)

    turned, *sent = pl.pallas_call(
        prepare_kernel,
        in_specs=[smem, vmem, vmem],
        out_specs=[vmem] * (1 + chips),
        out_shape=[jax.ShapeDtypeStruct((modes, term_count), jnp.bfloat16)]
        + [jax.ShapeDtypeStruct((own_modes + packet_rows, term_count), jnp.bfloat16)]
        * chips,
        compiler_params=params(16),
        name="prepare",
    )(me, in_hbm(correlations), in_hbm(run_inputs.T))
    blocks = to_chips(sent)

    block = math.gcd(512, slab_cells)

    def reorder(start, *after):
        return pl.pallas_call(
            reorder_kernel,
            in_specs=[vmem, vmem] + [anywhere] * len(after),
            out_specs=vmem,
            out_shape=jax.ShapeDtypeStruct((block, modes), jnp.bfloat16),
            compiler_params=params(16),
            cost_estimate=cost(2 * cells * block * modes, 2 * cells * modes),
            name="reorder",
        )(cell_map[None, start : start + block], slab_modes, *after)

    starts = range(0, slab_cells, block)
    early = len(starts) // 2
    ordered = [reorder(start, *blocks[1:3]) for start in starts[:early]]
    packets = pl.pallas_call(
        functools.partial(collect_kernel, chips),
        in_specs=[vmem] * chips + [anywhere] * early,
        out_specs=vmem,
        out_shape=jax.ShapeDtypeStruct((chips, packet_rows, term_count), jnp.bfloat16),
        compiler_params=params(8),
        name="collect",
    )(*blocks, *ordered)
    others = to_device(packets, 1)

    tile = term_count
    half = round_up(DEGREES * dim, LANES)
    core_runs = run_count * chips

    def design_of(packets):
        return pl.pallas_call(
            functools.partial(design_kernel, dim, run_count),
            grid_spec=pltpu.PrefetchScalarGridSpec(
                num_scalar_prefetch=1,
                grid=(chips,),
                in_specs=[
                    pl.BlockSpec((slots, tile), lambda i, me: (0, me[0] ^ (CORES * i))),
                    pl.BlockSpec(packets.shape, lambda i, me: (0, 0, 0)),
                ],
                out_specs=pl.BlockSpec((core_runs, tile), lambda i, me: (0, i)),
                scratch_shapes=[
                    pltpu.VMEM((core_runs, half), jnp.float32),
                    pltpu.VMEM((core_runs, 2 * half), jnp.bfloat16),
                    pltpu.VMEM((slots - slots // 4, 2 * half, tile), jnp.bfloat16),
                ],
            ),
            out_shape=jax.ShapeDtypeStruct((core_runs, core_terms), jnp.bfloat16),
            compiler_params=params(16),
            cost_estimate=cost(
                4 * core_runs * core_terms * slots * half, 2 * core_runs * core_terms
            ),
            name="design",
        )(me, in_hbm(term_codes.T), packets)

    designs = [design_of(packets), design_of(others)]

    fit_cost = cost(
        2 * total_runs * core_terms * own_modes, 2 * total_runs * core_terms
    )
    fitted, scale = pl.pallas_call(
        functools.partial(fit_kernel, 2 * rows),
        in_specs=[smem] + [vmem] * (3 + chips + CORES),
        out_specs=[vmem, vmem],
        out_shape=[
            jax.ShapeDtypeStruct((own_modes, total_runs), jnp.float32),
            jax.ShapeDtypeStruct((8, term_count), jnp.float32),
        ],
        scratch_shapes=[pltpu.VMEM((own_modes, core_terms), jnp.bfloat16)],
        compiler_params=params(16),
        cost_estimate=fit_cost,
        name="fit",
    )(me, weight_levels[None, :], packets, others, *blocks, *designs)
    summed = pl.pallas_call(
        functools.partial(sum_kernel, float(total_runs)),
        in_specs=[vmem] * (2 + CORES),
        out_specs=[vmem] * chips,
        out_shape=[jax.ShapeDtypeStruct((own_modes, term_count), jnp.bfloat16)] * chips,
        compiler_params=params(16),
        cost_estimate=fit_cost,
        name="sum",
    )(fitted, to_device(fitted, 1), *designs)
    returned = to_chips(summed)
    ordered += [reorder(start, *returned[1:3]) for start in starts[early:]]

    return pl.pallas_call(
        functools.partial(finish_kernel, len(ordered)),
        in_specs=[smem] + [vmem] * (2 + len(ordered) + chips),
        out_specs=(anywhere, anywhere),
        out_shape=(
            jax.ShapeDtypeStruct((term_count, modes), jnp.float32),
            jax.ShapeDtypeStruct((term_count, slab_cells), jnp.bfloat16),
        ),
        scratch_shapes=[
            pltpu.VMEM((modes, term_count), jnp.float32),
            pltpu.VMEM((term_count, modes), jnp.float32),
            pltpu.VMEM((term_count, modes), jnp.bfloat16),
            pltpu.VMEM((len(ordered), term_count, block), jnp.bfloat16),
            pltpu.SemaphoreType.DMA,
            pltpu.SemaphoreType.DMA((len(ordered),)),
        ],
        compiler_params=params(20),
        name="finish",
    )(me, turned, scale, *ordered, *returned)


def hermite_table(points):
    squared = points * points
    columns = [
        jnp.ones_like(points),
        points,
        (squared - 1.0) / ROOT_TWO,
        points * (squared - 3.0) / ROOT_SIX,
        (squared * squared - 6.0 * squared + 3.0) / ROOT_TWENTYFOUR,
    ]
    return jnp.stack(columns, axis=-1).reshape(points.shape[0], -1)


def basis(points, codes):
    hermite = hermite_table(points)
    product = jnp.take(hermite, codes[:, 0], axis=1)
    for column in range(1, codes.shape[1]):
        product = product * jnp.take(hermite, codes[:, column], axis=1)
    return product.astype(jnp.bfloat16)


def shrink(values, limits):
    length = jnp.sqrt(jnp.sum(values * values, axis=1, keepdims=True) + EPSILON)
    return values * jnp.maximum(0.0, 1.0 - limits[:, None] / length)


def transposed_product(left, right):
    return lax.dot_general(
        left, right, (((0,), (0,)), ((), ())), preferred_element_type=jnp.float32
    )


def split_by_runs(
    run_inputs, term_codes, weight_levels, correlations, slab_modes, cell_map
):
    run_count = run_inputs.shape[0]
    term_count = correlations.shape[0]
    devices = lax.axis_size("runs")
    offset = lax.axis_index("runs") * term_count
    total_runs = run_count * devices
    weights_all = jnp.exp2(weight_levels.astype(jnp.float32))
    own_weights = lax.dynamic_slice_in_dim(weights_all, offset, term_count)
    own_corr = correlations.astype(jnp.float32)
    ratio = jnp.max(jnp.sqrt(jnp.sum(own_corr * own_corr, axis=1)) / own_weights)
    penalty = LAMBDA_FRACTION * lax.pmax(ratio, "runs")
    first = shrink(STEP * own_corr, STEP * penalty * own_weights)
    design = basis(run_inputs, term_codes)
    fitted = jnp.dot(
        design,
        lax.all_gather(first.astype(jnp.bfloat16), "runs", axis=0, tiled=True),
        preferred_element_type=jnp.float32,
    )
    fitted_half = fitted.astype(jnp.bfloat16)
    all_points = lax.all_gather(run_inputs, "runs", axis=0, tiled=True)
    own_codes = lax.dynamic_slice_in_dim(term_codes, offset, term_count, 0)
    owned_design = basis(all_points, own_codes)
    summed = transposed_product(
        owned_design, lax.all_gather(fitted_half, "runs", axis=0, tiled=True)
    )
    gradient = summed / total_runs - own_corr
    coefficients = shrink(first - STEP * gradient, STEP * penalty * own_weights)
    modes = jnp.take(slab_modes, cell_map, axis=0)
    lifted = lax.dot_general(
        coefficients.astype(jnp.bfloat16),
        modes,
        (((1,), (1,)), ((), ())),
        preferred_element_type=jnp.float32,
    ).astype(jnp.bfloat16)
    return (coefficients, lifted)


def on_device(
    run_inputs, term_codes, weight_levels, correlations, slab_modes, cell_map
):
    devices = lax.axis_size("runs")
    run_count = run_inputs.shape[0]
    term_count, modes = correlations.shape
    chips = max(1, devices // CORES)
    whole_tiles = (
        devices >= CORES
        and devices & (devices - 1) == 0
        and modes % (LANES * chips) == 0
        and term_count % LANES == 0
        and DEGREES * run_inputs.shape[1] <= LANES
        and LANES % run_count == 0
        and chips % (LANES // run_count) == 0
        and term_count % run_count == 0
        and run_inputs.shape[1] % (term_count // run_count) == 0
        and slab_modes.shape[0] % LANES == 0
        and cell_map.shape[0] % LANES == 0
    )
    plan = split_by_modes if whole_tiles else split_by_runs
    return plan(
        run_inputs, term_codes, weight_levels, correlations, slab_modes, cell_map
    )


def solution(mesh):
    return jax.shard_map(
        on_device,
        mesh=mesh,
        in_specs=(
            P(("cases", "runs"), None),
            P(),
            P(),
            P(("cases", "runs"), None),
            P("cases", None),
            P(),
        ),
        out_specs=(P(("cases", "runs"), None), P(("cases", "runs"), None)),
        check_vma=False,
    )
```

```python
import functools
import math

import jax
import jax.numpy as jnp
from jax import lax
from jax.experimental import pallas as pl
from jax.experimental.pallas import tpu as pltpu
from jax.sharding import PartitionSpec as P

STEP = 0.5
LAMBDA_FRACTION = 0.05
EPSILON = 1e-06
DEGREES = 5
LANES = 128
CORES = 2
ROOT_TWO = math.sqrt(2.0)
ROOT_SIX = math.sqrt(6.0)
ROOT_TWENTYFOUR = math.sqrt(24.0)
MIB = 1 << 20


def round_up(value, multiple):
    return -(-value // multiple) * multiple


def split_in_two(values):
    high = values.astype(jnp.bfloat16).astype(jnp.float32)
    return [high, values - high]


def partner(slot, chips):
    return slot and (slot + chips // 2 - 2) % (chips - 1) + 1


def rows_of(index, count):
    return pl.ds(pl.multiple_of(index * count, count), count)


def prepare_kernel(me_ref, corr_ref, points_ref, turned_ref, *sent_refs):
    turned = corr_ref[...].astype(jnp.float32).T
    turned_ref[...] = turned.astype(jnp.bfloat16)
    squares = jnp.sum(turned * turned, axis=0, keepdims=True)
    sent_rows, terms = sent_refs[0].shape
    count = turned.shape[0] // len(sent_refs)
    dim, runs = points_ref.shape
    rows = dim * runs // terms
    points = jnp.concatenate(
        [points_ref[start : start + rows, :] for start in range(0, dim, rows)], axis=1
    )
    pieces = split_in_two(points) + split_in_two(squares)
    used = 2 * rows + 2
    if sent_rows - count > used:
        pieces.append(jnp.zeros((sent_rows - count - used, terms), jnp.float32))
    packet = jnp.concatenate(pieces, axis=0).astype(jnp.bfloat16)
    for k, sent_ref in enumerate(sent_refs):
        chip = (me_ref[0] // CORES) ^ partner(k, len(sent_refs))
        sent_ref[0:count, :] = turned_ref[rows_of(chip, count), :]
        sent_ref[count:sent_rows, :] = packet


def split_in_two(values):
    high = values.astype(jnp.bfloat16).astype(jnp.float32)
    return [high, values - high]


def hermite_columns(points):
    squared = points * points
    return jnp.concatenate(
        [
            jnp.ones_like(points),
            points,
            (squared - 1.0) / ROOT_TWO,
            points * (squared - 3.0) / ROOT_SIX,
            (squared * squared - 6.0 * squared + 3.0) / ROOT_TWENTYFOUR,
        ],
        axis=0,
    )


def collect_kernel(chips, *refs):
    packets_ref = refs[-1]
    rows = packets_ref.shape[1]
    for k, block_ref in enumerate(refs[:chips]):
        count = block_ref.shape[0]
        packets_ref[k] = block_ref[count - rows : count, :]


def choose_kernel(dim, chips, me_ref, codes_ref, *refs):
    chosen_ref, spots_ref = refs[-2:]
    matmuls, rows, terms = chosen_ref.shape
    half, tile = rows // 2, terms // chips
    row = lax.broadcasted_iota(jnp.int32, (half, tile), 0)
    for k in range(chips):
        device = me_ref[0] ^ (CORES * partner(k, chips))
        lanes = slice(k * tile, (k + 1) * tile)
        codes = codes_ref[:, rows_of(device, tile)]
        spots = (codes % DEGREES) * dim + codes // DEGREES
        spots_ref[:, lanes] = spots[matmuls:, :]
        for slot in range(matmuls):
            picked = jnp.where(row == spots[slot : slot + 1, :], 1.0, 0.0).astype(
                jnp.bfloat16
            )
            chosen_ref[slot, 0:half, lanes] = picked
            chosen_ref[slot, half:rows, lanes] = picked


def design_kernel(
    dim, run_count, packets_ref, chosen_ref, spots_ref, design_ref, exact, table
):
    chips, _, tile = packets_ref.shape
    half = exact.shape[1]
    rows = dim * run_count // tile
    terms = tile
    per = LANES // run_count
    for group in range(chips // per):
        owned = []
        for i in range(per):
            packet = packets_ref[group * per + i].astype(jnp.float32)
            owned.append(packet[0:rows, :] + packet[rows : 2 * rows, :])
        points = jnp.concatenate(
            [
                jnp.concatenate(
                    [inputs[:, start : start + run_count] for inputs in owned],
                    axis=1,
                )
                for start in range(0, terms, run_count)
            ],
            axis=0,
        )
        columns = hermite_columns(points)
        columns = jnp.concatenate(
            [
                columns,
                jnp.zeros((half - columns.shape[0], LANES), jnp.float32),
            ],
            axis=0,
        ).T
        high = columns.astype(jnp.bfloat16)
        low = (columns - high.astype(jnp.float32)).astype(jnp.bfloat16)
        block = slice(group * LANES, (group + 1) * LANES)
        exact[block, :] = columns
        table[block, 0:half] = high
        table[block, half : 2 * half] = low

    for start in range(0, table.shape[0], LANES):
        block = slice(start, start + LANES)
        values = exact[block, :]
        for first in range(0, design_ref.shape[1], tile):
            lanes = slice(first, first + tile)
            product = None
            for slot in range(chosen_ref.shape[0]):
                factor = jnp.dot(
                    table[block, :],
                    chosen_ref[slot, :, lanes],
                    preferred_element_type=jnp.float32,
                )
                product = factor if product is None else product * factor
            for part in range(0, tile, half):
                factor = product[:, part : part + half]
                lanes = slice(first + part, first + part + half)
                for slot in range(spots_ref.shape[0]):
                    spot = jnp.broadcast_to(
                        spots_ref[slot : slot + 1, lanes], values.shape
                    )
                    factor = factor * jnp.take_along_axis(values, spot, axis=1)
                design_ref[block, lanes] = factor.astype(jnp.bfloat16)


def shrink_factor(squares, limits):
    return jnp.maximum(0.0, 1.0 - limits / jnp.sqrt(squares + EPSILON))


def rows_and_weights(row, first, packets_ref, levels_ref):
    squares, levels = [], []
    for k in range(packets_ref.shape[0]):
        packet = packets_ref[k].astype(jnp.float32)
        squares.append(packet[row : row + 1, :] + packet[row + 1 : row + 2, :])
        device = first ^ (CORES * partner(k, packets_ref.shape[0]))
        levels.append(levels_ref[:, rows_of(device, packets_ref.shape[2])])
    weights = jnp.exp2(jnp.concatenate(levels, axis=1).astype(jnp.float32))
    return jnp.concatenate(squares, axis=1), weights


def fit_kernel(row, me_ref, levels_ref, own_ref, other_ref, *refs):
    *refs, fitted_ref, scale_ref, first_ref = refs
    block_refs, design_refs = refs[:-CORES], refs[-CORES:]
    count = fitted_ref.shape[0]
    term_count = own_ref.shape[2]
    me = me_ref[0]
    squares, weights = rows_and_weights(row, me, own_ref, levels_ref)
    others, other_weights = rows_and_weights(row, me ^ 1, other_ref, levels_ref)
    ratio = jnp.maximum(
        jnp.max(jnp.sqrt(squares) / weights, axis=1, keepdims=True),
        jnp.max(jnp.sqrt(others) / other_weights, axis=1, keepdims=True),
    )
    limits = STEP * (LAMBDA_FRACTION * ratio) * weights
    factor = shrink_factor(STEP * STEP * squares, limits)
    scale_ref[0:1, :] = factor[:, 0:term_count]
    scale_ref[1:2, :] = limits[:, 0:term_count]
    for k, block_ref in enumerate(block_refs):
        terms = slice(k * term_count, (k + 1) * term_count)
        first = STEP * block_ref[0:count, :].astype(jnp.float32) * factor[:, terms]
        first_ref[:, terms] = first.astype(jnp.bfloat16)
    runs = design_refs[0].shape[0]
    for i, design_ref in enumerate(design_refs):
        fitted_ref[:, i * runs : (i + 1) * runs] = lax.dot_general(
            first_ref[...],
            design_ref[...],
            (((1,), (1,)), ((), ())),
            preferred_element_type=jnp.float32,
        )


def sum_kernel(total_runs, own_ref, other_ref, *refs):
    design_refs, summed_refs = refs[:CORES], refs[CORES:]
    runs = design_refs[0].shape[0]
    near = own_ref[:, 0:runs] + other_ref[:, runs : 2 * runs]
    far = own_ref[:, runs : 2 * runs] + other_ref[:, 0:runs]
    near, far = near.astype(jnp.bfloat16), far.astype(jnp.bfloat16)
    term_count = summed_refs[0].shape[1]
    for k, summed_ref in enumerate(summed_refs):
        terms = slice(k * term_count, (k + 1) * term_count)
        summed = jnp.dot(
            near, design_refs[0][:, terms], preferred_element_type=jnp.float32
        ) + jnp.dot(far, design_refs[1][:, terms], preferred_element_type=jnp.float32)
        summed_ref[...] = (summed / total_runs).astype(jnp.bfloat16)


def reorder_kernel(map_ref, slab_ref, *refs):
    modes_ref = refs[-1]
    cells, block = slab_ref.shape[0], modes_ref.shape[0]
    row = lax.broadcasted_iota(jnp.int32, (cells, block), 0)
    chosen = jnp.where(row == map_ref[...], 1.0, 0.0).astype(jnp.bfloat16)
    modes_ref[...] = lax.dot_general(
        chosen,
        slab_ref[...],
        (((0,), (0,)), ((), ())),
        preferred_element_type=jnp.float32,
    ).astype(jnp.bfloat16)


def finish_kernel(pieces, me_ref, corr_ref, scale_ref, *refs):
    modes_refs, refs = refs[:pieces], refs[pieces:]
    *summed_refs, out_ref, lifted_ref, moved, values, half, lifted, out_sem, sems = refs
    modes, terms = corr_ref.shape
    count = summed_refs[0].shape[0]
    squares = jnp.zeros((1, terms), jnp.float32)
    for k, summed_ref in enumerate(summed_refs):
        rows = rows_of((me_ref[0] // CORES) ^ partner(k, len(summed_refs)), count)
        corr = corr_ref[rows, :].astype(jnp.float32)
        first = STEP * corr * scale_ref[0:1, :]
        gradient = summed_ref[...].astype(jnp.float32) - corr
        step = first - STEP * gradient
        moved[rows, :] = step
        squares = squares + jnp.sum(step * step, axis=0, keepdims=True)
    factor = shrink_factor(squares, scale_ref[1:2, :])
    for start in range(0, modes, LANES):
        block = slice(start, start + LANES)
        turned = (moved[block, :] * factor).T
        values[:, block] = turned
        half[:, block] = turned.astype(jnp.bfloat16)
    copies = [pltpu.make_async_copy(values, out_ref, out_sem)]
    copies[0].start()
    width = lifted.shape[2]
    for i, modes_ref in enumerate(modes_refs):
        block = slice(i * width, (i + 1) * width)
        lifted[i] = lax.dot_general(
            half[...],
            modes_ref[...],
            (((1,), (1,)), ((), ())),
            preferred_element_type=jnp.float32,
        ).astype(jnp.bfloat16)
        copies.append(
            pltpu.make_async_copy(lifted.at[i], lifted_ref.at[:, block], sems.at[i])
        )
        copies[-1].start()
    for copy in copies:
        copy.wait()


def in_hbm(array):
    return pltpu.with_memory_space_constraint(array, pltpu.HBM)


def params(limit):
    return pltpu.CompilerParams(vmem_limit_bytes=limit * MIB)


def cost(flops, moved):
    return pl.CostEstimate(flops=flops, bytes_accessed=moved, transcendentals=0)


def to_device(array, bits):
    devices = lax.axis_size("runs")
    return lax.ppermute(array, "runs", [(i, i ^ bits) for i in range(devices)])


def to_chips(arrays):
    chips = len(arrays)
    return [arrays[0]] + [
        to_device(arrays[k], CORES * partner(k, chips)) for k in range(1, chips)
    ]


def split_by_modes(
    run_inputs, term_codes, weight_levels, correlations, slab_modes, cell_map
):
    run_count, dim = run_inputs.shape
    term_count, modes = correlations.shape
    terms, slots = term_codes.shape
    cells = slab_modes.shape[0]
    slab_cells = cell_map.shape[0]
    chips = lax.axis_size("runs") // CORES
    total_runs = run_count * CORES * chips
    core_terms = terms // CORES
    own_modes = modes // chips
    rows = dim * run_count // term_count
    packet_rows = round_up(2 * rows + 2, 16)
    me = lax.axis_index("runs").astype(jnp.int32).reshape(1)
    smem = pl.BlockSpec(memory_space=pltpu.SMEM)
    vmem = pl.BlockSpec(memory_space=pltpu.VMEM)
    anywhere = pl.BlockSpec(memory_space=pl.ANY)

    turned, *sent = pl.pallas_call(
        prepare_kernel,
        in_specs=[smem, vmem, vmem],
        out_specs=[vmem] * (1 + chips),
        out_shape=[jax.ShapeDtypeStruct((modes, term_count), jnp.bfloat16)]
        + [jax.ShapeDtypeStruct((own_modes + packet_rows, term_count), jnp.bfloat16)]
        * chips,
        compiler_params=params(16),
        name="prepare",
    )(me, in_hbm(correlations), in_hbm(run_inputs.T))
    blocks = to_chips(sent)

    block = math.gcd(512, slab_cells)

    def reorder(start, *after):
        return pl.pallas_call(
            reorder_kernel,
            in_specs=[vmem, vmem] + [anywhere] * len(after),
            out_specs=vmem,
            out_shape=jax.ShapeDtypeStruct((block, modes), jnp.bfloat16),
            compiler_params=params(16),
            cost_estimate=cost(2 * cells * block * modes, 2 * cells * modes),
            name="reorder",
        )(cell_map[None, start : start + block], slab_modes, *after)

    starts = range(0, slab_cells, block)
    early = len(starts) // 2
    ordered = [reorder(start, *blocks[1:3]) for start in starts[:early]]
    half = round_up(DEGREES * dim, LANES)
    gathers = slots // 4
    chosen, spots = pl.pallas_call(
        functools.partial(choose_kernel, dim, chips),
        in_specs=[smem, vmem] + [anywhere] * 2,
        out_specs=[vmem, vmem],
        out_shape=[
            jax.ShapeDtypeStruct((slots - gathers, 2 * half, core_terms), jnp.bfloat16),
            jax.ShapeDtypeStruct((gathers, core_terms), jnp.int32),
        ],
        compiler_params=params(8),
        cost_estimate=cost(0, 2 * slots * half * core_terms),
        name="choose",
    )(me, in_hbm(term_codes.T), *blocks[1:3])
    packets = pl.pallas_call(
        functools.partial(collect_kernel, chips),
        in_specs=[vmem] * chips + [anywhere] * (early + 1),
        out_specs=vmem,
        out_shape=jax.ShapeDtypeStruct((chips, packet_rows, term_count), jnp.bfloat16),
        compiler_params=params(8),
        name="collect",
    )(*blocks, *ordered, spots)
    others = to_device(packets, 1)

    core_runs = run_count * chips

    def design_of(packets):
        return pl.pallas_call(
            functools.partial(design_kernel, dim, run_count),
            in_specs=[vmem] * 3,
            out_specs=vmem,
            out_shape=jax.ShapeDtypeStruct((core_runs, core_terms), jnp.bfloat16),
            scratch_shapes=[
                pltpu.VMEM((core_runs, half), jnp.float32),
                pltpu.VMEM((core_runs, 2 * half), jnp.bfloat16),
            ],
            compiler_params=params(16),
            cost_estimate=cost(
                4 * core_runs * core_terms * slots * half, 2 * core_runs * core_terms
            ),
            name="design",
        )(packets, chosen, spots)

    designs = [design_of(packets), design_of(others)]

    fit_cost = cost(
        2 * total_runs * core_terms * own_modes, 2 * total_runs * core_terms
    )
    fitted, scale = pl.pallas_call(
        functools.partial(fit_kernel, 2 * rows),
        in_specs=[smem] + [vmem] * (3 + chips + CORES),
        out_specs=[vmem, vmem],
        out_shape=[
            jax.ShapeDtypeStruct((own_modes, total_runs), jnp.float32),
            jax.ShapeDtypeStruct((8, term_count), jnp.float32),
        ],
        scratch_shapes=[pltpu.VMEM((own_modes, core_terms), jnp.bfloat16)],
        compiler_params=params(16),
        cost_estimate=fit_cost,
        name="fit",
    )(me, weight_levels[None, :], packets, others, *blocks, *designs)
    summed = pl.pallas_call(
        functools.partial(sum_kernel, float(total_runs)),
        in_specs=[vmem] * (2 + CORES),
        out_specs=[vmem] * chips,
        out_shape=[jax.ShapeDtypeStruct((own_modes, term_count), jnp.bfloat16)] * chips,
        compiler_params=params(16),
        cost_estimate=fit_cost,
        name="sum",
    )(fitted, to_device(fitted, 1), *designs)
    returned = to_chips(summed)
    ordered += [reorder(start, *returned[1:3]) for start in starts[early:]]

    return pl.pallas_call(
        functools.partial(finish_kernel, len(ordered)),
        in_specs=[smem] + [vmem] * (2 + len(ordered) + chips),
        out_specs=(anywhere, anywhere),
        out_shape=(
            jax.ShapeDtypeStruct((term_count, modes), jnp.float32),
            jax.ShapeDtypeStruct((term_count, slab_cells), jnp.bfloat16),
        ),
        scratch_shapes=[
            pltpu.VMEM((modes, term_count), jnp.float32),
            pltpu.VMEM((term_count, modes), jnp.float32),
            pltpu.VMEM((term_count, modes), jnp.bfloat16),
            pltpu.VMEM((len(ordered), term_count, block), jnp.bfloat16),
            pltpu.SemaphoreType.DMA,
            pltpu.SemaphoreType.DMA((len(ordered),)),
        ],
        compiler_params=params(20),
        name="finish",
    )(me, turned, scale, *ordered, *returned)


def hermite_table(points):
    squared = points * points
    columns = [
        jnp.ones_like(points),
        points,
        (squared - 1.0) / ROOT_TWO,
        points * (squared - 3.0) / ROOT_SIX,
        (squared * squared - 6.0 * squared + 3.0) / ROOT_TWENTYFOUR,
    ]
    return jnp.stack(columns, axis=-1).reshape(points.shape[0], -1)


def basis(points, codes):
    hermite = hermite_table(points)
    product = jnp.take(hermite, codes[:, 0], axis=1)
    for column in range(1, codes.shape[1]):
        product = product * jnp.take(hermite, codes[:, column], axis=1)
    return product.astype(jnp.bfloat16)


def shrink(values, limits):
    length = jnp.sqrt(jnp.sum(values * values, axis=1, keepdims=True) + EPSILON)
    return values * jnp.maximum(0.0, 1.0 - limits[:, None] / length)


def transposed_product(left, right):
    return lax.dot_general(
        left, right, (((0,), (0,)), ((), ())), preferred_element_type=jnp.float32
    )


def split_by_runs(
    run_inputs, term_codes, weight_levels, correlations, slab_modes, cell_map
):
    run_count = run_inputs.shape[0]
    term_count = correlations.shape[0]
    devices = lax.axis_size("runs")
    offset = lax.axis_index("runs") * term_count
    total_runs = run_count * devices
    weights_all = jnp.exp2(weight_levels.astype(jnp.float32))
    own_weights = lax.dynamic_slice_in_dim(weights_all, offset, term_count)
    own_corr = correlations.astype(jnp.float32)
    ratio = jnp.max(jnp.sqrt(jnp.sum(own_corr * own_corr, axis=1)) / own_weights)
    penalty = LAMBDA_FRACTION * lax.pmax(ratio, "runs")
    first = shrink(STEP * own_corr, STEP * penalty * own_weights)
    design = basis(run_inputs, term_codes)
    fitted = jnp.dot(
        design,
        lax.all_gather(first.astype(jnp.bfloat16), "runs", axis=0, tiled=True),
        preferred_element_type=jnp.float32,
    )
    fitted_half = fitted.astype(jnp.bfloat16)
    all_points = lax.all_gather(run_inputs, "runs", axis=0, tiled=True)
    own_codes = lax.dynamic_slice_in_dim(term_codes, offset, term_count, 0)
    owned_design = basis(all_points, own_codes)
    summed = transposed_product(
        owned_design, lax.all_gather(fitted_half, "runs", axis=0, tiled=True)
    )
    gradient = summed / total_runs - own_corr
    coefficients = shrink(first - STEP * gradient, STEP * penalty * own_weights)
    modes = jnp.take(slab_modes, cell_map, axis=0)
    lifted = lax.dot_general(
        coefficients.astype(jnp.bfloat16),
        modes,
        (((1,), (1,)), ((), ())),
        preferred_element_type=jnp.float32,
    ).astype(jnp.bfloat16)
    return (coefficients, lifted)


def on_device(
    run_inputs, term_codes, weight_levels, correlations, slab_modes, cell_map
):
    devices = lax.axis_size("runs")
    run_count = run_inputs.shape[0]
    term_count, modes = correlations.shape
    chips = max(1, devices // CORES)
    whole_tiles = (
        devices >= CORES
        and devices & (devices - 1) == 0
        and modes % (LANES * chips) == 0
        and term_count % LANES == 0
        and DEGREES * run_inputs.shape[1] <= LANES
        and LANES % run_count == 0
        and chips % (LANES // run_count) == 0
        and term_count % run_count == 0
        and run_inputs.shape[1] % (term_count // run_count) == 0
        and slab_modes.shape[0] % LANES == 0
        and cell_map.shape[0] % LANES == 0
    )
    plan = split_by_modes if whole_tiles else split_by_runs
    return plan(
        run_inputs, term_codes, weight_levels, correlations, slab_modes, cell_map
    )


def solution(mesh):
    return jax.shard_map(
        on_device,
        mesh=mesh,
        in_specs=(
            P(("cases", "runs"), None),
            P(),
            P(),
            P(("cases", "runs"), None),
            P("cases", None),
            P(),
        ),
        out_specs=(P(("cases", "runs"), None), P(("cases", "runs"), None)),
        check_vma=False,
    )
```

```python
import functools
import math

import jax
import jax.numpy as jnp
from jax import lax
from jax.experimental import pallas as pl
from jax.experimental.pallas import tpu as pltpu
from jax.sharding import PartitionSpec as P

STEP = 0.5
LAMBDA_FRACTION = 0.05
EPSILON = 1e-06
DEGREES = 5
LANES = 128
CORES = 2
ROOT_TWO = math.sqrt(2.0)
ROOT_SIX = math.sqrt(6.0)
ROOT_TWENTYFOUR = math.sqrt(24.0)
MIB = 1 << 20


def round_up(value, multiple):
    return -(-value // multiple) * multiple


def split_in_two(values):
    high = values.astype(jnp.bfloat16).astype(jnp.float32)
    return [high, values - high]


def partner(slot, chips):
    return slot and (slot + chips // 2 - 2) % (chips - 1) + 1


def rows_of(index, count):
    return pl.ds(pl.multiple_of(index * count, count), count)


def prepare_kernel(me_ref, corr_ref, points_ref, turned_ref, *sent_refs):
    turned = corr_ref[...].astype(jnp.float32).T
    turned_ref[...] = turned.astype(jnp.bfloat16)
    squares = jnp.sum(turned * turned, axis=0, keepdims=True)
    sent_rows, terms = sent_refs[0].shape
    count = turned.shape[0] // len(sent_refs)
    dim, runs = points_ref.shape
    rows = dim * runs // terms
    points = jnp.concatenate(
        [points_ref[start : start + rows, :] for start in range(0, dim, rows)], axis=1
    )
    pieces = split_in_two(points) + split_in_two(squares)
    used = 2 * rows + 2
    if sent_rows - count > used:
        pieces.append(jnp.zeros((sent_rows - count - used, terms), jnp.float32))
    packet = jnp.concatenate(pieces, axis=0).astype(jnp.bfloat16)
    for k, sent_ref in enumerate(sent_refs):
        chip = (me_ref[0] // CORES) ^ partner(k, len(sent_refs))
        sent_ref[0:count, :] = turned_ref[rows_of(chip, count), :]
        sent_ref[count:sent_rows, :] = packet


def split_in_two(values):
    high = values.astype(jnp.bfloat16).astype(jnp.float32)
    return [high, values - high]


def hermite_columns(points):
    squared = points * points
    return jnp.concatenate(
        [
            jnp.ones_like(points),
            points,
            (squared - 1.0) / ROOT_TWO,
            points * (squared - 3.0) / ROOT_SIX,
            (squared * squared - 6.0 * squared + 3.0) / ROOT_TWENTYFOUR,
        ],
        axis=0,
    )


def collect_kernel(chips, *refs):
    packets_ref = refs[-1]
    rows = packets_ref.shape[1]
    for k, block_ref in enumerate(refs[:chips]):
        count = block_ref.shape[0]
        packets_ref[k] = block_ref[count - rows : count, :]


def choose_kernel(dim, chips, me_ref, codes_ref, *refs):
    chosen_ref, spots_ref = refs[-2:]
    matmuls, rows, terms = chosen_ref.shape
    half, tile = rows // 2, terms // chips
    row = lax.broadcasted_iota(jnp.int32, (half, tile), 0)
    for k in range(chips):
        device = me_ref[0] ^ (CORES * partner(k, chips))
        lanes = slice(k * tile, (k + 1) * tile)
        codes = codes_ref[:, rows_of(device, tile)]
        spots = (codes % DEGREES) * dim + codes // DEGREES
        spots_ref[:, lanes] = spots[matmuls:, :]
        for slot in range(matmuls):
            picked = jnp.where(row == spots[slot : slot + 1, :], 1.0, 0.0).astype(
                jnp.bfloat16
            )
            chosen_ref[slot, 0:half, lanes] = picked
            chosen_ref[slot, half:rows, lanes] = picked


def design_kernel(
    dim, run_count, packets_ref, chosen_ref, spots_ref, design_ref, exact, table
):
    chips, _, tile = packets_ref.shape
    half = exact.shape[1]
    rows = dim * run_count // tile
    terms = tile
    per = LANES // run_count
    for group in range(chips // per):
        owned = []
        for i in range(per):
            packet = packets_ref[group * per + i].astype(jnp.float32)
            owned.append(packet[0:rows, :] + packet[rows : 2 * rows, :])
        points = jnp.concatenate(
            [
                jnp.concatenate(
                    [inputs[:, start : start + run_count] for inputs in owned],
                    axis=1,
                )
                for start in range(0, terms, run_count)
            ],
            axis=0,
        )
        columns = hermite_columns(points)
        columns = jnp.concatenate(
            [
                columns,
                jnp.zeros((half - columns.shape[0], LANES), jnp.float32),
            ],
            axis=0,
        ).T
        high = columns.astype(jnp.bfloat16)
        low = (columns - high.astype(jnp.float32)).astype(jnp.bfloat16)
        block = slice(group * LANES, (group + 1) * LANES)
        exact[block, :] = columns
        table[block, 0:half] = high
        table[block, half : 2 * half] = low

    for start in range(0, table.shape[0], LANES):
        block = slice(start, start + LANES)
        values = exact[block, :]
        for first in range(0, design_ref.shape[1], tile):
            lanes = slice(first, first + tile)
            product = None
            for slot in range(chosen_ref.shape[0]):
                factor = jnp.dot(
                    table[block, :],
                    chosen_ref[slot, :, lanes],
                    preferred_element_type=jnp.float32,
                )
                product = factor if product is None else product * factor
            for part in range(0, tile, half):
                factor = product[:, part : part + half]
                lanes = slice(first + part, first + part + half)
                for slot in range(spots_ref.shape[0]):
                    spot = jnp.broadcast_to(
                        spots_ref[slot : slot + 1, lanes], values.shape
                    )
                    factor = factor * jnp.take_along_axis(values, spot, axis=1)
                design_ref[block, lanes] = factor.astype(jnp.bfloat16)


def shrink_factor(squares, limits):
    return jnp.maximum(0.0, 1.0 - limits / jnp.sqrt(squares + EPSILON))


def rows_and_weights(row, first, packets_ref, levels_ref):
    squares, levels = [], []
    for k in range(packets_ref.shape[0]):
        packet = packets_ref[k].astype(jnp.float32)
        squares.append(packet[row : row + 1, :] + packet[row + 1 : row + 2, :])
        device = first ^ (CORES * partner(k, packets_ref.shape[0]))
        levels.append(levels_ref[:, rows_of(device, packets_ref.shape[2])])
    weights = jnp.exp2(jnp.concatenate(levels, axis=1).astype(jnp.float32))
    return jnp.concatenate(squares, axis=1), weights


def fit_kernel(row, me_ref, levels_ref, own_ref, other_ref, *refs):
    *refs, fitted_ref, scale_ref, first_ref = refs
    block_refs, design_refs = refs[:-CORES], refs[-CORES:]
    count = fitted_ref.shape[0]
    term_count = own_ref.shape[2]
    me = me_ref[0]
    squares, weights = rows_and_weights(row, me, own_ref, levels_ref)
    others, other_weights = rows_and_weights(row, me ^ 1, other_ref, levels_ref)
    ratio = jnp.maximum(
        jnp.max(jnp.sqrt(squares) / weights, axis=1, keepdims=True),
        jnp.max(jnp.sqrt(others) / other_weights, axis=1, keepdims=True),
    )
    limits = STEP * (LAMBDA_FRACTION * ratio) * weights
    factor = shrink_factor(STEP * STEP * squares, limits)
    scale_ref[0:1, :] = factor[:, 0:term_count]
    scale_ref[1:2, :] = limits[:, 0:term_count]
    for k, block_ref in enumerate(block_refs):
        terms = slice(k * term_count, (k + 1) * term_count)
        first = STEP * block_ref[0:count, :].astype(jnp.float32) * factor[:, terms]
        first_ref[:, terms] = first.astype(jnp.bfloat16)
    runs = design_refs[0].shape[0]
    for i, design_ref in enumerate(design_refs):
        fitted_ref[:, i * runs : (i + 1) * runs] = lax.dot_general(
            first_ref[...],
            design_ref[...],
            (((1,), (1,)), ((), ())),
            preferred_element_type=jnp.float32,
        )


def sum_kernel(total_runs, chips, own_ref, other_ref, *refs):
    design_refs = refs[:CORES]
    summed_refs = refs[len(refs) - chips :]
    runs = design_refs[0].shape[0]
    near = own_ref[:, 0:runs] + other_ref[:, runs : 2 * runs]
    far = own_ref[:, runs : 2 * runs] + other_ref[:, 0:runs]
    near, far = near.astype(jnp.bfloat16), far.astype(jnp.bfloat16)
    term_count = summed_refs[0].shape[1]
    for k, summed_ref in enumerate(summed_refs):
        terms = slice(k * term_count, (k + 1) * term_count)
        summed = jnp.dot(
            near, design_refs[0][:, terms], preferred_element_type=jnp.float32
        ) + jnp.dot(far, design_refs[1][:, terms], preferred_element_type=jnp.float32)
        summed_ref[...] = (summed / total_runs).astype(jnp.bfloat16)


def reorder_kernel(map_ref, slab_ref, *refs):
    modes_ref = refs[-1]
    cells, block = slab_ref.shape[0], modes_ref.shape[0]
    row = lax.broadcasted_iota(jnp.int32, (cells, block), 0)
    chosen = jnp.where(row == map_ref[...], 1.0, 0.0).astype(jnp.bfloat16)
    modes_ref[...] = lax.dot_general(
        chosen,
        slab_ref[...],
        (((0,), (0,)), ((), ())),
        preferred_element_type=jnp.float32,
    ).astype(jnp.bfloat16)


def finish_kernel(pieces, me_ref, corr_ref, scale_ref, *refs):
    modes_refs, refs = refs[:pieces], refs[pieces:]
    *summed_refs, out_ref, lifted_ref, moved, values, half, lifted, out_sem, sems = refs
    modes, terms = corr_ref.shape
    count = summed_refs[0].shape[0]
    squares = jnp.zeros((1, terms), jnp.float32)
    for k, summed_ref in enumerate(summed_refs):
        rows = rows_of((me_ref[0] // CORES) ^ partner(k, len(summed_refs)), count)
        corr = corr_ref[rows, :].astype(jnp.float32)
        first = STEP * corr * scale_ref[0:1, :]
        gradient = summed_ref[...].astype(jnp.float32) - corr
        step = first - STEP * gradient
        moved[rows, :] = step
        squares = squares + jnp.sum(step * step, axis=0, keepdims=True)
    factor = shrink_factor(squares, scale_ref[1:2, :])
    for start in range(0, modes, LANES):
        block = slice(start, start + LANES)
        turned = (moved[block, :] * factor).T
        values[:, block] = turned
        half[:, block] = turned.astype(jnp.bfloat16)
    copies = [pltpu.make_async_copy(values, out_ref, out_sem)]
    copies[0].start()
    width = lifted.shape[2]
    for i, modes_ref in enumerate(modes_refs):
        block = slice(i * width, (i + 1) * width)
        lifted[i] = lax.dot_general(
            half[...],
            modes_ref[...],
            (((1,), (1,)), ((), ())),
            preferred_element_type=jnp.float32,
        ).astype(jnp.bfloat16)
        copies.append(
            pltpu.make_async_copy(lifted.at[i], lifted_ref.at[:, block], sems.at[i])
        )
        copies[-1].start()
    for copy in copies:
        copy.wait()


def in_hbm(array):
    return pltpu.with_memory_space_constraint(array, pltpu.HBM)


def params(limit):
    return pltpu.CompilerParams(vmem_limit_bytes=limit * MIB)


def cost(flops, moved):
    return pl.CostEstimate(flops=flops, bytes_accessed=moved, transcendentals=0)


def to_device(array, bits):
    devices = lax.axis_size("runs")
    return lax.ppermute(array, "runs", [(i, i ^ bits) for i in range(devices)])


def to_chips(arrays):
    chips = len(arrays)
    return [arrays[0]] + [
        to_device(arrays[k], CORES * partner(k, chips)) for k in range(1, chips)
    ]


def split_by_modes(
    run_inputs, term_codes, weight_levels, correlations, slab_modes, cell_map
):
    run_count, dim = run_inputs.shape
    term_count, modes = correlations.shape
    terms, slots = term_codes.shape
    cells = slab_modes.shape[0]
    slab_cells = cell_map.shape[0]
    chips = lax.axis_size("runs") // CORES
    total_runs = run_count * CORES * chips
    core_terms = terms // CORES
    own_modes = modes // chips
    rows = dim * run_count // term_count
    packet_rows = round_up(2 * rows + 2, 16)
    me = lax.axis_index("runs").astype(jnp.int32).reshape(1)
    smem = pl.BlockSpec(memory_space=pltpu.SMEM)
    vmem = pl.BlockSpec(memory_space=pltpu.VMEM)
    anywhere = pl.BlockSpec(memory_space=pl.ANY)

    turned, *sent = pl.pallas_call(
        prepare_kernel,
        in_specs=[smem, vmem, vmem],
        out_specs=[vmem] * (1 + chips),
        out_shape=[jax.ShapeDtypeStruct((modes, term_count), jnp.bfloat16)]
        + [jax.ShapeDtypeStruct((own_modes + packet_rows, term_count), jnp.bfloat16)]
        * chips,
        compiler_params=params(16),
        name="prepare",
    )(me, in_hbm(correlations), in_hbm(run_inputs.T))
    blocks = to_chips(sent)

    block = math.gcd(512, slab_cells)

    def reorder(start, *after):
        return pl.pallas_call(
            reorder_kernel,
            in_specs=[vmem, vmem] + [anywhere] * len(after),
            out_specs=vmem,
            out_shape=jax.ShapeDtypeStruct((block, modes), jnp.bfloat16),
            compiler_params=params(16),
            cost_estimate=cost(2 * cells * block * modes, 2 * cells * modes),
            name="reorder",
        )(cell_map[None, start : start + block], slab_modes, *after)

    starts = range(0, slab_cells, block)
    quarters = [starts[i * len(starts) // 4 : (i + 1) * len(starts) // 4] for i in range(4)]
    ordered = [reorder(start) for start in quarters[0]]
    half = round_up(DEGREES * dim, LANES)
    gathers = slots // 4
    chosen, spots = pl.pallas_call(
        functools.partial(choose_kernel, dim, chips),
        in_specs=[smem, vmem] + [anywhere] * 2,
        out_specs=[vmem, vmem],
        out_shape=[
            jax.ShapeDtypeStruct((slots - gathers, 2 * half, core_terms), jnp.bfloat16),
            jax.ShapeDtypeStruct((gathers, core_terms), jnp.int32),
        ],
        compiler_params=params(8),
        cost_estimate=cost(0, 2 * slots * half * core_terms),
        name="choose",
    )(me, in_hbm(term_codes.T), *blocks[1:3])
    packets = pl.pallas_call(
        functools.partial(collect_kernel, chips),
        in_specs=[vmem] * chips + [anywhere] * (1 + len(ordered)),
        out_specs=vmem,
        out_shape=jax.ShapeDtypeStruct((chips, packet_rows, term_count), jnp.bfloat16),
        compiler_params=params(8),
        name="collect",
    )(*blocks, *ordered, spots)
    others = to_device(packets, 1)

    core_runs = run_count * chips

    def design_of(packets):
        return pl.pallas_call(
            functools.partial(design_kernel, dim, run_count),
            in_specs=[vmem] * 3,
            out_specs=vmem,
            out_shape=jax.ShapeDtypeStruct((core_runs, core_terms), jnp.bfloat16),
            scratch_shapes=[
                pltpu.VMEM((core_runs, half), jnp.float32),
                pltpu.VMEM((core_runs, 2 * half), jnp.bfloat16),
            ],
            compiler_params=params(16),
            cost_estimate=cost(
                4 * core_runs * core_terms * slots * half, 2 * core_runs * core_terms
            ),
            name="design",
        )(packets, chosen, spots)

    designs = [design_of(packets), design_of(others)]

    fit_cost = cost(
        2 * total_runs * core_terms * own_modes, 2 * total_runs * core_terms
    )
    fitted, scale = pl.pallas_call(
        functools.partial(fit_kernel, 2 * rows),
        in_specs=[smem] + [vmem] * (3 + chips + CORES),
        out_specs=[vmem, vmem],
        out_shape=[
            jax.ShapeDtypeStruct((own_modes, total_runs), jnp.float32),
            jax.ShapeDtypeStruct((8, term_count), jnp.float32),
        ],
        scratch_shapes=[pltpu.VMEM((own_modes, core_terms), jnp.bfloat16)],
        compiler_params=params(16),
        cost_estimate=fit_cost,
        name="fit",
    )(me, weight_levels[None, :], packets, others, *blocks, *designs)
    beside = [reorder(start, fitted) for start in quarters[1]]
    summed = pl.pallas_call(
        functools.partial(sum_kernel, float(total_runs), chips),
        in_specs=[vmem] * (2 + CORES) + [anywhere] * len(beside),
        out_specs=[vmem] * chips,
        out_shape=[jax.ShapeDtypeStruct((own_modes, term_count), jnp.bfloat16)] * chips,
        compiler_params=params(16),
        cost_estimate=fit_cost,
        name="sum",
    )(fitted, to_device(fitted, 1), *designs, *beside)
    returned = to_chips(summed)
    ordered += beside
    ordered += [reorder(start, summed[0]) for start in quarters[2]]
    ordered += [reorder(start, *returned[1:3]) for start in quarters[3]]

    return pl.pallas_call(
        functools.partial(finish_kernel, len(ordered)),
        in_specs=[smem] + [vmem] * (2 + len(ordered) + chips),
        out_specs=(anywhere, anywhere),
        out_shape=(
            jax.ShapeDtypeStruct((term_count, modes), jnp.float32),
            jax.ShapeDtypeStruct((term_count, slab_cells), jnp.bfloat16),
        ),
        scratch_shapes=[
            pltpu.VMEM((modes, term_count), jnp.float32),
            pltpu.VMEM((term_count, modes), jnp.float32),
            pltpu.VMEM((term_count, modes), jnp.bfloat16),
            pltpu.VMEM((len(ordered), term_count, block), jnp.bfloat16),
            pltpu.SemaphoreType.DMA,
            pltpu.SemaphoreType.DMA((len(ordered),)),
        ],
        compiler_params=params(20),
        name="finish",
    )(me, turned, scale, *ordered, *returned)


def hermite_table(points):
    squared = points * points
    columns = [
        jnp.ones_like(points),
        points,
        (squared - 1.0) / ROOT_TWO,
        points * (squared - 3.0) / ROOT_SIX,
        (squared * squared - 6.0 * squared + 3.0) / ROOT_TWENTYFOUR,
    ]
    return jnp.stack(columns, axis=-1).reshape(points.shape[0], -1)


def basis(points, codes):
    hermite = hermite_table(points)
    product = jnp.take(hermite, codes[:, 0], axis=1)
    for column in range(1, codes.shape[1]):
        product = product * jnp.take(hermite, codes[:, column], axis=1)
    return product.astype(jnp.bfloat16)


def shrink(values, limits):
    length = jnp.sqrt(jnp.sum(values * values, axis=1, keepdims=True) + EPSILON)
    return values * jnp.maximum(0.0, 1.0 - limits[:, None] / length)


def transposed_product(left, right):
    return lax.dot_general(
        left, right, (((0,), (0,)), ((), ())), preferred_element_type=jnp.float32
    )


def split_by_runs(
    run_inputs, term_codes, weight_levels, correlations, slab_modes, cell_map
):
    run_count = run_inputs.shape[0]
    term_count = correlations.shape[0]
    devices = lax.axis_size("runs")
    offset = lax.axis_index("runs") * term_count
    total_runs = run_count * devices
    weights_all = jnp.exp2(weight_levels.astype(jnp.float32))
    own_weights = lax.dynamic_slice_in_dim(weights_all, offset, term_count)
    own_corr = correlations.astype(jnp.float32)
    ratio = jnp.max(jnp.sqrt(jnp.sum(own_corr * own_corr, axis=1)) / own_weights)
    penalty = LAMBDA_FRACTION * lax.pmax(ratio, "runs")
    first = shrink(STEP * own_corr, STEP * penalty * own_weights)
    design = basis(run_inputs, term_codes)
    fitted = jnp.dot(
        design,
        lax.all_gather(first.astype(jnp.bfloat16), "runs", axis=0, tiled=True),
        preferred_element_type=jnp.float32,
    )
    fitted_half = fitted.astype(jnp.bfloat16)
    all_points = lax.all_gather(run_inputs, "runs", axis=0, tiled=True)
    own_codes = lax.dynamic_slice_in_dim(term_codes, offset, term_count, 0)
    owned_design = basis(all_points, own_codes)
    summed = transposed_product(
        owned_design, lax.all_gather(fitted_half, "runs", axis=0, tiled=True)
    )
    gradient = summed / total_runs - own_corr
    coefficients = shrink(first - STEP * gradient, STEP * penalty * own_weights)
    modes = jnp.take(slab_modes, cell_map, axis=0)
    lifted = lax.dot_general(
        coefficients.astype(jnp.bfloat16),
        modes,
        (((1,), (1,)), ((), ())),
        preferred_element_type=jnp.float32,
    ).astype(jnp.bfloat16)
    return (coefficients, lifted)


def on_device(
    run_inputs, term_codes, weight_levels, correlations, slab_modes, cell_map
):
    devices = lax.axis_size("runs")
    run_count = run_inputs.shape[0]
    term_count, modes = correlations.shape
    chips = max(1, devices // CORES)
    whole_tiles = (
        devices >= CORES
        and devices & (devices - 1) == 0
        and modes % (LANES * chips) == 0
        and term_count % LANES == 0
        and DEGREES * run_inputs.shape[1] <= LANES
        and LANES % run_count == 0
        and chips % (LANES // run_count) == 0
        and term_count % run_count == 0
        and run_inputs.shape[1] % (term_count // run_count) == 0
        and slab_modes.shape[0] % LANES == 0
        and cell_map.shape[0] % LANES == 0
    )
    plan = split_by_modes if whole_tiles else split_by_runs
    return plan(
        run_inputs, term_codes, weight_levels, correlations, slab_modes, cell_map
    )


def solution(mesh):
    return jax.shard_map(
        on_device,
        mesh=mesh,
        in_specs=(
            P(("cases", "runs"), None),
            P(),
            P(),
            P(("cases", "runs"), None),
            P("cases", None),
            P(),
        ),
        out_specs=(P(("cases", "runs"), None), P(("cases", "runs"), None)),
        check_vma=False,
    )
```

```python
import functools
import math

import jax
import jax.numpy as jnp
from jax import lax
from jax.experimental import pallas as pl
from jax.experimental.pallas import tpu as pltpu
from jax.sharding import PartitionSpec as P

STEP = 0.5
LAMBDA_FRACTION = 0.05
EPSILON = 1e-06
DEGREES = 5
LANES = 128
CORES = 2
FIRST_SLOTS = 6
ROOT_TWO = math.sqrt(2.0)
ROOT_SIX = math.sqrt(6.0)
ROOT_TWENTYFOUR = math.sqrt(24.0)
MIB = 1 << 20


def round_up(value, multiple):
    return -(-value // multiple) * multiple


def split_in_two(values):
    high = values.astype(jnp.bfloat16).astype(jnp.float32)
    return [high, values - high]


def partner(slot, chips):
    return slot and (slot + chips // 2 - 2) % (chips - 1) + 1


def rows_of(index, count):
    return pl.ds(pl.multiple_of(index * count, count), count)


def prepare_kernel(chips, me_ref, corr_ref, points_ref, turned_ref, packet_ref, *sent_refs):
    turned = corr_ref[...].astype(jnp.float32).T
    turned_ref[...] = turned.astype(jnp.bfloat16)
    squares = jnp.sum(turned * turned, axis=0, keepdims=True)
    packet_rows, terms = packet_ref.shape
    dim, runs = points_ref.shape
    rows = dim * runs // terms
    points = jnp.concatenate(
        [points_ref[start : start + rows, :] for start in range(0, dim, rows)], axis=1
    )
    pieces = split_in_two(points) + split_in_two(squares)
    used = 2 * rows + 2
    if packet_rows > used:
        pieces.append(jnp.zeros((packet_rows - used, terms), jnp.float32))
    packet_ref[...] = jnp.concatenate(pieces, axis=0).astype(jnp.bfloat16)
    fill_blocks(chips, 0, me_ref, turned_ref, packet_ref, sent_refs)


def fill_blocks(chips, first, me_ref, turned_ref, packet_ref, sent_refs):
    count = turned_ref.shape[0] // chips
    for k, sent_ref in enumerate(sent_refs, first):
        chip = (me_ref[0] // CORES) ^ partner(k, chips)
        sent_ref[0:count, :] = turned_ref[rows_of(chip, count), :]
        sent_ref[count : sent_ref.shape[0], :] = packet_ref[...]


def late_kernel(chips, me_ref, turned_ref, packet_ref, *refs):
    sent_refs = refs[len(refs) - (chips - FIRST_SLOTS) :]
    fill_blocks(chips, FIRST_SLOTS, me_ref, turned_ref, packet_ref, sent_refs)


def split_in_two(values):
    high = values.astype(jnp.bfloat16).astype(jnp.float32)
    return [high, values - high]


def hermite_columns(points):
    squared = points * points
    return jnp.concatenate(
        [
            jnp.ones_like(points),
            points,
            (squared - 1.0) / ROOT_TWO,
            points * (squared - 3.0) / ROOT_SIX,
            (squared * squared - 6.0 * squared + 3.0) / ROOT_TWENTYFOUR,
        ],
        axis=0,
    )


def collect_kernel(chips, *refs):
    packets_ref = refs[-1]
    rows = packets_ref.shape[1]
    for k, block_ref in enumerate(refs[:chips]):
        count = block_ref.shape[0]
        packets_ref[k] = block_ref[count - rows : count, :]


def choose_kernel(dim, chips, me_ref, codes_ref, *refs):
    chosen_ref, spots_ref = refs[-2:]
    matmuls, rows, terms = chosen_ref.shape
    half, tile = rows // 2, terms // chips
    row = lax.broadcasted_iota(jnp.int32, (half, tile), 0)
    for k in range(chips):
        device = me_ref[0] ^ (CORES * partner(k, chips))
        lanes = slice(k * tile, (k + 1) * tile)
        codes = codes_ref[:, rows_of(device, tile)]
        spots = (codes % DEGREES) * dim + codes // DEGREES
        spots_ref[:, lanes] = spots[matmuls:, :]
        for slot in range(matmuls):
            picked = jnp.where(row == spots[slot : slot + 1, :], 1.0, 0.0).astype(
                jnp.bfloat16
            )
            chosen_ref[slot, 0:half, lanes] = picked
            chosen_ref[slot, half:rows, lanes] = picked


def design_kernel(
    dim, run_count, packets_ref, chosen_ref, spots_ref, design_ref, exact, table
):
    chips, _, tile = packets_ref.shape
    half = exact.shape[1]
    rows = dim * run_count // tile
    terms = tile
    per = LANES // run_count
    for group in range(chips // per):
        owned = []
        for i in range(per):
            packet = packets_ref[group * per + i].astype(jnp.float32)
            owned.append(packet[0:rows, :] + packet[rows : 2 * rows, :])
        points = jnp.concatenate(
            [
                jnp.concatenate(
                    [inputs[:, start : start + run_count] for inputs in owned],
                    axis=1,
                )
                for start in range(0, terms, run_count)
            ],
            axis=0,
        )
        columns = hermite_columns(points)
        columns = jnp.concatenate(
            [
                columns,
                jnp.zeros((half - columns.shape[0], LANES), jnp.float32),
            ],
            axis=0,
        ).T
        high = columns.astype(jnp.bfloat16)
        low = (columns - high.astype(jnp.float32)).astype(jnp.bfloat16)
        block = slice(group * LANES, (group + 1) * LANES)
        exact[block, :] = columns
        table[block, 0:half] = high
        table[block, half : 2 * half] = low

    for start in range(0, table.shape[0], LANES):
        block = slice(start, start + LANES)
        values = exact[block, :]
        for first in range(0, design_ref.shape[1], tile):
            lanes = slice(first, first + tile)
            product = None
            for slot in range(chosen_ref.shape[0]):
                factor = jnp.dot(
                    table[block, :],
                    chosen_ref[slot, :, lanes],
                    preferred_element_type=jnp.float32,
                )
                product = factor if product is None else product * factor
            for part in range(0, tile, half):
                factor = product[:, part : part + half]
                lanes = slice(first + part, first + part + half)
                for slot in range(spots_ref.shape[0]):
                    spot = jnp.broadcast_to(
                        spots_ref[slot : slot + 1, lanes], values.shape
                    )
                    factor = factor * jnp.take_along_axis(values, spot, axis=1)
                design_ref[block, lanes] = factor.astype(jnp.bfloat16)


def shrink_factor(squares, limits):
    return jnp.maximum(0.0, 1.0 - limits / jnp.sqrt(squares + EPSILON))


def rows_and_weights(row, first, packets_ref, levels_ref):
    squares, levels = [], []
    for k in range(packets_ref.shape[0]):
        packet = packets_ref[k].astype(jnp.float32)
        squares.append(packet[row : row + 1, :] + packet[row + 1 : row + 2, :])
        device = first ^ (CORES * partner(k, packets_ref.shape[0]))
        levels.append(levels_ref[:, rows_of(device, packets_ref.shape[2])])
    weights = jnp.exp2(jnp.concatenate(levels, axis=1).astype(jnp.float32))
    return jnp.concatenate(squares, axis=1), weights


def fit_kernel(row, me_ref, levels_ref, own_ref, other_ref, *refs):
    *refs, fitted_ref, scale_ref, first_ref = refs
    block_refs, design_refs = refs[:-CORES], refs[-CORES:]
    count = fitted_ref.shape[0]
    term_count = own_ref.shape[2]
    me = me_ref[0]
    squares, weights = rows_and_weights(row, me, own_ref, levels_ref)
    others, other_weights = rows_and_weights(row, me ^ 1, other_ref, levels_ref)
    ratio = jnp.maximum(
        jnp.max(jnp.sqrt(squares) / weights, axis=1, keepdims=True),
        jnp.max(jnp.sqrt(others) / other_weights, axis=1, keepdims=True),
    )
    limits = STEP * (LAMBDA_FRACTION * ratio) * weights
    factor = shrink_factor(STEP * STEP * squares, limits)
    scale_ref[0:1, :] = factor[:, 0:term_count]
    scale_ref[1:2, :] = limits[:, 0:term_count]
    for k, block_ref in enumerate(block_refs):
        terms = slice(k * term_count, (k + 1) * term_count)
        first = STEP * block_ref[0:count, :].astype(jnp.float32) * factor[:, terms]
        first_ref[:, terms] = first.astype(jnp.bfloat16)
    runs = design_refs[0].shape[0]
    for i, design_ref in enumerate(design_refs):
        fitted_ref[:, i * runs : (i + 1) * runs] = lax.dot_general(
            first_ref[...],
            design_ref[...],
            (((1,), (1,)), ((), ())),
            preferred_element_type=jnp.float32,
        )


def sum_kernel(total_runs, chips, own_ref, other_ref, *refs):
    design_refs = refs[:CORES]
    summed_refs = refs[len(refs) - chips :]
    runs = design_refs[0].shape[0]
    near = own_ref[:, 0:runs] + other_ref[:, runs : 2 * runs]
    far = own_ref[:, runs : 2 * runs] + other_ref[:, 0:runs]
    near, far = near.astype(jnp.bfloat16), far.astype(jnp.bfloat16)
    term_count = summed_refs[0].shape[1]
    for k, summed_ref in enumerate(summed_refs):
        terms = slice(k * term_count, (k + 1) * term_count)
        summed = jnp.dot(
            near, design_refs[0][:, terms], preferred_element_type=jnp.float32
        ) + jnp.dot(far, design_refs[1][:, terms], preferred_element_type=jnp.float32)
        summed_ref[...] = (summed / total_runs).astype(jnp.bfloat16)


def reorder_kernel(map_ref, slab_ref, *refs):
    modes_ref = refs[-1]
    cells, block = slab_ref.shape[0], modes_ref.shape[0]
    row = lax.broadcasted_iota(jnp.int32, (cells, block), 0)
    chosen = jnp.where(row == map_ref[...], 1.0, 0.0).astype(jnp.bfloat16)
    modes_ref[...] = lax.dot_general(
        chosen,
        slab_ref[...],
        (((0,), (0,)), ((), ())),
        preferred_element_type=jnp.float32,
    ).astype(jnp.bfloat16)


def finish_kernel(pieces, me_ref, corr_ref, scale_ref, *refs):
    modes_refs, refs = refs[:pieces], refs[pieces:]
    *summed_refs, out_ref, lifted_ref, moved, values, half, lifted, out_sem, sems = refs
    modes, terms = corr_ref.shape
    count = summed_refs[0].shape[0]
    squares = jnp.zeros((1, terms), jnp.float32)
    for k, summed_ref in enumerate(summed_refs):
        rows = rows_of((me_ref[0] // CORES) ^ partner(k, len(summed_refs)), count)
        corr = corr_ref[rows, :].astype(jnp.float32)
        first = STEP * corr * scale_ref[0:1, :]
        gradient = summed_ref[...].astype(jnp.float32) - corr
        step = first - STEP * gradient
        moved[rows, :] = step
        squares = squares + jnp.sum(step * step, axis=0, keepdims=True)
    factor = shrink_factor(squares, scale_ref[1:2, :])
    for start in range(0, modes, LANES):
        block = slice(start, start + LANES)
        turned = (moved[block, :] * factor).T
        values[:, block] = turned
        half[:, block] = turned.astype(jnp.bfloat16)
    copies = [pltpu.make_async_copy(values, out_ref, out_sem)]
    copies[0].start()
    width = lifted.shape[2]
    for i, modes_ref in enumerate(modes_refs):
        block = slice(i * width, (i + 1) * width)
        lifted[i] = lax.dot_general(
            half[...],
            modes_ref[...],
            (((1,), (1,)), ((), ())),
            preferred_element_type=jnp.float32,
        ).astype(jnp.bfloat16)
        copies.append(
            pltpu.make_async_copy(lifted.at[i], lifted_ref.at[:, block], sems.at[i])
        )
        copies[-1].start()
    for copy in copies:
        copy.wait()


def in_hbm(array):
    return pltpu.with_memory_space_constraint(array, pltpu.HBM)


def params(limit):
    return pltpu.CompilerParams(vmem_limit_bytes=limit * MIB)


def cost(flops, moved):
    return pl.CostEstimate(flops=flops, bytes_accessed=moved, transcendentals=0)


def to_device(array, bits):
    devices = lax.axis_size("runs")
    return lax.ppermute(array, "runs", [(i, i ^ bits) for i in range(devices)])


def to_chips(arrays):
    chips = len(arrays)
    return [arrays[0]] + [
        to_device(arrays[k], CORES * partner(k, chips)) for k in range(1, chips)
    ]


def split_by_modes(
    run_inputs, term_codes, weight_levels, correlations, slab_modes, cell_map
):
    run_count, dim = run_inputs.shape
    term_count, modes = correlations.shape
    terms, slots = term_codes.shape
    cells = slab_modes.shape[0]
    slab_cells = cell_map.shape[0]
    chips = lax.axis_size("runs") // CORES
    total_runs = run_count * CORES * chips
    core_terms = terms // CORES
    own_modes = modes // chips
    rows = dim * run_count // term_count
    packet_rows = round_up(2 * rows + 2, 16)
    me = lax.axis_index("runs").astype(jnp.int32).reshape(1)
    smem = pl.BlockSpec(memory_space=pltpu.SMEM)
    vmem = pl.BlockSpec(memory_space=pltpu.VMEM)
    anywhere = pl.BlockSpec(memory_space=pl.ANY)

    early = min(chips, FIRST_SLOTS)
    block_type = jax.ShapeDtypeStruct((own_modes + packet_rows, term_count), jnp.bfloat16)
    turned, packet, *sent = pl.pallas_call(
        functools.partial(prepare_kernel, chips),
        in_specs=[smem, vmem, vmem],
        out_specs=[vmem] * (2 + early),
        out_shape=[
            jax.ShapeDtypeStruct((modes, term_count), jnp.bfloat16),
            jax.ShapeDtypeStruct((packet_rows, term_count), jnp.bfloat16),
        ]
        + [block_type] * early,
        compiler_params=params(16),
        name="prepare",
    )(me, in_hbm(correlations), in_hbm(run_inputs.T))

    block = math.gcd(512, slab_cells)

    def reorder(start, *after):
        return pl.pallas_call(
            reorder_kernel,
            in_specs=[vmem, vmem] + [anywhere] * len(after),
            out_specs=vmem,
            out_shape=jax.ShapeDtypeStruct((block, modes), jnp.bfloat16),
            compiler_params=params(16),
            cost_estimate=cost(2 * cells * block * modes, 2 * cells * modes),
            name="reorder",
        )(cell_map[None, start : start + block], slab_modes, *after)

    starts = range(0, slab_cells, block)
    quarters = [starts[i * len(starts) // 4 : (i + 1) * len(starts) // 4] for i in range(4)]
    ordered = [reorder(start) for start in quarters[0]]
    half = round_up(DEGREES * dim, LANES)
    gathers = slots // 4
    chosen, spots = pl.pallas_call(
        functools.partial(choose_kernel, dim, chips),
        in_specs=[smem, vmem],
        out_specs=[vmem, vmem],
        out_shape=[
            jax.ShapeDtypeStruct((slots - gathers, 2 * half, core_terms), jnp.bfloat16),
            jax.ShapeDtypeStruct((gathers, core_terms), jnp.int32),
        ],
        compiler_params=params(8),
        cost_estimate=cost(0, 2 * slots * half * core_terms),
        name="choose",
    )(me, in_hbm(term_codes.T))
    if chips > early:
        sent += pl.pallas_call(
            functools.partial(late_kernel, chips),
            in_specs=[smem, vmem, vmem] + [anywhere] * (1 + len(ordered)),
            out_specs=[vmem] * (chips - early),
            out_shape=[block_type] * (chips - early),
            compiler_params=params(8),
            name="late",
        )(me, turned, packet, spots, *ordered)
    blocks = to_chips(sent)
    packets = pl.pallas_call(
        functools.partial(collect_kernel, chips),
        in_specs=[vmem] * chips,
        out_specs=vmem,
        out_shape=jax.ShapeDtypeStruct((chips, packet_rows, term_count), jnp.bfloat16),
        compiler_params=params(8),
        name="collect",
    )(*blocks)
    others = to_device(packets, 1)

    core_runs = run_count * chips

    def design_of(packets):
        return pl.pallas_call(
            functools.partial(design_kernel, dim, run_count),
            in_specs=[vmem] * 3,
            out_specs=vmem,
            out_shape=jax.ShapeDtypeStruct((core_runs, core_terms), jnp.bfloat16),
            scratch_shapes=[
                pltpu.VMEM((core_runs, half), jnp.float32),
                pltpu.VMEM((core_runs, 2 * half), jnp.bfloat16),
            ],
            compiler_params=params(16),
            cost_estimate=cost(
                4 * core_runs * core_terms * slots * half, 2 * core_runs * core_terms
            ),
            name="design",
        )(packets, chosen, spots)

    designs = [design_of(packets), design_of(others)]

    fit_cost = cost(
        2 * total_runs * core_terms * own_modes, 2 * total_runs * core_terms
    )
    fitted, scale = pl.pallas_call(
        functools.partial(fit_kernel, 2 * rows),
        in_specs=[smem] + [vmem] * (3 + chips + CORES),
        out_specs=[vmem, vmem],
        out_shape=[
            jax.ShapeDtypeStruct((own_modes, total_runs), jnp.float32),
            jax.ShapeDtypeStruct((8, term_count), jnp.float32),
        ],
        scratch_shapes=[pltpu.VMEM((own_modes, core_terms), jnp.bfloat16)],
        compiler_params=params(16),
        cost_estimate=fit_cost,
        name="fit",
    )(me, weight_levels[None, :], packets, others, *blocks, *designs)
    beside = [reorder(start, fitted) for start in quarters[1]]
    summed = pl.pallas_call(
        functools.partial(sum_kernel, float(total_runs), chips),
        in_specs=[vmem] * (2 + CORES) + [anywhere] * len(beside),
        out_specs=[vmem] * chips,
        out_shape=[jax.ShapeDtypeStruct((own_modes, term_count), jnp.bfloat16)] * chips,
        compiler_params=params(16),
        cost_estimate=fit_cost,
        name="sum",
    )(fitted, to_device(fitted, 1), *designs, *beside)
    returned = to_chips(summed)
    ordered += beside
    ordered += [reorder(start, summed[0]) for start in quarters[2]]
    ordered += [reorder(start, *returned[1:3]) for start in quarters[3]]

    return pl.pallas_call(
        functools.partial(finish_kernel, len(ordered)),
        in_specs=[smem] + [vmem] * (2 + len(ordered) + chips),
        out_specs=(anywhere, anywhere),
        out_shape=(
            jax.ShapeDtypeStruct((term_count, modes), jnp.float32),
            jax.ShapeDtypeStruct((term_count, slab_cells), jnp.bfloat16),
        ),
        scratch_shapes=[
            pltpu.VMEM((modes, term_count), jnp.float32),
            pltpu.VMEM((term_count, modes), jnp.float32),
            pltpu.VMEM((term_count, modes), jnp.bfloat16),
            pltpu.VMEM((len(ordered), term_count, block), jnp.bfloat16),
            pltpu.SemaphoreType.DMA,
            pltpu.SemaphoreType.DMA((len(ordered),)),
        ],
        compiler_params=params(20),
        name="finish",
    )(me, turned, scale, *ordered, *returned)


def hermite_table(points):
    squared = points * points
    columns = [
        jnp.ones_like(points),
        points,
        (squared - 1.0) / ROOT_TWO,
        points * (squared - 3.0) / ROOT_SIX,
        (squared * squared - 6.0 * squared + 3.0) / ROOT_TWENTYFOUR,
    ]
    return jnp.stack(columns, axis=-1).reshape(points.shape[0], -1)


def basis(points, codes):
    hermite = hermite_table(points)
    product = jnp.take(hermite, codes[:, 0], axis=1)
    for column in range(1, codes.shape[1]):
        product = product * jnp.take(hermite, codes[:, column], axis=1)
    return product.astype(jnp.bfloat16)


def shrink(values, limits):
    length = jnp.sqrt(jnp.sum(values * values, axis=1, keepdims=True) + EPSILON)
    return values * jnp.maximum(0.0, 1.0 - limits[:, None] / length)


def transposed_product(left, right):
    return lax.dot_general(
        left, right, (((0,), (0,)), ((), ())), preferred_element_type=jnp.float32
    )


def split_by_runs(
    run_inputs, term_codes, weight_levels, correlations, slab_modes, cell_map
):
    run_count = run_inputs.shape[0]
    term_count = correlations.shape[0]
    devices = lax.axis_size("runs")
    offset = lax.axis_index("runs") * term_count
    total_runs = run_count * devices
    weights_all = jnp.exp2(weight_levels.astype(jnp.float32))
    own_weights = lax.dynamic_slice_in_dim(weights_all, offset, term_count)
    own_corr = correlations.astype(jnp.float32)
    ratio = jnp.max(jnp.sqrt(jnp.sum(own_corr * own_corr, axis=1)) / own_weights)
    penalty = LAMBDA_FRACTION * lax.pmax(ratio, "runs")
    first = shrink(STEP * own_corr, STEP * penalty * own_weights)
    design = basis(run_inputs, term_codes)
    fitted = jnp.dot(
        design,
        lax.all_gather(first.astype(jnp.bfloat16), "runs", axis=0, tiled=True),
        preferred_element_type=jnp.float32,
    )
    fitted_half = fitted.astype(jnp.bfloat16)
    all_points = lax.all_gather(run_inputs, "runs", axis=0, tiled=True)
    own_codes = lax.dynamic_slice_in_dim(term_codes, offset, term_count, 0)
    owned_design = basis(all_points, own_codes)
    summed = transposed_product(
        owned_design, lax.all_gather(fitted_half, "runs", axis=0, tiled=True)
    )
    gradient = summed / total_runs - own_corr
    coefficients = shrink(first - STEP * gradient, STEP * penalty * own_weights)
    modes = jnp.take(slab_modes, cell_map, axis=0)
    lifted = lax.dot_general(
        coefficients.astype(jnp.bfloat16),
        modes,
        (((1,), (1,)), ((), ())),
        preferred_element_type=jnp.float32,
    ).astype(jnp.bfloat16)
    return (coefficients, lifted)


def on_device(
    run_inputs, term_codes, weight_levels, correlations, slab_modes, cell_map
):
    devices = lax.axis_size("runs")
    run_count = run_inputs.shape[0]
    term_count, modes = correlations.shape
    chips = max(1, devices // CORES)
    whole_tiles = (
        devices >= CORES
        and devices & (devices - 1) == 0
        and modes % (LANES * chips) == 0
        and term_count % LANES == 0
        and DEGREES * run_inputs.shape[1] <= LANES
        and LANES % run_count == 0
        and chips % (LANES // run_count) == 0
        and term_count % run_count == 0
        and run_inputs.shape[1] % (term_count // run_count) == 0
        and slab_modes.shape[0] % LANES == 0
        and cell_map.shape[0] % LANES == 0
    )
    plan = split_by_modes if whole_tiles else split_by_runs
    return plan(
        run_inputs, term_codes, weight_levels, correlations, slab_modes, cell_map
    )


def solution(mesh):
    return jax.shard_map(
        on_device,
        mesh=mesh,
        in_specs=(
            P(("cases", "runs"), None),
            P(),
            P(),
            P(("cases", "runs"), None),
            P("cases", None),
            P(),
        ),
        out_specs=(P(("cases", "runs"), None), P(("cases", "runs"), None)),
        check_vma=False,
    )
```

```python
import functools
import math

import jax
import jax.numpy as jnp
from jax import lax
from jax.experimental import pallas as pl
from jax.experimental.pallas import tpu as pltpu
from jax.sharding import PartitionSpec as P

STEP = 0.5
LAMBDA_FRACTION = 0.05
EPSILON = 1e-06
DEGREES = 5
LANES = 128
CORES = 2
FIRST_SLOTS = 6
ROOT_TWO = math.sqrt(2.0)
ROOT_SIX = math.sqrt(6.0)
ROOT_TWENTYFOUR = math.sqrt(24.0)
MIB = 1 << 20


def round_up(value, multiple):
    return -(-value // multiple) * multiple


def split_in_two(values):
    high = values.astype(jnp.bfloat16).astype(jnp.float32)
    return [high, values - high]


def partner(slot, chips):
    return slot and (slot + chips // 2 - 2) % (chips - 1) + 1


def rows_of(index, count):
    return pl.ds(pl.multiple_of(index * count, count), count)


def prepare_kernel(chips, me_ref, corr_ref, points_ref, turned_ref, packet_ref, *sent_refs):
    turned = corr_ref[...].astype(jnp.float32).T
    turned_ref[...] = turned.astype(jnp.bfloat16)
    squares = jnp.sum(turned * turned, axis=0, keepdims=True)
    packet_rows, terms = packet_ref.shape
    dim, runs = points_ref.shape
    rows = dim * runs // terms
    points = jnp.concatenate(
        [points_ref[start : start + rows, :] for start in range(0, dim, rows)], axis=1
    )
    pieces = split_in_two(points) + split_in_two(squares)
    used = 2 * rows + 2
    if packet_rows > used:
        pieces.append(jnp.zeros((packet_rows - used, terms), jnp.float32))
    packet_ref[...] = jnp.concatenate(pieces, axis=0).astype(jnp.bfloat16)
    fill_blocks(chips, 0, me_ref, turned_ref, packet_ref, sent_refs)


def fill_blocks(chips, first, me_ref, turned_ref, packet_ref, sent_refs):
    count = turned_ref.shape[0] // chips
    for k, sent_ref in enumerate(sent_refs, first):
        chip = (me_ref[0] // CORES) ^ partner(k, chips)
        sent_ref[0:count, :] = turned_ref[rows_of(chip, count), :]
        sent_ref[count : sent_ref.shape[0], :] = packet_ref[...]


def late_kernel(chips, me_ref, turned_ref, packet_ref, *refs):
    sent_refs = refs[len(refs) - (chips - FIRST_SLOTS) :]
    fill_blocks(chips, FIRST_SLOTS, me_ref, turned_ref, packet_ref, sent_refs)


def split_in_two(values):
    high = values.astype(jnp.bfloat16).astype(jnp.float32)
    return [high, values - high]


def hermite_columns(points):
    squared = points * points
    return jnp.concatenate(
        [
            jnp.ones_like(points),
            points,
            (squared - 1.0) / ROOT_TWO,
            points * (squared - 3.0) / ROOT_SIX,
            (squared * squared - 6.0 * squared + 3.0) / ROOT_TWENTYFOUR,
        ],
        axis=0,
    )


def collect_kernel(chips, *refs):
    packets_ref = refs[-1]
    rows = packets_ref.shape[1]
    for k, block_ref in enumerate(refs[:chips]):
        count = block_ref.shape[0]
        packets_ref[k] = block_ref[count - rows : count, :]


def choose_kernel(dim, chips, me_ref, codes_ref, *refs):
    chosen_ref, spots_ref = refs[-2:]
    matmuls, rows, terms = chosen_ref.shape
    half, tile = rows // 2, terms // chips
    row = lax.broadcasted_iota(jnp.int32, (half, tile), 0)
    for k in range(chips):
        device = me_ref[0] ^ (CORES * partner(k, chips))
        lanes = slice(k * tile, (k + 1) * tile)
        codes = codes_ref[:, rows_of(device, tile)]
        spots = (codes % DEGREES) * dim + codes // DEGREES
        spots_ref[:, lanes] = spots[matmuls:, :]
        for slot in range(matmuls):
            picked = jnp.where(row == spots[slot : slot + 1, :], 1.0, 0.0).astype(
                jnp.bfloat16
            )
            chosen_ref[slot, 0:half, lanes] = picked
            chosen_ref[slot, half:rows, lanes] = picked


def design_kernel(
    dim, run_count, packets_ref, chosen_ref, spots_ref, design_ref, exact, table
):
    chips, _, tile = packets_ref.shape
    half = exact.shape[1]
    rows = dim * run_count // tile
    terms = tile
    per = LANES // run_count
    for group in range(chips // per):
        owned = []
        for i in range(per):
            packet = packets_ref[group * per + i].astype(jnp.float32)
            owned.append(packet[0:rows, :] + packet[rows : 2 * rows, :])
        points = jnp.concatenate(
            [
                jnp.concatenate(
                    [inputs[:, start : start + run_count] for inputs in owned],
                    axis=1,
                )
                for start in range(0, terms, run_count)
            ],
            axis=0,
        )
        columns = hermite_columns(points)
        columns = jnp.concatenate(
            [
                columns,
                jnp.zeros((half - columns.shape[0], LANES), jnp.float32),
            ],
            axis=0,
        ).T
        high = columns.astype(jnp.bfloat16)
        low = (columns - high.astype(jnp.float32)).astype(jnp.bfloat16)
        block = slice(group * LANES, (group + 1) * LANES)
        exact[block, :] = columns
        table[block, 0:half] = high
        table[block, half : 2 * half] = low

    for start in range(0, table.shape[0], LANES):
        block = slice(start, start + LANES)
        values = exact[block, :]
        for first in range(0, design_ref.shape[1], tile):
            lanes = slice(first, first + tile)
            product = None
            for slot in range(chosen_ref.shape[0]):
                factor = jnp.dot(
                    table[block, :],
                    chosen_ref[slot, :, lanes],
                    preferred_element_type=jnp.float32,
                )
                product = factor if product is None else product * factor
            for part in range(0, tile, half):
                factor = product[:, part : part + half]
                lanes = slice(first + part, first + part + half)
                for slot in range(spots_ref.shape[0]):
                    spot = jnp.broadcast_to(
                        spots_ref[slot : slot + 1, lanes], values.shape
                    )
                    factor = factor * jnp.take_along_axis(values, spot, axis=1)
                design_ref[block, lanes] = factor.astype(jnp.bfloat16)


def shrink_factor(squares, limits):
    return jnp.maximum(0.0, 1.0 - limits / jnp.sqrt(squares + EPSILON))


def rows_and_weights(row, first, packets_ref, levels_ref):
    squares, levels = [], []
    for k in range(packets_ref.shape[0]):
        packet = packets_ref[k].astype(jnp.float32)
        squares.append(packet[row : row + 1, :] + packet[row + 1 : row + 2, :])
        device = first ^ (CORES * partner(k, packets_ref.shape[0]))
        levels.append(levels_ref[:, rows_of(device, packets_ref.shape[2])])
    weights = jnp.exp2(jnp.concatenate(levels, axis=1).astype(jnp.float32))
    return jnp.concatenate(squares, axis=1), weights


def fit_kernel(row, me_ref, levels_ref, own_ref, other_ref, *refs):
    *refs, fitted_ref, scale_ref, first_ref = refs
    block_refs, design_refs = refs[:-CORES], refs[-CORES:]
    count = fitted_ref.shape[0]
    term_count = own_ref.shape[2]
    me = me_ref[0]
    squares, weights = rows_and_weights(row, me, own_ref, levels_ref)
    others, other_weights = rows_and_weights(row, me ^ 1, other_ref, levels_ref)
    ratio = jnp.maximum(
        jnp.max(jnp.sqrt(squares) / weights, axis=1, keepdims=True),
        jnp.max(jnp.sqrt(others) / other_weights, axis=1, keepdims=True),
    )
    limits = STEP * (LAMBDA_FRACTION * ratio) * weights
    factor = shrink_factor(STEP * STEP * squares, limits)
    scale_ref[0:1, :] = factor[:, 0:term_count]
    scale_ref[1:2, :] = limits[:, 0:term_count]
    for k, block_ref in enumerate(block_refs):
        terms = slice(k * term_count, (k + 1) * term_count)
        first = STEP * block_ref[0:count, :].astype(jnp.float32) * factor[:, terms]
        first_ref[:, terms] = first.astype(jnp.bfloat16)
    runs = design_refs[0].shape[0]
    for i, design_ref in enumerate(design_refs):
        fitted_ref[:, i * runs : (i + 1) * runs] = lax.dot_general(
            first_ref[...],
            design_ref[...],
            (((1,), (1,)), ((), ())),
            preferred_element_type=jnp.float32,
        )


def sum_kernel(total_runs, chips, own_ref, other_ref, *refs):
    design_refs = refs[:CORES]
    summed_refs = refs[len(refs) - chips :]
    runs = design_refs[0].shape[0]
    near = own_ref[:, 0:runs] + other_ref[:, runs : 2 * runs]
    far = own_ref[:, runs : 2 * runs] + other_ref[:, 0:runs]
    near, far = near.astype(jnp.bfloat16), far.astype(jnp.bfloat16)
    term_count = summed_refs[0].shape[1]
    for k, summed_ref in enumerate(summed_refs):
        terms = slice(k * term_count, (k + 1) * term_count)
        summed = jnp.dot(
            near, design_refs[0][:, terms], preferred_element_type=jnp.float32
        ) + jnp.dot(far, design_refs[1][:, terms], preferred_element_type=jnp.float32)
        summed_ref[...] = (summed / total_runs).astype(jnp.bfloat16)


def reorder_kernel(map_ref, slab_ref, *refs):
    modes_ref = refs[-1]
    cells, block = slab_ref.shape[0], modes_ref.shape[0]
    row = lax.broadcasted_iota(jnp.int32, (cells, block), 0)
    chosen = jnp.where(row == map_ref[...], 1.0, 0.0).astype(jnp.bfloat16)
    modes_ref[...] = lax.dot_general(
        chosen,
        slab_ref[...],
        (((0,), (0,)), ((), ())),
        preferred_element_type=jnp.float32,
    ).astype(jnp.bfloat16)


def finish_kernel(pieces, me_ref, corr_ref, scale_ref, *refs):
    modes_refs, refs = refs[:pieces], refs[pieces:]
    *summed_refs, out_ref, lifted_ref, moved, values, half, lifted, out_sem, sems = refs
    modes, terms = corr_ref.shape
    count = summed_refs[0].shape[0]
    squares = jnp.zeros((1, terms), jnp.float32)
    for k, summed_ref in enumerate(summed_refs):
        rows = rows_of((me_ref[0] // CORES) ^ partner(k, len(summed_refs)), count)
        corr = corr_ref[rows, :].astype(jnp.float32)
        first = STEP * corr * scale_ref[0:1, :]
        gradient = summed_ref[...].astype(jnp.float32) - corr
        step = first - STEP * gradient
        moved[rows, :] = step
        squares = squares + jnp.sum(step * step, axis=0, keepdims=True)
    factor = shrink_factor(squares, scale_ref[1:2, :])
    for start in range(0, modes, LANES):
        block = slice(start, start + LANES)
        turned = (moved[block, :] * factor).T
        values[:, block] = turned
        half[:, block] = turned.astype(jnp.bfloat16)
    copies = [pltpu.make_async_copy(values, out_ref, out_sem)]
    copies[0].start()
    width = lifted.shape[2]
    for i, modes_ref in enumerate(modes_refs):
        block = slice(i * width, (i + 1) * width)
        lifted[i] = lax.dot_general(
            half[...],
            modes_ref[...],
            (((1,), (1,)), ((), ())),
            preferred_element_type=jnp.float32,
        ).astype(jnp.bfloat16)
        copies.append(
            pltpu.make_async_copy(lifted.at[i], lifted_ref.at[:, block], sems.at[i])
        )
        copies[-1].start()
    for copy in copies:
        copy.wait()


def in_hbm(array):
    return pltpu.with_memory_space_constraint(array, pltpu.HBM)


def params(limit):
    return pltpu.CompilerParams(vmem_limit_bytes=limit * MIB)


def cost(flops, moved):
    return pl.CostEstimate(flops=flops, bytes_accessed=moved, transcendentals=0)


def to_device(array, bits):
    devices = lax.axis_size("runs")
    return lax.ppermute(array, "runs", [(i, i ^ bits) for i in range(devices)])


def to_chips(arrays):
    chips = len(arrays)
    return [arrays[0]] + [
        to_device(arrays[k], CORES * partner(k, chips)) for k in range(1, chips)
    ]


def split_by_modes(
    run_inputs, term_codes, weight_levels, correlations, slab_modes, cell_map
):
    run_count, dim = run_inputs.shape
    term_count, modes = correlations.shape
    terms, slots = term_codes.shape
    cells = slab_modes.shape[0]
    slab_cells = cell_map.shape[0]
    chips = lax.axis_size("runs") // CORES
    total_runs = run_count * CORES * chips
    core_terms = terms // CORES
    own_modes = modes // chips
    rows = dim * run_count // term_count
    packet_rows = round_up(2 * rows + 2, 16)
    me = lax.axis_index("runs").astype(jnp.int32).reshape(1)
    smem = pl.BlockSpec(memory_space=pltpu.SMEM)
    vmem = pl.BlockSpec(memory_space=pltpu.VMEM)
    anywhere = pl.BlockSpec(memory_space=pl.ANY)

    early = min(chips, FIRST_SLOTS)
    block_type = jax.ShapeDtypeStruct((own_modes + packet_rows, term_count), jnp.bfloat16)
    turned, packet, *sent = pl.pallas_call(
        functools.partial(prepare_kernel, chips),
        in_specs=[smem, vmem, vmem],
        out_specs=[vmem] * (2 + early),
        out_shape=[
            jax.ShapeDtypeStruct((modes, term_count), jnp.bfloat16),
            jax.ShapeDtypeStruct((packet_rows, term_count), jnp.bfloat16),
        ]
        + [block_type] * early,
        compiler_params=params(16),
        name="prepare",
    )(me, in_hbm(correlations), in_hbm(run_inputs.T))

    block = math.gcd(512, slab_cells)

    def reorder(start, *after):
        return pl.pallas_call(
            reorder_kernel,
            in_specs=[vmem, vmem] + [anywhere] * len(after),
            out_specs=vmem,
            out_shape=jax.ShapeDtypeStruct((block, modes), jnp.bfloat16),
            compiler_params=params(16),
            cost_estimate=cost(2 * cells * block * modes, 2 * cells * modes),
            name="reorder",
        )(cell_map[None, start : start + block], slab_modes, *after)

    starts = range(0, slab_cells, block)
    quarters = [starts[i * len(starts) // 4 : (i + 1) * len(starts) // 4] for i in range(4)]
    ordered = [reorder(start) for start in quarters[0]]
    half = round_up(DEGREES * dim, LANES)
    gathers = slots // 4
    chosen, spots = pl.pallas_call(
        functools.partial(choose_kernel, dim, chips),
        in_specs=[smem, vmem],
        out_specs=[vmem, vmem],
        out_shape=[
            jax.ShapeDtypeStruct((slots - gathers, 2 * half, core_terms), jnp.bfloat16),
            jax.ShapeDtypeStruct((gathers, core_terms), jnp.int32),
        ],
        compiler_params=params(8),
        cost_estimate=cost(0, 2 * slots * half * core_terms),
        name="choose",
    )(me, in_hbm(term_codes.T))
    if chips > early:
        sent += pl.pallas_call(
            functools.partial(late_kernel, chips),
            in_specs=[smem, vmem, vmem] + [anywhere] * (1 + len(ordered)),
            out_specs=[vmem] * (chips - early),
            out_shape=[block_type] * (chips - early),
            compiler_params=params(8),
            name="late",
        )(me, turned, packet, spots, *ordered)
    blocks = to_chips(sent)
    tail = [reorder(start, *blocks[1:3]) for start in quarters[1]]
    packets = pl.pallas_call(
        functools.partial(collect_kernel, chips),
        in_specs=[vmem] * chips + [anywhere] * len(tail),
        out_specs=vmem,
        out_shape=jax.ShapeDtypeStruct((chips, packet_rows, term_count), jnp.bfloat16),
        compiler_params=params(8),
        name="collect",
    )(*blocks, *tail)
    others = to_device(packets, 1)

    core_runs = run_count * chips

    def design_of(packets):
        return pl.pallas_call(
            functools.partial(design_kernel, dim, run_count),
            in_specs=[vmem] * 3,
            out_specs=vmem,
            out_shape=jax.ShapeDtypeStruct((core_runs, core_terms), jnp.bfloat16),
            scratch_shapes=[
                pltpu.VMEM((core_runs, half), jnp.float32),
                pltpu.VMEM((core_runs, 2 * half), jnp.bfloat16),
            ],
            compiler_params=params(16),
            cost_estimate=cost(
                4 * core_runs * core_terms * slots * half, 2 * core_runs * core_terms
            ),
            name="design",
        )(packets, chosen, spots)

    designs = [design_of(packets), design_of(others)]

    fit_cost = cost(
        2 * total_runs * core_terms * own_modes, 2 * total_runs * core_terms
    )
    fitted, scale = pl.pallas_call(
        functools.partial(fit_kernel, 2 * rows),
        in_specs=[smem] + [vmem] * (3 + chips + CORES),
        out_specs=[vmem, vmem],
        out_shape=[
            jax.ShapeDtypeStruct((own_modes, total_runs), jnp.float32),
            jax.ShapeDtypeStruct((8, term_count), jnp.float32),
        ],
        scratch_shapes=[pltpu.VMEM((own_modes, core_terms), jnp.bfloat16)],
        compiler_params=params(16),
        cost_estimate=fit_cost,
        name="fit",
    )(me, weight_levels[None, :], packets, others, *blocks, *designs)
    beside = [reorder(start, fitted) for start in quarters[2]]
    summed = pl.pallas_call(
        functools.partial(sum_kernel, float(total_runs), chips),
        in_specs=[vmem] * (2 + CORES) + [anywhere] * len(beside),
        out_specs=[vmem] * chips,
        out_shape=[jax.ShapeDtypeStruct((own_modes, term_count), jnp.bfloat16)] * chips,
        compiler_params=params(16),
        cost_estimate=fit_cost,
        name="sum",
    )(fitted, to_device(fitted, 1), *designs, *beside)
    returned = to_chips(summed)
    ordered += tail + beside
    ordered += [reorder(start, summed[0]) for start in quarters[3]]

    return pl.pallas_call(
        functools.partial(finish_kernel, len(ordered)),
        in_specs=[smem] + [vmem] * (2 + len(ordered) + chips),
        out_specs=(anywhere, anywhere),
        out_shape=(
            jax.ShapeDtypeStruct((term_count, modes), jnp.float32),
            jax.ShapeDtypeStruct((term_count, slab_cells), jnp.bfloat16),
        ),
        scratch_shapes=[
            pltpu.VMEM((modes, term_count), jnp.float32),
            pltpu.VMEM((term_count, modes), jnp.float32),
            pltpu.VMEM((term_count, modes), jnp.bfloat16),
            pltpu.VMEM((len(ordered), term_count, block), jnp.bfloat16),
            pltpu.SemaphoreType.DMA,
            pltpu.SemaphoreType.DMA((len(ordered),)),
        ],
        compiler_params=params(20),
        name="finish",
    )(me, turned, scale, *ordered, *returned)


def hermite_table(points):
    squared = points * points
    columns = [
        jnp.ones_like(points),
        points,
        (squared - 1.0) / ROOT_TWO,
        points * (squared - 3.0) / ROOT_SIX,
        (squared * squared - 6.0 * squared + 3.0) / ROOT_TWENTYFOUR,
    ]
    return jnp.stack(columns, axis=-1).reshape(points.shape[0], -1)


def basis(points, codes):
    hermite = hermite_table(points)
    product = jnp.take(hermite, codes[:, 0], axis=1)
    for column in range(1, codes.shape[1]):
        product = product * jnp.take(hermite, codes[:, column], axis=1)
    return product.astype(jnp.bfloat16)


def shrink(values, limits):
    length = jnp.sqrt(jnp.sum(values * values, axis=1, keepdims=True) + EPSILON)
    return values * jnp.maximum(0.0, 1.0 - limits[:, None] / length)


def transposed_product(left, right):
    return lax.dot_general(
        left, right, (((0,), (0,)), ((), ())), preferred_element_type=jnp.float32
    )


def split_by_runs(
    run_inputs, term_codes, weight_levels, correlations, slab_modes, cell_map
):
    run_count = run_inputs.shape[0]
    term_count = correlations.shape[0]
    devices = lax.axis_size("runs")
    offset = lax.axis_index("runs") * term_count
    total_runs = run_count * devices
    weights_all = jnp.exp2(weight_levels.astype(jnp.float32))
    own_weights = lax.dynamic_slice_in_dim(weights_all, offset, term_count)
    own_corr = correlations.astype(jnp.float32)
    ratio = jnp.max(jnp.sqrt(jnp.sum(own_corr * own_corr, axis=1)) / own_weights)
    penalty = LAMBDA_FRACTION * lax.pmax(ratio, "runs")
    first = shrink(STEP * own_corr, STEP * penalty * own_weights)
    design = basis(run_inputs, term_codes)
    fitted = jnp.dot(
        design,
        lax.all_gather(first.astype(jnp.bfloat16), "runs", axis=0, tiled=True),
        preferred_element_type=jnp.float32,
    )
    fitted_half = fitted.astype(jnp.bfloat16)
    all_points = lax.all_gather(run_inputs, "runs", axis=0, tiled=True)
    own_codes = lax.dynamic_slice_in_dim(term_codes, offset, term_count, 0)
    owned_design = basis(all_points, own_codes)
    summed = transposed_product(
        owned_design, lax.all_gather(fitted_half, "runs", axis=0, tiled=True)
    )
    gradient = summed / total_runs - own_corr
    coefficients = shrink(first - STEP * gradient, STEP * penalty * own_weights)
    modes = jnp.take(slab_modes, cell_map, axis=0)
    lifted = lax.dot_general(
        coefficients.astype(jnp.bfloat16),
        modes,
        (((1,), (1,)), ((), ())),
        preferred_element_type=jnp.float32,
    ).astype(jnp.bfloat16)
    return (coefficients, lifted)


def on_device(
    run_inputs, term_codes, weight_levels, correlations, slab_modes, cell_map
):
    devices = lax.axis_size("runs")
    run_count = run_inputs.shape[0]
    term_count, modes = correlations.shape
    chips = max(1, devices // CORES)
    whole_tiles = (
        devices >= CORES
        and devices & (devices - 1) == 0
        and modes % (LANES * chips) == 0
        and term_count % LANES == 0
        and DEGREES * run_inputs.shape[1] <= LANES
        and LANES % run_count == 0
        and chips % (LANES // run_count) == 0
        and term_count % run_count == 0
        and run_inputs.shape[1] % (term_count // run_count) == 0
        and slab_modes.shape[0] % LANES == 0
        and cell_map.shape[0] % LANES == 0
    )
    plan = split_by_modes if whole_tiles else split_by_runs
    return plan(
        run_inputs, term_codes, weight_levels, correlations, slab_modes, cell_map
    )


def solution(mesh):
    return jax.shard_map(
        on_device,
        mesh=mesh,
        in_specs=(
            P(("cases", "runs"), None),
            P(),
            P(),
            P(("cases", "runs"), None),
            P("cases", None),
            P(),
        ),
        out_specs=(P(("cases", "runs"), None), P(("cases", "runs"), None)),
        check_vma=False,
    )
```

```python
import functools
import math

import jax
import jax.numpy as jnp
from jax import lax
from jax.experimental import pallas as pl
from jax.experimental.pallas import tpu as pltpu
from jax.sharding import PartitionSpec as P

STEP = 0.5
LAMBDA_FRACTION = 0.05
EPSILON = 1e-06
DEGREES = 5
LANES = 128
CORES = 2
FIRST_SLOTS = 7
ROOT_TWO = math.sqrt(2.0)
ROOT_SIX = math.sqrt(6.0)
ROOT_TWENTYFOUR = math.sqrt(24.0)
MIB = 1 << 20


def round_up(value, multiple):
    return -(-value // multiple) * multiple


def split_in_two(values):
    high = values.astype(jnp.bfloat16).astype(jnp.float32)
    return [high, values - high]


def partner(slot, chips):
    return slot and slot % (chips - 1) + 1


def rows_of(index, count):
    return pl.ds(pl.multiple_of(index * count, count), count)


def prepare_kernel(chips, me_ref, corr_ref, points_ref, turned_ref, packet_ref, *sent_refs):
    turned = corr_ref[...].astype(jnp.float32).T
    turned_ref[...] = turned.astype(jnp.bfloat16)
    squares = jnp.sum(turned * turned, axis=0, keepdims=True)
    packet_rows, terms = packet_ref.shape
    dim, runs = points_ref.shape
    rows = dim * runs // terms
    points = jnp.concatenate(
        [points_ref[start : start + rows, :] for start in range(0, dim, rows)], axis=1
    )
    pieces = split_in_two(points) + split_in_two(squares)
    used = 2 * rows + 2
    if packet_rows > used:
        pieces.append(jnp.zeros((packet_rows - used, terms), jnp.float32))
    packet_ref[...] = jnp.concatenate(pieces, axis=0).astype(jnp.bfloat16)
    fill_blocks(chips, 0, me_ref, turned_ref, packet_ref, sent_refs)


def fill_blocks(chips, first, me_ref, turned_ref, packet_ref, sent_refs):
    count = turned_ref.shape[0] // chips
    for k, sent_ref in enumerate(sent_refs, first):
        chip = (me_ref[0] // CORES) ^ partner(k, chips)
        sent_ref[0:count, :] = turned_ref[rows_of(chip, count), :]
        sent_ref[count : sent_ref.shape[0], :] = packet_ref[...]


def late_kernel(chips, me_ref, turned_ref, packet_ref, *refs):
    sent_refs = refs[len(refs) - (chips - FIRST_SLOTS) :]
    fill_blocks(chips, FIRST_SLOTS, me_ref, turned_ref, packet_ref, sent_refs)


def split_in_two(values):
    high = values.astype(jnp.bfloat16).astype(jnp.float32)
    return [high, values - high]


def hermite_columns(points):
    squared = points * points
    return jnp.concatenate(
        [
            jnp.ones_like(points),
            points,
            (squared - 1.0) / ROOT_TWO,
            points * (squared - 3.0) / ROOT_SIX,
            (squared * squared - 6.0 * squared + 3.0) / ROOT_TWENTYFOUR,
        ],
        axis=0,
    )


def collect_kernel(chips, *refs):
    packets_ref = refs[-1]
    rows = packets_ref.shape[1]
    for k, block_ref in enumerate(refs[:chips]):
        count = block_ref.shape[0]
        packets_ref[k] = block_ref[count - rows : count, :]


def choose_kernel(dim, chips, me_ref, codes_ref, *refs):
    chosen_ref, spots_ref = refs[-2:]
    matmuls, rows, terms = chosen_ref.shape
    half, tile = rows // 2, terms // chips
    row = lax.broadcasted_iota(jnp.int32, (half, tile), 0)
    for k in range(chips):
        device = me_ref[0] ^ (CORES * partner(k, chips))
        lanes = slice(k * tile, (k + 1) * tile)
        codes = codes_ref[:, rows_of(device, tile)]
        spots = (codes % DEGREES) * dim + codes // DEGREES
        spots_ref[:, lanes] = spots[matmuls:, :]
        for slot in range(matmuls):
            picked = jnp.where(row == spots[slot : slot + 1, :], 1.0, 0.0).astype(
                jnp.bfloat16
            )
            chosen_ref[slot, 0:half, lanes] = picked
            chosen_ref[slot, half:rows, lanes] = picked


def design_kernel(
    dim, run_count, packets_ref, chosen_ref, spots_ref, design_ref, exact, table
):
    chips, _, tile = packets_ref.shape
    half = exact.shape[1]
    rows = dim * run_count // tile
    terms = tile
    per = LANES // run_count
    for group in range(chips // per):
        owned = []
        for i in range(per):
            packet = packets_ref[group * per + i].astype(jnp.float32)
            owned.append(packet[0:rows, :] + packet[rows : 2 * rows, :])
        points = jnp.concatenate(
            [
                jnp.concatenate(
                    [inputs[:, start : start + run_count] for inputs in owned],
                    axis=1,
                )
                for start in range(0, terms, run_count)
            ],
            axis=0,
        )
        columns = hermite_columns(points)
        columns = jnp.concatenate(
            [
                columns,
                jnp.zeros((half - columns.shape[0], LANES), jnp.float32),
            ],
            axis=0,
        ).T
        high = columns.astype(jnp.bfloat16)
        low = (columns - high.astype(jnp.float32)).astype(jnp.bfloat16)
        block = slice(group * LANES, (group + 1) * LANES)
        exact[block, :] = columns
        table[block, 0:half] = high
        table[block, half : 2 * half] = low

    for start in range(0, table.shape[0], LANES):
        block = slice(start, start + LANES)
        values = exact[block, :]
        for first in range(0, design_ref.shape[1], tile):
            lanes = slice(first, first + tile)
            product = None
            for slot in range(chosen_ref.shape[0]):
                factor = jnp.dot(
                    table[block, :],
                    chosen_ref[slot, :, lanes],
                    preferred_element_type=jnp.float32,
                )
                product = factor if product is None else product * factor
            for part in range(0, tile, half):
                factor = product[:, part : part + half]
                lanes = slice(first + part, first + part + half)
                for slot in range(spots_ref.shape[0]):
                    spot = jnp.broadcast_to(
                        spots_ref[slot : slot + 1, lanes], values.shape
                    )
                    factor = factor * jnp.take_along_axis(values, spot, axis=1)
                design_ref[block, lanes] = factor.astype(jnp.bfloat16)


def shrink_factor(squares, limits):
    return jnp.maximum(0.0, 1.0 - limits / jnp.sqrt(squares + EPSILON))


def rows_and_weights(row, first, packets_ref, levels_ref):
    squares, levels = [], []
    for k in range(packets_ref.shape[0]):
        packet = packets_ref[k].astype(jnp.float32)
        squares.append(packet[row : row + 1, :] + packet[row + 1 : row + 2, :])
        device = first ^ (CORES * partner(k, packets_ref.shape[0]))
        levels.append(levels_ref[:, rows_of(device, packets_ref.shape[2])])
    weights = jnp.exp2(jnp.concatenate(levels, axis=1).astype(jnp.float32))
    return jnp.concatenate(squares, axis=1), weights


def fit_kernel(row, me_ref, levels_ref, own_ref, other_ref, *refs):
    *refs, fitted_ref, scale_ref, first_ref = refs
    block_refs, design_refs = refs[:-CORES], refs[-CORES:]
    count = fitted_ref.shape[0]
    term_count = own_ref.shape[2]
    me = me_ref[0]
    squares, weights = rows_and_weights(row, me, own_ref, levels_ref)
    others, other_weights = rows_and_weights(row, me ^ 1, other_ref, levels_ref)
    ratio = jnp.maximum(
        jnp.max(jnp.sqrt(squares) / weights, axis=1, keepdims=True),
        jnp.max(jnp.sqrt(others) / other_weights, axis=1, keepdims=True),
    )
    limits = STEP * (LAMBDA_FRACTION * ratio) * weights
    factor = shrink_factor(STEP * STEP * squares, limits)
    scale_ref[0:1, :] = factor[:, 0:term_count]
    scale_ref[1:2, :] = limits[:, 0:term_count]
    for k, block_ref in enumerate(block_refs):
        terms = slice(k * term_count, (k + 1) * term_count)
        first = STEP * block_ref[0:count, :].astype(jnp.float32) * factor[:, terms]
        first_ref[:, terms] = first.astype(jnp.bfloat16)
    runs = design_refs[0].shape[0]
    for i, design_ref in enumerate(design_refs):
        fitted_ref[:, i * runs : (i + 1) * runs] = lax.dot_general(
            first_ref[...],
            design_ref[...],
            (((1,), (1,)), ((), ())),
            preferred_element_type=jnp.float32,
        )


def sum_kernel(total_runs, chips, own_ref, other_ref, *refs):
    design_refs = refs[:CORES]
    summed_refs = refs[len(refs) - chips :]
    runs = design_refs[0].shape[0]
    near = own_ref[:, 0:runs] + other_ref[:, runs : 2 * runs]
    far = own_ref[:, runs : 2 * runs] + other_ref[:, 0:runs]
    near, far = near.astype(jnp.bfloat16), far.astype(jnp.bfloat16)
    term_count = summed_refs[0].shape[1]
    for k, summed_ref in enumerate(summed_refs):
        terms = slice(k * term_count, (k + 1) * term_count)
        summed = jnp.dot(
            near, design_refs[0][:, terms], preferred_element_type=jnp.float32
        ) + jnp.dot(far, design_refs[1][:, terms], preferred_element_type=jnp.float32)
        summed_ref[...] = (summed / total_runs).astype(jnp.bfloat16)


def reorder_kernel(map_ref, slab_ref, *refs):
    modes_ref = refs[-1]
    cells, block = slab_ref.shape[0], modes_ref.shape[0]
    row = lax.broadcasted_iota(jnp.int32, (cells, block), 0)
    chosen = jnp.where(row == map_ref[...], 1.0, 0.0).astype(jnp.bfloat16)
    modes_ref[...] = lax.dot_general(
        chosen,
        slab_ref[...],
        (((0,), (0,)), ((), ())),
        preferred_element_type=jnp.float32,
    ).astype(jnp.bfloat16)


def finish_kernel(pieces, me_ref, corr_ref, scale_ref, *refs):
    modes_refs, refs = refs[:pieces], refs[pieces:]
    *summed_refs, out_ref, lifted_ref, moved, values, half, lifted, out_sem, sems = refs
    modes, terms = corr_ref.shape
    count = summed_refs[0].shape[0]
    squares = jnp.zeros((1, terms), jnp.float32)
    for k, summed_ref in enumerate(summed_refs):
        rows = rows_of((me_ref[0] // CORES) ^ partner(k, len(summed_refs)), count)
        corr = corr_ref[rows, :].astype(jnp.float32)
        first = STEP * corr * scale_ref[0:1, :]
        gradient = summed_ref[...].astype(jnp.float32) - corr
        step = first - STEP * gradient
        moved[rows, :] = step
        squares = squares + jnp.sum(step * step, axis=0, keepdims=True)
    factor = shrink_factor(squares, scale_ref[1:2, :])
    for start in range(0, modes, LANES):
        block = slice(start, start + LANES)
        turned = (moved[block, :] * factor).T
        values[:, block] = turned
        half[:, block] = turned.astype(jnp.bfloat16)
    copies = [pltpu.make_async_copy(values, out_ref, out_sem)]
    copies[0].start()
    width = lifted.shape[2]
    for i, modes_ref in enumerate(modes_refs):
        block = slice(i * width, (i + 1) * width)
        lifted[i] = lax.dot_general(
            half[...],
            modes_ref[...],
            (((1,), (1,)), ((), ())),
            preferred_element_type=jnp.float32,
        ).astype(jnp.bfloat16)
        copies.append(
            pltpu.make_async_copy(lifted.at[i], lifted_ref.at[:, block], sems.at[i])
        )
        copies[-1].start()
    for copy in copies:
        copy.wait()


def in_hbm(array):
    return pltpu.with_memory_space_constraint(array, pltpu.HBM)


def params(limit):
    return pltpu.CompilerParams(vmem_limit_bytes=limit * MIB)


def cost(flops, moved):
    return pl.CostEstimate(flops=flops, bytes_accessed=moved, transcendentals=0)


def to_device(array, bits):
    devices = lax.axis_size("runs")
    return lax.ppermute(array, "runs", [(i, i ^ bits) for i in range(devices)])


def to_chips(arrays):
    chips = len(arrays)
    return [arrays[0]] + [
        to_device(arrays[k], CORES * partner(k, chips)) for k in range(1, chips)
    ]


def split_by_modes(
    run_inputs, term_codes, weight_levels, correlations, slab_modes, cell_map
):
    run_count, dim = run_inputs.shape
    term_count, modes = correlations.shape
    terms, slots = term_codes.shape
    cells = slab_modes.shape[0]
    slab_cells = cell_map.shape[0]
    chips = lax.axis_size("runs") // CORES
    total_runs = run_count * CORES * chips
    core_terms = terms // CORES
    own_modes = modes // chips
    rows = dim * run_count // term_count
    packet_rows = round_up(2 * rows + 2, 16)
    me = lax.axis_index("runs").astype(jnp.int32).reshape(1)
    smem = pl.BlockSpec(memory_space=pltpu.SMEM)
    vmem = pl.BlockSpec(memory_space=pltpu.VMEM)
    anywhere = pl.BlockSpec(memory_space=pl.ANY)

    early = min(chips, FIRST_SLOTS)
    block_type = jax.ShapeDtypeStruct((own_modes + packet_rows, term_count), jnp.bfloat16)
    turned, packet, *sent = pl.pallas_call(
        functools.partial(prepare_kernel, chips),
        in_specs=[smem, vmem, vmem],
        out_specs=[vmem] * (2 + early),
        out_shape=[
            jax.ShapeDtypeStruct((modes, term_count), jnp.bfloat16),
            jax.ShapeDtypeStruct((packet_rows, term_count), jnp.bfloat16),
        ]
        + [block_type] * early,
        compiler_params=params(16),
        name="prepare",
    )(me, in_hbm(correlations), in_hbm(run_inputs.T))

    block = math.gcd(512, slab_cells)

    def reorder(start, *after):
        return pl.pallas_call(
            reorder_kernel,
            in_specs=[vmem, vmem] + [anywhere] * len(after),
            out_specs=vmem,
            out_shape=jax.ShapeDtypeStruct((block, modes), jnp.bfloat16),
            compiler_params=params(16),
            cost_estimate=cost(2 * cells * block * modes, 2 * cells * modes),
            name="reorder",
        )(cell_map[None, start : start + block], slab_modes, *after)

    starts = range(0, slab_cells, block)
    quarters = [starts[i * len(starts) // 4 : (i + 1) * len(starts) // 4] for i in range(4)]
    ordered = [reorder(start) for start in quarters[0]]
    half = round_up(DEGREES * dim, LANES)
    gathers = slots // 4
    chosen, spots = pl.pallas_call(
        functools.partial(choose_kernel, dim, chips),
        in_specs=[smem, vmem],
        out_specs=[vmem, vmem],
        out_shape=[
            jax.ShapeDtypeStruct((slots - gathers, 2 * half, core_terms), jnp.bfloat16),
            jax.ShapeDtypeStruct((gathers, core_terms), jnp.int32),
        ],
        compiler_params=params(8),
        cost_estimate=cost(0, 2 * slots * half * core_terms),
        name="choose",
    )(me, in_hbm(term_codes.T))
    if chips > early:
        sent += pl.pallas_call(
            functools.partial(late_kernel, chips),
            in_specs=[smem, vmem, vmem] + [anywhere] * (1 + len(ordered)),
            out_specs=[vmem] * (chips - early),
            out_shape=[block_type] * (chips - early),
            compiler_params=params(8),
            name="late",
        )(me, turned, packet, spots, *ordered)
    blocks = to_chips(sent)
    tail = [reorder(start, *blocks[1:3]) for start in quarters[1]]
    packets = pl.pallas_call(
        functools.partial(collect_kernel, chips),
        in_specs=[vmem] * chips + [anywhere] * len(tail),
        out_specs=vmem,
        out_shape=jax.ShapeDtypeStruct((chips, packet_rows, term_count), jnp.bfloat16),
        compiler_params=params(8),
        name="collect",
    )(*blocks, *tail)
    others = to_device(packets, 1)

    core_runs = run_count * chips

    def design_of(packets):
        return pl.pallas_call(
            functools.partial(design_kernel, dim, run_count),
            in_specs=[vmem] * 3,
            out_specs=vmem,
            out_shape=jax.ShapeDtypeStruct((core_runs, core_terms), jnp.bfloat16),
            scratch_shapes=[
                pltpu.VMEM((core_runs, half), jnp.float32),
                pltpu.VMEM((core_runs, 2 * half), jnp.bfloat16),
            ],
            compiler_params=params(16),
            cost_estimate=cost(
                4 * core_runs * core_terms * slots * half, 2 * core_runs * core_terms
            ),
            name="design",
        )(packets, chosen, spots)

    designs = [design_of(packets), design_of(others)]

    fit_cost = cost(
        2 * total_runs * core_terms * own_modes, 2 * total_runs * core_terms
    )
    fitted, scale = pl.pallas_call(
        functools.partial(fit_kernel, 2 * rows),
        in_specs=[smem] + [vmem] * (3 + chips + CORES),
        out_specs=[vmem, vmem],
        out_shape=[
            jax.ShapeDtypeStruct((own_modes, total_runs), jnp.float32),
            jax.ShapeDtypeStruct((8, term_count), jnp.float32),
        ],
        scratch_shapes=[pltpu.VMEM((own_modes, core_terms), jnp.bfloat16)],
        compiler_params=params(16),
        cost_estimate=fit_cost,
        name="fit",
    )(me, weight_levels[None, :], packets, others, *blocks, *designs)
    beside = [reorder(start, fitted) for start in quarters[2]]
    summed = pl.pallas_call(
        functools.partial(sum_kernel, float(total_runs), chips),
        in_specs=[vmem] * (2 + CORES) + [anywhere] * len(beside),
        out_specs=[vmem] * chips,
        out_shape=[jax.ShapeDtypeStruct((own_modes, term_count), jnp.bfloat16)] * chips,
        compiler_params=params(16),
        cost_estimate=fit_cost,
        name="sum",
    )(fitted, to_device(fitted, 1), *designs, *beside)
    returned = to_chips(summed)
    ordered += tail + beside
    ordered += [reorder(start, summed[0]) for start in quarters[3]]

    return pl.pallas_call(
        functools.partial(finish_kernel, len(ordered)),
        in_specs=[smem] + [vmem] * (2 + len(ordered) + chips),
        out_specs=(anywhere, anywhere),
        out_shape=(
            jax.ShapeDtypeStruct((term_count, modes), jnp.float32),
            jax.ShapeDtypeStruct((term_count, slab_cells), jnp.bfloat16),
        ),
        scratch_shapes=[
            pltpu.VMEM((modes, term_count), jnp.float32),
            pltpu.VMEM((term_count, modes), jnp.float32),
            pltpu.VMEM((term_count, modes), jnp.bfloat16),
            pltpu.VMEM((len(ordered), term_count, block), jnp.bfloat16),
            pltpu.SemaphoreType.DMA,
            pltpu.SemaphoreType.DMA((len(ordered),)),
        ],
        compiler_params=params(20),
        name="finish",
    )(me, turned, scale, *ordered, *returned)


def hermite_table(points):
    squared = points * points
    columns = [
        jnp.ones_like(points),
        points,
        (squared - 1.0) / ROOT_TWO,
        points * (squared - 3.0) / ROOT_SIX,
        (squared * squared - 6.0 * squared + 3.0) / ROOT_TWENTYFOUR,
    ]
    return jnp.stack(columns, axis=-1).reshape(points.shape[0], -1)


def basis(points, codes):
    hermite = hermite_table(points)
    product = jnp.take(hermite, codes[:, 0], axis=1)
    for column in range(1, codes.shape[1]):
        product = product * jnp.take(hermite, codes[:, column], axis=1)
    return product.astype(jnp.bfloat16)


def shrink(values, limits):
    length = jnp.sqrt(jnp.sum(values * values, axis=1, keepdims=True) + EPSILON)
    return values * jnp.maximum(0.0, 1.0 - limits[:, None] / length)


def transposed_product(left, right):
    return lax.dot_general(
        left, right, (((0,), (0,)), ((), ())), preferred_element_type=jnp.float32
    )


def split_by_runs(
    run_inputs, term_codes, weight_levels, correlations, slab_modes, cell_map
):
    run_count = run_inputs.shape[0]
    term_count = correlations.shape[0]
    devices = lax.axis_size("runs")
    offset = lax.axis_index("runs") * term_count
    total_runs = run_count * devices
    weights_all = jnp.exp2(weight_levels.astype(jnp.float32))
    own_weights = lax.dynamic_slice_in_dim(weights_all, offset, term_count)
    own_corr = correlations.astype(jnp.float32)
    ratio = jnp.max(jnp.sqrt(jnp.sum(own_corr * own_corr, axis=1)) / own_weights)
    penalty = LAMBDA_FRACTION * lax.pmax(ratio, "runs")
    first = shrink(STEP * own_corr, STEP * penalty * own_weights)
    design = basis(run_inputs, term_codes)
    fitted = jnp.dot(
        design,
        lax.all_gather(first.astype(jnp.bfloat16), "runs", axis=0, tiled=True),
        preferred_element_type=jnp.float32,
    )
    fitted_half = fitted.astype(jnp.bfloat16)
    all_points = lax.all_gather(run_inputs, "runs", axis=0, tiled=True)
    own_codes = lax.dynamic_slice_in_dim(term_codes, offset, term_count, 0)
    owned_design = basis(all_points, own_codes)
    summed = transposed_product(
        owned_design, lax.all_gather(fitted_half, "runs", axis=0, tiled=True)
    )
    gradient = summed / total_runs - own_corr
    coefficients = shrink(first - STEP * gradient, STEP * penalty * own_weights)
    modes = jnp.take(slab_modes, cell_map, axis=0)
    lifted = lax.dot_general(
        coefficients.astype(jnp.bfloat16),
        modes,
        (((1,), (1,)), ((), ())),
        preferred_element_type=jnp.float32,
    ).astype(jnp.bfloat16)
    return (coefficients, lifted)


def on_device(
    run_inputs, term_codes, weight_levels, correlations, slab_modes, cell_map
):
    devices = lax.axis_size("runs")
    run_count = run_inputs.shape[0]
    term_count, modes = correlations.shape
    chips = max(1, devices // CORES)
    whole_tiles = (
        devices >= CORES
        and devices & (devices - 1) == 0
        and modes % (LANES * chips) == 0
        and term_count % LANES == 0
        and DEGREES * run_inputs.shape[1] <= LANES
        and LANES % run_count == 0
        and chips % (LANES // run_count) == 0
        and term_count % run_count == 0
        and run_inputs.shape[1] % (term_count // run_count) == 0
        and slab_modes.shape[0] % LANES == 0
        and cell_map.shape[0] % LANES == 0
    )
    plan = split_by_modes if whole_tiles else split_by_runs
    return plan(
        run_inputs, term_codes, weight_levels, correlations, slab_modes, cell_map
    )


def solution(mesh):
    return jax.shard_map(
        on_device,
        mesh=mesh,
        in_specs=(
            P(("cases", "runs"), None),
            P(),
            P(),
            P(("cases", "runs"), None),
            P("cases", None),
            P(),
        ),
        out_specs=(P(("cases", "runs"), None), P(("cases", "runs"), None)),
        check_vma=False,
    )
```

```python
import functools
import math

import jax
import jax.numpy as jnp
from jax import lax
from jax.experimental import pallas as pl
from jax.experimental.pallas import tpu as pltpu
from jax.sharding import PartitionSpec as P

STEP = 0.5
LAMBDA_FRACTION = 0.05
EPSILON = 1e-06
DEGREES = 5
LANES = 128
CORES = 2
ROOT_TWO = math.sqrt(2.0)
ROOT_SIX = math.sqrt(6.0)
ROOT_TWENTYFOUR = math.sqrt(24.0)
MIB = 1 << 20


def round_up(value, multiple):
    return -(-value // multiple) * multiple


def split_in_two(values):
    high = values.astype(jnp.bfloat16).astype(jnp.float32)
    return [high, values - high]


def partner(slot, chips):
    return slot and slot % (chips - 1) + 1


def rows_of(index, count):
    return pl.ds(pl.multiple_of(index * count, count), count)


def prepare_kernel(chips, me_ref, corr_ref, points_ref, turned_ref, packet_ref, *sent_refs):
    turned = corr_ref[...].astype(jnp.float32).T
    turned_ref[...] = turned.astype(jnp.bfloat16)
    squares = jnp.sum(turned * turned, axis=0, keepdims=True)
    packet_rows, terms = packet_ref.shape
    dim, runs = points_ref.shape
    rows = dim * runs // terms
    points = jnp.concatenate(
        [points_ref[start : start + rows, :] for start in range(0, dim, rows)], axis=1
    )
    pieces = split_in_two(points) + split_in_two(squares)
    used = 2 * rows + 2
    if packet_rows > used:
        pieces.append(jnp.zeros((packet_rows - used, terms), jnp.float32))
    packet_ref[...] = jnp.concatenate(pieces, axis=0).astype(jnp.bfloat16)
    fill_blocks(chips, me_ref, turned_ref, packet_ref, sent_refs)


def fill_blocks(chips, me_ref, turned_ref, packet_ref, sent_refs):
    count = turned_ref.shape[0] // chips
    for k, sent_ref in enumerate(sent_refs):
        chip = (me_ref[0] // CORES) ^ partner(k, chips)
        sent_ref[0:count, :] = turned_ref[rows_of(chip, count), :]
        sent_ref[count : sent_ref.shape[0], :] = packet_ref[...]


def split_in_two(values):
    high = values.astype(jnp.bfloat16).astype(jnp.float32)
    return [high, values - high]


def partner(slot, chips):
    return slot and slot % (chips - 1) + 1


def rows_of(index, count):
    return pl.ds(pl.multiple_of(index * count, count), count)


def prepare_kernel(chips, me_ref, corr_ref, points_ref, turned_ref, packet_ref, *sent_refs):
    turned = corr_ref[...].astype(jnp.float32).T
    turned_ref[...] = turned.astype(jnp.bfloat16)
    squares = jnp.sum(turned * turned, axis=0, keepdims=True)
    packet_rows, terms = packet_ref.shape
    dim, runs = points_ref.shape
    rows = dim * runs // terms
    points = jnp.concatenate(
        [points_ref[start : start + rows, :] for start in range(0, dim, rows)], axis=1
    )
    pieces = split_in_two(points) + split_in_two(squares)
    used = 2 * rows + 2
    if packet_rows > used:
        pieces.append(jnp.zeros((packet_rows - used, terms), jnp.float32))
    packet_ref[...] = jnp.concatenate(pieces, axis=0).astype(jnp.bfloat16)
    fill_blocks(chips, me_ref, turned_ref, packet_ref, sent_refs)


def fill_blocks(chips, me_ref, turned_ref, packet_ref, sent_refs):
    count = turned_ref.shape[0] // chips
    for k, sent_ref in enumerate(sent_refs):
        chip = (me_ref[0] // CORES) ^ partner(k, chips)
        sent_ref[0:count, :] = turned_ref[rows_of(chip, count), :]
        sent_ref[count : sent_ref.shape[0], :] = packet_ref[...]


def late_kernel(chips, me_ref, turned_ref, packet_ref, *refs):
    sent_refs = refs[len(refs) - (chips - FIRST_SLOTS) :]
    fill_blocks(chips, FIRST_SLOTS, me_ref, turned_ref, packet_ref, sent_refs)


def split_in_two(values):
    high = values.astype(jnp.bfloat16).astype(jnp.float32)
    return [high, values - high]


def hermite_columns(points):
    squared = points * points
    return jnp.concatenate(
        [
            jnp.ones_like(points),
            points,
            (squared - 1.0) / ROOT_TWO,
            points * (squared - 3.0) / ROOT_SIX,
            (squared * squared - 6.0 * squared + 3.0) / ROOT_TWENTYFOUR,
        ],
        axis=0,
    )


def collect_kernel(chips, *refs):
    packets_ref = refs[-1]
    rows = packets_ref.shape[1]
    for k, block_ref in enumerate(refs[:chips]):
        count = block_ref.shape[0]
        packets_ref[k] = block_ref[count - rows : count, :]


def choose_kernel(dim, chips, me_ref, codes_ref, *refs):
    chosen_ref, spots_ref = refs[-2:]
    matmuls, rows, terms = chosen_ref.shape
    half, tile = rows // 2, terms // chips
    row = lax.broadcasted_iota(jnp.int32, (half, tile), 0)
    for k in range(chips):
        device = me_ref[0] ^ (CORES * partner(k, chips))
        lanes = slice(k * tile, (k + 1) * tile)
        codes = codes_ref[:, rows_of(device, tile)]
        spots = (codes % DEGREES) * dim + codes // DEGREES
        spots_ref[:, lanes] = spots[matmuls:, :]
        for slot in range(matmuls):
            picked = jnp.where(row == spots[slot : slot + 1, :], 1.0, 0.0).astype(
                jnp.bfloat16
            )
            chosen_ref[slot, 0:half, lanes] = picked
            chosen_ref[slot, half:rows, lanes] = picked


def design_kernel(
    dim, run_count, packets_ref, chosen_ref, spots_ref, design_ref, exact, table
):
    chips, _, tile = packets_ref.shape
    half = exact.shape[1]
    rows = dim * run_count // tile
    terms = tile
    per = LANES // run_count
    for group in range(chips // per):
        owned = []
        for i in range(per):
            packet = packets_ref[group * per + i].astype(jnp.float32)
            owned.append(packet[0:rows, :] + packet[rows : 2 * rows, :])
        points = jnp.concatenate(
            [
                jnp.concatenate(
                    [inputs[:, start : start + run_count] for inputs in owned],
                    axis=1,
                )
                for start in range(0, terms, run_count)
            ],
            axis=0,
        )
        columns = hermite_columns(points)
        columns = jnp.concatenate(
            [
                columns,
                jnp.zeros((half - columns.shape[0], LANES), jnp.float32),
            ],
            axis=0,
        ).T
        high = columns.astype(jnp.bfloat16)
        low = (columns - high.astype(jnp.float32)).astype(jnp.bfloat16)
        block = slice(group * LANES, (group + 1) * LANES)
        exact[block, :] = columns
        table[block, 0:half] = high
        table[block, half : 2 * half] = low

    for start in range(0, table.shape[0], LANES):
        block = slice(start, start + LANES)
        values = exact[block, :]
        for first in range(0, design_ref.shape[1], tile):
            lanes = slice(first, first + tile)
            product = None
            for slot in range(chosen_ref.shape[0]):
                factor = jnp.dot(
                    table[block, :],
                    chosen_ref[slot, :, lanes],
                    preferred_element_type=jnp.float32,
                )
                product = factor if product is None else product * factor
            for part in range(0, tile, half):
                factor = product[:, part : part + half]
                lanes = slice(first + part, first + part + half)
                for slot in range(spots_ref.shape[0]):
                    spot = jnp.broadcast_to(
                        spots_ref[slot : slot + 1, lanes], values.shape
                    )
                    factor = factor * jnp.take_along_axis(values, spot, axis=1)
                design_ref[block, lanes] = factor.astype(jnp.bfloat16)


def shrink_factor(squares, limits):
    return jnp.maximum(0.0, 1.0 - limits / jnp.sqrt(squares + EPSILON))


def rows_and_weights(row, first, packets_ref, levels_ref):
    squares, levels = [], []
    for k in range(packets_ref.shape[0]):
        packet = packets_ref[k].astype(jnp.float32)
        squares.append(packet[row : row + 1, :] + packet[row + 1 : row + 2, :])
        device = first ^ (CORES * partner(k, packets_ref.shape[0]))
        levels.append(levels_ref[:, rows_of(device, packets_ref.shape[2])])
    weights = jnp.exp2(jnp.concatenate(levels, axis=1).astype(jnp.float32))
    return jnp.concatenate(squares, axis=1), weights


def fit_kernel(row, me_ref, levels_ref, own_ref, other_ref, *refs):
    *refs, fitted_ref, scale_ref, first_ref = refs
    block_refs, design_refs = refs[:-CORES], refs[-CORES:]
    count = fitted_ref.shape[0]
    term_count = own_ref.shape[2]
    me = me_ref[0]
    squares, weights = rows_and_weights(row, me, own_ref, levels_ref)
    others, other_weights = rows_and_weights(row, me ^ 1, other_ref, levels_ref)
    ratio = jnp.maximum(
        jnp.max(jnp.sqrt(squares) / weights, axis=1, keepdims=True),
        jnp.max(jnp.sqrt(others) / other_weights, axis=1, keepdims=True),
    )
    limits = STEP * (LAMBDA_FRACTION * ratio) * weights
    factor = shrink_factor(STEP * STEP * squares, limits)
    scale_ref[0:1, :] = factor[:, 0:term_count]
    scale_ref[1:2, :] = limits[:, 0:term_count]
    for k, block_ref in enumerate(block_refs):
        terms = slice(k * term_count, (k + 1) * term_count)
        first = STEP * block_ref[0:count, :].astype(jnp.float32) * factor[:, terms]
        first_ref[:, terms] = first.astype(jnp.bfloat16)
    runs = design_refs[0].shape[0]
    for i, design_ref in enumerate(design_refs):
        fitted_ref[:, i * runs : (i + 1) * runs] = lax.dot_general(
            first_ref[...],
            design_ref[...],
            (((1,), (1,)), ((), ())),
            preferred_element_type=jnp.float32,
        )


def sum_kernel(total_runs, chips, own_ref, other_ref, *refs):
    design_refs = refs[:CORES]
    summed_refs = refs[len(refs) - chips :]
    runs = design_refs[0].shape[0]
    near = own_ref[:, 0:runs] + other_ref[:, runs : 2 * runs]
    far = own_ref[:, runs : 2 * runs] + other_ref[:, 0:runs]
    near, far = near.astype(jnp.bfloat16), far.astype(jnp.bfloat16)
    term_count = summed_refs[0].shape[1]
    for k, summed_ref in enumerate(summed_refs):
        terms = slice(k * term_count, (k + 1) * term_count)
        summed = jnp.dot(
            near, design_refs[0][:, terms], preferred_element_type=jnp.float32
        ) + jnp.dot(far, design_refs[1][:, terms], preferred_element_type=jnp.float32)
        summed_ref[...] = (summed / total_runs).astype(jnp.bfloat16)


def reorder_kernel(map_ref, slab_ref, *refs):
    modes_ref = refs[-1]
    cells, block = slab_ref.shape[0], modes_ref.shape[0]
    row = lax.broadcasted_iota(jnp.int32, (cells, block), 0)
    chosen = jnp.where(row == map_ref[...], 1.0, 0.0).astype(jnp.bfloat16)
    modes_ref[...] = lax.dot_general(
        chosen,
        slab_ref[...],
        (((0,), (0,)), ((), ())),
        preferred_element_type=jnp.float32,
    ).astype(jnp.bfloat16)


def finish_kernel(pieces, me_ref, corr_ref, scale_ref, *refs):
    modes_refs, refs = refs[:pieces], refs[pieces:]
    *summed_refs, out_ref, lifted_ref, moved, values, half, lifted, out_sem, sems = refs
    modes, terms = corr_ref.shape
    count = summed_refs[0].shape[0]
    squares = jnp.zeros((1, terms), jnp.float32)
    for k, summed_ref in enumerate(summed_refs):
        rows = rows_of((me_ref[0] // CORES) ^ partner(k, len(summed_refs)), count)
        corr = corr_ref[rows, :].astype(jnp.float32)
        first = STEP * corr * scale_ref[0:1, :]
        gradient = summed_ref[...].astype(jnp.float32) - corr
        step = first - STEP * gradient
        moved[rows, :] = step
        squares = squares + jnp.sum(step * step, axis=0, keepdims=True)
    factor = shrink_factor(squares, scale_ref[1:2, :])
    for start in range(0, modes, LANES):
        block = slice(start, start + LANES)
        turned = (moved[block, :] * factor).T
        values[:, block] = turned
        half[:, block] = turned.astype(jnp.bfloat16)
    copies = [pltpu.make_async_copy(values, out_ref, out_sem)]
    copies[0].start()
    width = lifted.shape[2]
    for i, modes_ref in enumerate(modes_refs):
        block = slice(i * width, (i + 1) * width)
        lifted[i] = lax.dot_general(
            half[...],
            modes_ref[...],
            (((1,), (1,)), ((), ())),
            preferred_element_type=jnp.float32,
        ).astype(jnp.bfloat16)
        copies.append(
            pltpu.make_async_copy(lifted.at[i], lifted_ref.at[:, block], sems.at[i])
        )
        copies[-1].start()
    for copy in copies:
        copy.wait()


def in_hbm(array):
    return pltpu.with_memory_space_constraint(array, pltpu.HBM)


def params(limit):
    return pltpu.CompilerParams(vmem_limit_bytes=limit * MIB)


def cost(flops, moved):
    return pl.CostEstimate(flops=flops, bytes_accessed=moved, transcendentals=0)


def to_device(array, bits):
    devices = lax.axis_size("runs")
    return lax.ppermute(array, "runs", [(i, i ^ bits) for i in range(devices)])


def to_chips(arrays):
    chips = len(arrays)
    return [arrays[0]] + [
        to_device(arrays[k], CORES * partner(k, chips)) for k in range(1, chips)
    ]


def split_by_modes(
    run_inputs, term_codes, weight_levels, correlations, slab_modes, cell_map
):
    run_count, dim = run_inputs.shape
    term_count, modes = correlations.shape
    terms, slots = term_codes.shape
    cells = slab_modes.shape[0]
    slab_cells = cell_map.shape[0]
    chips = lax.axis_size("runs") // CORES
    total_runs = run_count * CORES * chips
    core_terms = terms // CORES
    own_modes = modes // chips
    rows = dim * run_count // term_count
    packet_rows = round_up(2 * rows + 2, 16)
    me = lax.axis_index("runs").astype(jnp.int32).reshape(1)
    smem = pl.BlockSpec(memory_space=pltpu.SMEM)
    vmem = pl.BlockSpec(memory_space=pltpu.VMEM)
    anywhere = pl.BlockSpec(memory_space=pl.ANY)

    block_type = jax.ShapeDtypeStruct((own_modes + packet_rows, term_count), jnp.bfloat16)
    turned, packet, *sent = pl.pallas_call(
        functools.partial(prepare_kernel, chips),
        in_specs=[smem, vmem, vmem],
        out_specs=[vmem] * (2 + chips),
        out_shape=[
            jax.ShapeDtypeStruct((modes, term_count), jnp.bfloat16),
            jax.ShapeDtypeStruct((packet_rows, term_count), jnp.bfloat16),
        ]
        + [block_type] * chips,
        compiler_params=params(16),
        name="prepare",
    )(me, in_hbm(correlations), in_hbm(run_inputs.T))

    block = math.gcd(512, slab_cells)

    def reorder(start, *after):
        return pl.pallas_call(
            reorder_kernel,
            in_specs=[vmem, vmem] + [anywhere] * len(after),
            out_specs=vmem,
            out_shape=jax.ShapeDtypeStruct((block, modes), jnp.bfloat16),
            compiler_params=params(16),
            cost_estimate=cost(2 * cells * block * modes, 2 * cells * modes),
            name="reorder",
        )(cell_map[None, start : start + block], slab_modes, *after)

    starts = range(0, slab_cells, block)
    quarters = [starts[i * len(starts) // 4 : (i + 1) * len(starts) // 4] for i in range(4)]
    blocks = to_chips(sent)
    half = round_up(DEGREES * dim, LANES)
    gathers = slots // 4
    chosen, spots = pl.pallas_call(
        functools.partial(choose_kernel, dim, chips),
        in_specs=[smem, vmem] + [anywhere] * len(blocks[1:3]),
        out_specs=[vmem, vmem],
        out_shape=[
            jax.ShapeDtypeStruct((slots - gathers, 2 * half, core_terms), jnp.bfloat16),
            jax.ShapeDtypeStruct((gathers, core_terms), jnp.int32),
        ],
        compiler_params=params(8),
        cost_estimate=cost(0, 2 * slots * half * core_terms),
        name="choose",
    )(me, in_hbm(term_codes.T), *blocks[1:3])
    ordered = [
        reorder(start, *blocks[1:3]) for start in [*quarters[0], *quarters[1]]
    ]
    packets = pl.pallas_call(
        functools.partial(collect_kernel, chips),
        in_specs=[vmem] * chips + [anywhere] * (1 + len(ordered)),
        out_specs=vmem,
        out_shape=jax.ShapeDtypeStruct((chips, packet_rows, term_count), jnp.bfloat16),
        compiler_params=params(8),
        name="collect",
    )(*blocks, spots, *ordered)
    others = to_device(packets, 1)

    core_runs = run_count * chips

    def design_of(packets):
        return pl.pallas_call(
            functools.partial(design_kernel, dim, run_count),
            in_specs=[vmem] * 3,
            out_specs=vmem,
            out_shape=jax.ShapeDtypeStruct((core_runs, core_terms), jnp.bfloat16),
            scratch_shapes=[
                pltpu.VMEM((core_runs, half), jnp.float32),
                pltpu.VMEM((core_runs, 2 * half), jnp.bfloat16),
            ],
            compiler_params=params(16),
            cost_estimate=cost(
                4 * core_runs * core_terms * slots * half, 2 * core_runs * core_terms
            ),
            name="design",
        )(packets, chosen, spots)

    designs = [design_of(packets), design_of(others)]

    fit_cost = cost(
        2 * total_runs * core_terms * own_modes, 2 * total_runs * core_terms
    )
    fitted, scale = pl.pallas_call(
        functools.partial(fit_kernel, 2 * rows),
        in_specs=[smem] + [vmem] * (3 + chips + CORES),
        out_specs=[vmem, vmem],
        out_shape=[
            jax.ShapeDtypeStruct((own_modes, total_runs), jnp.float32),
            jax.ShapeDtypeStruct((8, term_count), jnp.float32),
        ],
        scratch_shapes=[pltpu.VMEM((own_modes, core_terms), jnp.bfloat16)],
        compiler_params=params(16),
        cost_estimate=fit_cost,
        name="fit",
    )(me, weight_levels[None, :], packets, others, *blocks, *designs)
    beside = [reorder(start, fitted) for start in quarters[2]]
    summed = pl.pallas_call(
        functools.partial(sum_kernel, float(total_runs), chips),
        in_specs=[vmem] * (2 + CORES) + [anywhere] * len(beside),
        out_specs=[vmem] * chips,
        out_shape=[jax.ShapeDtypeStruct((own_modes, term_count), jnp.bfloat16)] * chips,
        compiler_params=params(16),
        cost_estimate=fit_cost,
        name="sum",
    )(fitted, to_device(fitted, 1), *designs, *beside)
    returned = to_chips(summed)
    ordered += beside
    ordered += [reorder(start, summed[0]) for start in quarters[3]]

    return pl.pallas_call(
        functools.partial(finish_kernel, len(ordered)),
        in_specs=[smem] + [vmem] * (2 + len(ordered) + chips),
        out_specs=(anywhere, anywhere),
        out_shape=(
            jax.ShapeDtypeStruct((term_count, modes), jnp.float32),
            jax.ShapeDtypeStruct((term_count, slab_cells), jnp.bfloat16),
        ),
        scratch_shapes=[
            pltpu.VMEM((modes, term_count), jnp.float32),
            pltpu.VMEM((term_count, modes), jnp.float32),
            pltpu.VMEM((term_count, modes), jnp.bfloat16),
            pltpu.VMEM((len(ordered), term_count, block), jnp.bfloat16),
            pltpu.SemaphoreType.DMA,
            pltpu.SemaphoreType.DMA((len(ordered),)),
        ],
        compiler_params=params(20),
        name="finish",
    )(me, turned, scale, *ordered, *returned)


def hermite_table(points):
    squared = points * points
    columns = [
        jnp.ones_like(points),
        points,
        (squared - 1.0) / ROOT_TWO,
        points * (squared - 3.0) / ROOT_SIX,
        (squared * squared - 6.0 * squared + 3.0) / ROOT_TWENTYFOUR,
    ]
    return jnp.stack(columns, axis=-1).reshape(points.shape[0], -1)


def basis(points, codes):
    hermite = hermite_table(points)
    product = jnp.take(hermite, codes[:, 0], axis=1)
    for column in range(1, codes.shape[1]):
        product = product * jnp.take(hermite, codes[:, column], axis=1)
    return product.astype(jnp.bfloat16)


def shrink(values, limits):
    length = jnp.sqrt(jnp.sum(values * values, axis=1, keepdims=True) + EPSILON)
    return values * jnp.maximum(0.0, 1.0 - limits[:, None] / length)


def transposed_product(left, right):
    return lax.dot_general(
        left, right, (((0,), (0,)), ((), ())), preferred_element_type=jnp.float32
    )


def split_by_runs(
    run_inputs, term_codes, weight_levels, correlations, slab_modes, cell_map
):
    run_count = run_inputs.shape[0]
    term_count = correlations.shape[0]
    devices = lax.axis_size("runs")
    offset = lax.axis_index("runs") * term_count
    total_runs = run_count * devices
    weights_all = jnp.exp2(weight_levels.astype(jnp.float32))
    own_weights = lax.dynamic_slice_in_dim(weights_all, offset, term_count)
    own_corr = correlations.astype(jnp.float32)
    ratio = jnp.max(jnp.sqrt(jnp.sum(own_corr * own_corr, axis=1)) / own_weights)
    penalty = LAMBDA_FRACTION * lax.pmax(ratio, "runs")
    first = shrink(STEP * own_corr, STEP * penalty * own_weights)
    design = basis(run_inputs, term_codes)
    fitted = jnp.dot(
        design,
        lax.all_gather(first.astype(jnp.bfloat16), "runs", axis=0, tiled=True),
        preferred_element_type=jnp.float32,
    )
    fitted_half = fitted.astype(jnp.bfloat16)
    all_points = lax.all_gather(run_inputs, "runs", axis=0, tiled=True)
    own_codes = lax.dynamic_slice_in_dim(term_codes, offset, term_count, 0)
    owned_design = basis(all_points, own_codes)
    summed = transposed_product(
        owned_design, lax.all_gather(fitted_half, "runs", axis=0, tiled=True)
    )
    gradient = summed / total_runs - own_corr
    coefficients = shrink(first - STEP * gradient, STEP * penalty * own_weights)
    modes = jnp.take(slab_modes, cell_map, axis=0)
    lifted = lax.dot_general(
        coefficients.astype(jnp.bfloat16),
        modes,
        (((1,), (1,)), ((), ())),
        preferred_element_type=jnp.float32,
    ).astype(jnp.bfloat16)
    return (coefficients, lifted)


def on_device(
    run_inputs, term_codes, weight_levels, correlations, slab_modes, cell_map
):
    devices = lax.axis_size("runs")
    run_count = run_inputs.shape[0]
    term_count, modes = correlations.shape
    chips = max(1, devices // CORES)
    whole_tiles = (
        devices >= CORES
        and devices & (devices - 1) == 0
        and modes % (LANES * chips) == 0
        and term_count % LANES == 0
        and DEGREES * run_inputs.shape[1] <= LANES
        and LANES % run_count == 0
        and chips % (LANES // run_count) == 0
        and term_count % run_count == 0
        and run_inputs.shape[1] % (term_count // run_count) == 0
        and slab_modes.shape[0] % LANES == 0
        and cell_map.shape[0] % LANES == 0
    )
    plan = split_by_modes if whole_tiles else split_by_runs
    return plan(
        run_inputs, term_codes, weight_levels, correlations, slab_modes, cell_map
    )


def solution(mesh):
    return jax.shard_map(
        on_device,
        mesh=mesh,
        in_specs=(
            P(("cases", "runs"), None),
            P(),
            P(),
            P(("cases", "runs"), None),
            P("cases", None),
            P(),
        ),
        out_specs=(P(("cases", "runs"), None), P(("cases", "runs"), None)),
        check_vma=False,
    )
```

```python
import functools
import math

import jax
import jax.numpy as jnp
from jax import lax
from jax.experimental import pallas as pl
from jax.experimental.pallas import tpu as pltpu
from jax.sharding import PartitionSpec as P

STEP = 0.5
LAMBDA_FRACTION = 0.05
EPSILON = 1e-06
DEGREES = 5
LANES = 128
CORES = 2
ROOT_TWO = math.sqrt(2.0)
ROOT_SIX = math.sqrt(6.0)
ROOT_TWENTYFOUR = math.sqrt(24.0)
MIB = 1 << 20


def round_up(value, multiple):
    return -(-value // multiple) * multiple


def split_in_two(values):
    high = values.astype(jnp.bfloat16).astype(jnp.float32)
    return [high, values - high]


def partner(slot, chips):
    return slot and slot % (chips - 1) + 1


def rows_of(index, count):
    return pl.ds(pl.multiple_of(index * count, count), count)


def prepare_kernel(chips, me_ref, corr_ref, points_ref, turned_ref, *refs):
    turned = corr_ref[...].astype(jnp.float32).T
    turned_ref[...] = turned.astype(jnp.bfloat16)
    squares = jnp.sum(turned * turned, axis=0, keepdims=True)
    *sent_refs, packet_ref = refs
    packet_rows, terms = packet_ref.shape
    dim, runs = points_ref.shape
    rows = dim * runs // terms
    points = jnp.concatenate(
        [points_ref[start : start + rows, :] for start in range(0, dim, rows)], axis=1
    )
    pieces = split_in_two(points) + split_in_two(squares)
    used = 2 * rows + 2
    if packet_rows > used:
        pieces.append(jnp.zeros((packet_rows - used, terms), jnp.float32))
    packet_ref[...] = jnp.concatenate(pieces, axis=0).astype(jnp.bfloat16)
    fill_blocks(chips, me_ref, turned_ref, packet_ref, sent_refs)


def fill_blocks(chips, me_ref, turned_ref, packet_ref, sent_refs):
    count = turned_ref.shape[0] // chips
    for k, sent_ref in enumerate(sent_refs):
        chip = (me_ref[0] // CORES) ^ partner(k, chips)
        sent_ref[0:count, :] = turned_ref[rows_of(chip, count), :]
        sent_ref[count : sent_ref.shape[0], :] = packet_ref[...]


def hermite_columns(points):
    squared = points * points
    return jnp.concatenate(
        [
            jnp.ones_like(points),
            points,
            (squared - 1.0) / ROOT_TWO,
            points * (squared - 3.0) / ROOT_SIX,
            (squared * squared - 6.0 * squared + 3.0) / ROOT_TWENTYFOUR,
        ],
        axis=0,
    )


def collect_kernel(chips, *refs):
    packets_ref = refs[-1]
    rows = packets_ref.shape[1]
    for k, block_ref in enumerate(refs[:chips]):
        count = block_ref.shape[0]
        packets_ref[k] = block_ref[count - rows : count, :]


def choose_kernel(dim, chips, me_ref, codes_ref, *refs):
    chosen_ref, spots_ref = refs[-2:]
    matmuls, rows, terms = chosen_ref.shape
    half, tile = rows // 2, terms // chips
    row = lax.broadcasted_iota(jnp.int32, (half, tile), 0)
    for k in range(chips):
        device = me_ref[0] ^ (CORES * partner(k, chips))
        lanes = slice(k * tile, (k + 1) * tile)
        codes = codes_ref[:, rows_of(device, tile)]
        spots = (codes % DEGREES) * dim + codes // DEGREES
        spots_ref[:, lanes] = spots[matmuls:, :]
        for slot in range(matmuls):
            picked = jnp.where(row == spots[slot : slot + 1, :], 1.0, 0.0).astype(
                jnp.bfloat16
            )
            chosen_ref[slot, 0:half, lanes] = picked
            chosen_ref[slot, half:rows, lanes] = picked


def design_kernel(
    dim, run_count, packets_ref, chosen_ref, spots_ref, design_ref, exact, table
):
    chips, _, tile = packets_ref.shape
    half = exact.shape[1]
    rows = dim * run_count // tile
    terms = tile
    per = LANES // run_count
    for group in range(chips // per):
        owned = []
        for i in range(per):
            packet = packets_ref[group * per + i].astype(jnp.float32)
            owned.append(packet[0:rows, :] + packet[rows : 2 * rows, :])
        points = jnp.concatenate(
            [
                jnp.concatenate(
                    [inputs[:, start : start + run_count] for inputs in owned],
                    axis=1,
                )
                for start in range(0, terms, run_count)
            ],
            axis=0,
        )
        columns = hermite_columns(points)
        columns = jnp.concatenate(
            [
                columns,
                jnp.zeros((half - columns.shape[0], LANES), jnp.float32),
            ],
            axis=0,
        ).T
        high = columns.astype(jnp.bfloat16)
        low = (columns - high.astype(jnp.float32)).astype(jnp.bfloat16)
        block = slice(group * LANES, (group + 1) * LANES)
        exact[block, :] = columns
        table[block, 0:half] = high
        table[block, half : 2 * half] = low

    for start in range(0, table.shape[0], LANES):
        block = slice(start, start + LANES)
        values = exact[block, :]
        for first in range(0, design_ref.shape[1], tile):
            lanes = slice(first, first + tile)
            product = None
            for slot in range(chosen_ref.shape[0]):
                factor = jnp.dot(
                    table[block, :],
                    chosen_ref[slot, :, lanes],
                    preferred_element_type=jnp.float32,
                )
                product = factor if product is None else product * factor
            for part in range(0, tile, half):
                factor = product[:, part : part + half]
                lanes = slice(first + part, first + part + half)
                for slot in range(spots_ref.shape[0]):
                    spot = jnp.broadcast_to(
                        spots_ref[slot : slot + 1, lanes], values.shape
                    )
                    factor = factor * jnp.take_along_axis(values, spot, axis=1)
                design_ref[block, lanes] = factor.astype(jnp.bfloat16)


def shrink_factor(squares, limits):
    return jnp.maximum(0.0, 1.0 - limits / jnp.sqrt(squares + EPSILON))


def rows_and_weights(row, first, packets_ref, levels_ref):
    squares, levels = [], []
    for k in range(packets_ref.shape[0]):
        packet = packets_ref[k].astype(jnp.float32)
        squares.append(packet[row : row + 1, :] + packet[row + 1 : row + 2, :])
        device = first ^ (CORES * partner(k, packets_ref.shape[0]))
        levels.append(levels_ref[:, rows_of(device, packets_ref.shape[2])])
    weights = jnp.exp2(jnp.concatenate(levels, axis=1).astype(jnp.float32))
    return jnp.concatenate(squares, axis=1), weights


def fit_kernel(row, me_ref, levels_ref, own_ref, other_ref, *refs):
    *refs, fitted_ref, scale_ref, first_ref = refs
    block_refs, design_refs = refs[:-CORES], refs[-CORES:]
    count = fitted_ref.shape[0]
    term_count = own_ref.shape[2]
    me = me_ref[0]
    squares, weights = rows_and_weights(row, me, own_ref, levels_ref)
    others, other_weights = rows_and_weights(row, me ^ 1, other_ref, levels_ref)
    ratio = jnp.maximum(
        jnp.max(jnp.sqrt(squares) / weights, axis=1, keepdims=True),
        jnp.max(jnp.sqrt(others) / other_weights, axis=1, keepdims=True),
    )
    limits = STEP * (LAMBDA_FRACTION * ratio) * weights
    factor = shrink_factor(STEP * STEP * squares, limits)
    scale_ref[0:1, :] = factor[:, 0:term_count]
    scale_ref[1:2, :] = limits[:, 0:term_count]
    for k, block_ref in enumerate(block_refs):
        terms = slice(k * term_count, (k + 1) * term_count)
        first = STEP * block_ref[0:count, :].astype(jnp.float32) * factor[:, terms]
        first_ref[:, terms] = first.astype(jnp.bfloat16)
    runs = design_refs[0].shape[0]
    for i, design_ref in enumerate(design_refs):
        fitted_ref[:, i * runs : (i + 1) * runs] = lax.dot_general(
            first_ref[...],
            design_ref[...],
            (((1,), (1,)), ((), ())),
            preferred_element_type=jnp.float32,
        )


def sum_kernel(total_runs, chips, own_ref, other_ref, *refs):
    design_refs = refs[:CORES]
    summed_refs = refs[len(refs) - chips :]
    runs = design_refs[0].shape[0]
    near = own_ref[:, 0:runs] + other_ref[:, runs : 2 * runs]
    far = own_ref[:, runs : 2 * runs] + other_ref[:, 0:runs]
    near, far = near.astype(jnp.bfloat16), far.astype(jnp.bfloat16)
    term_count = summed_refs[0].shape[1]
    for k, summed_ref in enumerate(summed_refs):
        terms = slice(k * term_count, (k + 1) * term_count)
        summed = jnp.dot(
            near, design_refs[0][:, terms], preferred_element_type=jnp.float32
        ) + jnp.dot(far, design_refs[1][:, terms], preferred_element_type=jnp.float32)
        summed_ref[...] = (summed / total_runs).astype(jnp.bfloat16)


def reorder_kernel(map_ref, slab_ref, *refs):
    modes_ref = refs[-1]
    cells, block = slab_ref.shape[0], modes_ref.shape[0]
    row = lax.broadcasted_iota(jnp.int32, (cells, block), 0)
    chosen = jnp.where(row == map_ref[...], 1.0, 0.0).astype(jnp.bfloat16)
    modes_ref[...] = lax.dot_general(
        chosen,
        slab_ref[...],
        (((0,), (0,)), ((), ())),
        preferred_element_type=jnp.float32,
    ).astype(jnp.bfloat16)


def finish_kernel(pieces, me_ref, corr_ref, scale_ref, *refs):
    modes_refs, refs = refs[:pieces], refs[pieces:]
    *summed_refs, out_ref, lifted_ref, moved, values, half, lifted, out_sem, sems = refs
    modes, terms = corr_ref.shape
    count = summed_refs[0].shape[0]
    squares = jnp.zeros((1, terms), jnp.float32)
    for k, summed_ref in enumerate(summed_refs):
        rows = rows_of((me_ref[0] // CORES) ^ partner(k, len(summed_refs)), count)
        corr = corr_ref[rows, :].astype(jnp.float32)
        first = STEP * corr * scale_ref[0:1, :]
        gradient = summed_ref[...].astype(jnp.float32) - corr
        step = first - STEP * gradient
        moved[rows, :] = step
        squares = squares + jnp.sum(step * step, axis=0, keepdims=True)
    factor = shrink_factor(squares, scale_ref[1:2, :])
    for start in range(0, modes, LANES):
        block = slice(start, start + LANES)
        turned = (moved[block, :] * factor).T
        values[:, block] = turned
        half[:, block] = turned.astype(jnp.bfloat16)
    copies = [pltpu.make_async_copy(values, out_ref, out_sem)]
    copies[0].start()
    width = lifted.shape[2]
    for i, modes_ref in enumerate(modes_refs):
        block = slice(i * width, (i + 1) * width)
        lifted[i] = lax.dot_general(
            half[...],
            modes_ref[...],
            (((1,), (1,)), ((), ())),
            preferred_element_type=jnp.float32,
        ).astype(jnp.bfloat16)
        copies.append(
            pltpu.make_async_copy(lifted.at[i], lifted_ref.at[:, block], sems.at[i])
        )
        copies[-1].start()
    for copy in copies:
        copy.wait()


def in_hbm(array):
    return pltpu.with_memory_space_constraint(array, pltpu.HBM)


def params(limit):
    return pltpu.CompilerParams(vmem_limit_bytes=limit * MIB)


def cost(flops, moved):
    return pl.CostEstimate(flops=flops, bytes_accessed=moved, transcendentals=0)


def to_device(array, bits):
    devices = lax.axis_size("runs")
    return lax.ppermute(array, "runs", [(i, i ^ bits) for i in range(devices)])


def to_chips(arrays):
    chips = len(arrays)
    return [arrays[0]] + [
        to_device(arrays[k], CORES * partner(k, chips)) for k in range(1, chips)
    ]


def split_by_modes(
    run_inputs, term_codes, weight_levels, correlations, slab_modes, cell_map
):
    run_count, dim = run_inputs.shape
    term_count, modes = correlations.shape
    terms, slots = term_codes.shape
    cells = slab_modes.shape[0]
    slab_cells = cell_map.shape[0]
    chips = lax.axis_size("runs") // CORES
    total_runs = run_count * CORES * chips
    core_terms = terms // CORES
    own_modes = modes // chips
    rows = dim * run_count // term_count
    packet_rows = round_up(2 * rows + 2, 16)
    me = lax.axis_index("runs").astype(jnp.int32).reshape(1)
    smem = pl.BlockSpec(memory_space=pltpu.SMEM)
    vmem = pl.BlockSpec(memory_space=pltpu.VMEM)
    anywhere = pl.BlockSpec(memory_space=pl.ANY)

    block_type = jax.ShapeDtypeStruct((own_modes + packet_rows, term_count), jnp.bfloat16)
    turned, *sent = pl.pallas_call(
        functools.partial(prepare_kernel, chips),
        in_specs=[smem, vmem, vmem],
        out_specs=[vmem] * (1 + chips),
        out_shape=[jax.ShapeDtypeStruct((modes, term_count), jnp.bfloat16)]
        + [block_type] * chips,
        scratch_shapes=[pltpu.VMEM((packet_rows, term_count), jnp.bfloat16)],
        compiler_params=params(16),
        name="prepare",
    )(me, in_hbm(correlations), in_hbm(run_inputs.T))

    block = math.gcd(512, slab_cells)

    def reorder(start, *after):
        return pl.pallas_call(
            reorder_kernel,
            in_specs=[vmem, vmem] + [anywhere] * len(after),
            out_specs=vmem,
            out_shape=jax.ShapeDtypeStruct((block, modes), jnp.bfloat16),
            compiler_params=params(16),
            cost_estimate=cost(2 * cells * block * modes, 2 * cells * modes),
            name="reorder",
        )(cell_map[None, start : start + block], slab_modes, *after)

    starts = range(0, slab_cells, block)
    quarters = [starts[i * len(starts) // 4 : (i + 1) * len(starts) // 4] for i in range(4)]
    blocks = to_chips(sent)
    half = round_up(DEGREES * dim, LANES)
    gathers = slots // 4
    chosen, spots = pl.pallas_call(
        functools.partial(choose_kernel, dim, chips),
        in_specs=[smem, vmem] + [anywhere] * len(blocks[1:3]),
        out_specs=[vmem, vmem],
        out_shape=[
            jax.ShapeDtypeStruct((slots - gathers, 2 * half, core_terms), jnp.bfloat16),
            jax.ShapeDtypeStruct((gathers, core_terms), jnp.int32),
        ],
        compiler_params=params(8),
        cost_estimate=cost(0, 2 * slots * half * core_terms),
        name="choose",
    )(me, in_hbm(term_codes.T), *blocks[1:3])
    ordered = [
        reorder(start, *blocks[1:3]) for start in [*quarters[0], *quarters[1]]
    ]
    packets = pl.pallas_call(
        functools.partial(collect_kernel, chips),
        in_specs=[vmem] * chips + [anywhere] * (1 + len(ordered)),
        out_specs=vmem,
        out_shape=jax.ShapeDtypeStruct((chips, packet_rows, term_count), jnp.bfloat16),
        compiler_params=params(8),
        name="collect",
    )(*blocks, spots, *ordered)
    others = to_device(packets, 1)

    core_runs = run_count * chips

    def design_of(packets):
        return pl.pallas_call(
            functools.partial(design_kernel, dim, run_count),
            in_specs=[vmem] * 3,
            out_specs=vmem,
            out_shape=jax.ShapeDtypeStruct((core_runs, core_terms), jnp.bfloat16),
            scratch_shapes=[
                pltpu.VMEM((core_runs, half), jnp.float32),
                pltpu.VMEM((core_runs, 2 * half), jnp.bfloat16),
            ],
            compiler_params=params(16),
            cost_estimate=cost(
                4 * core_runs * core_terms * slots * half, 2 * core_runs * core_terms
            ),
            name="design",
        )(packets, chosen, spots)

    designs = [design_of(packets), design_of(others)]

    fit_cost = cost(
        2 * total_runs * core_terms * own_modes, 2 * total_runs * core_terms
    )
    fitted, scale = pl.pallas_call(
        functools.partial(fit_kernel, 2 * rows),
        in_specs=[smem] + [vmem] * (3 + chips + CORES),
        out_specs=[vmem, vmem],
        out_shape=[
            jax.ShapeDtypeStruct((own_modes, total_runs), jnp.float32),
            jax.ShapeDtypeStruct((8, term_count), jnp.float32),
        ],
        scratch_shapes=[pltpu.VMEM((own_modes, core_terms), jnp.bfloat16)],
        compiler_params=params(16),
        cost_estimate=fit_cost,
        name="fit",
    )(me, weight_levels[None, :], packets, others, *blocks, *designs)
    beside = [reorder(start, fitted) for start in quarters[2]]
    summed = pl.pallas_call(
        functools.partial(sum_kernel, float(total_runs), chips),
        in_specs=[vmem] * (2 + CORES) + [anywhere] * len(beside),
        out_specs=[vmem] * chips,
        out_shape=[jax.ShapeDtypeStruct((own_modes, term_count), jnp.bfloat16)] * chips,
        compiler_params=params(16),
        cost_estimate=fit_cost,
        name="sum",
    )(fitted, to_device(fitted, 1), *designs, *beside)
    returned = to_chips(summed)
    ordered += beside
    ordered += [reorder(start, summed[0]) for start in quarters[3]]

    return pl.pallas_call(
        functools.partial(finish_kernel, len(ordered)),
        in_specs=[smem] + [vmem] * (2 + len(ordered) + chips),
        out_specs=(anywhere, anywhere),
        out_shape=(
            jax.ShapeDtypeStruct((term_count, modes), jnp.float32),
            jax.ShapeDtypeStruct((term_count, slab_cells), jnp.bfloat16),
        ),
        scratch_shapes=[
            pltpu.VMEM((modes, term_count), jnp.float32),
            pltpu.VMEM((term_count, modes), jnp.float32),
            pltpu.VMEM((term_count, modes), jnp.bfloat16),
            pltpu.VMEM((len(ordered), term_count, block), jnp.bfloat16),
            pltpu.SemaphoreType.DMA,
            pltpu.SemaphoreType.DMA((len(ordered),)),
        ],
        compiler_params=params(20),
        name="finish",
    )(me, turned, scale, *ordered, *returned)


def hermite_table(points):
    squared = points * points
    columns = [
        jnp.ones_like(points),
        points,
        (squared - 1.0) / ROOT_TWO,
        points * (squared - 3.0) / ROOT_SIX,
        (squared * squared - 6.0 * squared + 3.0) / ROOT_TWENTYFOUR,
    ]
    return jnp.stack(columns, axis=-1).reshape(points.shape[0], -1)


def basis(points, codes):
    hermite = hermite_table(points)
    product = jnp.take(hermite, codes[:, 0], axis=1)
    for column in range(1, codes.shape[1]):
        product = product * jnp.take(hermite, codes[:, column], axis=1)
    return product.astype(jnp.bfloat16)


def shrink(values, limits):
    length = jnp.sqrt(jnp.sum(values * values, axis=1, keepdims=True) + EPSILON)
    return values * jnp.maximum(0.0, 1.0 - limits[:, None] / length)


def transposed_product(left, right):
    return lax.dot_general(
        left, right, (((0,), (0,)), ((), ())), preferred_element_type=jnp.float32
    )


def split_by_runs(
    run_inputs, term_codes, weight_levels, correlations, slab_modes, cell_map
):
    run_count = run_inputs.shape[0]
    term_count = correlations.shape[0]
    devices = lax.axis_size("runs")
    offset = lax.axis_index("runs") * term_count
    total_runs = run_count * devices
    weights_all = jnp.exp2(weight_levels.astype(jnp.float32))
    own_weights = lax.dynamic_slice_in_dim(weights_all, offset, term_count)
    own_corr = correlations.astype(jnp.float32)
    ratio = jnp.max(jnp.sqrt(jnp.sum(own_corr * own_corr, axis=1)) / own_weights)
    penalty = LAMBDA_FRACTION * lax.pmax(ratio, "runs")
    first = shrink(STEP * own_corr, STEP * penalty * own_weights)
    design = basis(run_inputs, term_codes)
    fitted = jnp.dot(
        design,
        lax.all_gather(first.astype(jnp.bfloat16), "runs", axis=0, tiled=True),
        preferred_element_type=jnp.float32,
    )
    fitted_half = fitted.astype(jnp.bfloat16)
    all_points = lax.all_gather(run_inputs, "runs", axis=0, tiled=True)
    own_codes = lax.dynamic_slice_in_dim(term_codes, offset, term_count, 0)
    owned_design = basis(all_points, own_codes)
    summed = transposed_product(
        owned_design, lax.all_gather(fitted_half, "runs", axis=0, tiled=True)
    )
    gradient = summed / total_runs - own_corr
    coefficients = shrink(first - STEP * gradient, STEP * penalty * own_weights)
    modes = jnp.take(slab_modes, cell_map, axis=0)
    lifted = lax.dot_general(
        coefficients.astype(jnp.bfloat16),
        modes,
        (((1,), (1,)), ((), ())),
        preferred_element_type=jnp.float32,
    ).astype(jnp.bfloat16)
    return (coefficients, lifted)


def on_device(
    run_inputs, term_codes, weight_levels, correlations, slab_modes, cell_map
):
    devices = lax.axis_size("runs")
    run_count = run_inputs.shape[0]
    term_count, modes = correlations.shape
    chips = max(1, devices // CORES)
    whole_tiles = (
        devices >= CORES
        and devices & (devices - 1) == 0
        and modes % (LANES * chips) == 0
        and term_count % LANES == 0
        and DEGREES * run_inputs.shape[1] <= LANES
        and LANES % run_count == 0
        and chips % (LANES // run_count) == 0
        and term_count % run_count == 0
        and run_inputs.shape[1] % (term_count // run_count) == 0
        and slab_modes.shape[0] % LANES == 0
        and cell_map.shape[0] % LANES == 0
    )
    plan = split_by_modes if whole_tiles else split_by_runs
    return plan(
        run_inputs, term_codes, weight_levels, correlations, slab_modes, cell_map
    )


def solution(mesh):
    return jax.shard_map(
        on_device,
        mesh=mesh,
        in_specs=(
            P(("cases", "runs"), None),
            P(),
            P(),
            P(("cases", "runs"), None),
            P("cases", None),
            P(),
        ),
        out_specs=(P(("cases", "runs"), None), P(("cases", "runs"), None)),
        check_vma=False,
    )
```

```python
import functools
import math

import jax
import jax.numpy as jnp
from jax import lax
from jax.experimental import pallas as pl
from jax.experimental.pallas import tpu as pltpu
from jax.sharding import PartitionSpec as P

STEP = 0.5
LAMBDA_FRACTION = 0.05
EPSILON = 1e-06
DEGREES = 5
LANES = 128
CORES = 2
ROOT_TWO = math.sqrt(2.0)
ROOT_SIX = math.sqrt(6.0)
ROOT_TWENTYFOUR = math.sqrt(24.0)
MIB = 1 << 20


def round_up(value, multiple):
    return -(-value // multiple) * multiple


def split_in_two(values):
    high = values.astype(jnp.bfloat16).astype(jnp.float32)
    return [high, values - high]


def partner(slot, chips):
    return slot and slot % (chips - 1) + 1


def rows_of(index, count):
    return pl.ds(pl.multiple_of(index * count, count), count)


def prepare_kernel(chips, me_ref, corr_ref, points_ref, turned_ref, *refs):
    turned = corr_ref[...].astype(jnp.float32).T
    turned_ref[...] = turned.astype(jnp.bfloat16)
    squares = jnp.sum(turned * turned, axis=0, keepdims=True)
    *sent_refs, packet_ref = refs
    packet_rows, terms = packet_ref.shape
    dim, runs = points_ref.shape
    rows = dim * runs // terms
    points = jnp.concatenate(
        [points_ref[start : start + rows, :] for start in range(0, dim, rows)], axis=1
    )
    pieces = split_in_two(points) + split_in_two(squares)
    used = 2 * rows + 2
    if packet_rows > used:
        pieces.append(jnp.zeros((packet_rows - used, terms), jnp.float32))
    packet_ref[...] = jnp.concatenate(pieces, axis=0).astype(jnp.bfloat16)
    fill_blocks(chips, me_ref, turned_ref, packet_ref, sent_refs)


def fill_blocks(chips, me_ref, turned_ref, packet_ref, sent_refs):
    count = turned_ref.shape[0] // chips
    for k, sent_ref in enumerate(sent_refs):
        chip = (me_ref[0] // CORES) ^ partner(k, chips)
        sent_ref[0:count, :] = turned_ref[rows_of(chip, count), :]
        sent_ref[count : sent_ref.shape[0], :] = packet_ref[...]


def hermite_columns(points):
    squared = points * points
    return jnp.concatenate(
        [
            jnp.ones_like(points),
            points,
            (squared - 1.0) / ROOT_TWO,
            points * (squared - 3.0) / ROOT_SIX,
            (squared * squared - 6.0 * squared + 3.0) / ROOT_TWENTYFOUR,
        ],
        axis=0,
    )


def collect_kernel(chips, *refs):
    packets_ref = refs[-1]
    rows = packets_ref.shape[1]
    for k, block_ref in enumerate(refs[:chips]):
        count = block_ref.shape[0]
        packets_ref[k] = block_ref[count - rows : count, :]


def choose_kernel(dim, chips, me_ref, codes_ref, *refs):
    chosen_ref, spots_ref = refs[-2:]
    matmuls, rows, terms = chosen_ref.shape
    half, tile = rows // 2, terms // chips
    row = lax.broadcasted_iota(jnp.int32, (half, tile), 0)
    for k in range(chips):
        device = me_ref[0] ^ (CORES * partner(k, chips))
        lanes = slice(k * tile, (k + 1) * tile)
        codes = codes_ref[:, rows_of(device, tile)]
        spots = (codes % DEGREES) * dim + codes // DEGREES
        spots_ref[:, lanes] = spots[matmuls:, :]
        for slot in range(matmuls):
            picked = jnp.where(row == spots[slot : slot + 1, :], 1.0, 0.0).astype(
                jnp.bfloat16
            )
            chosen_ref[slot, 0:half, lanes] = picked
            chosen_ref[slot, half:rows, lanes] = picked


def design_kernel(
    dim, run_count, packets_ref, chosen_ref, spots_ref, design_ref, exact, table
):
    chips, _, tile = packets_ref.shape
    half = exact.shape[1]
    rows = dim * run_count // tile
    terms = tile
    per = LANES // run_count
    for group in range(chips // per):
        owned = []
        for i in range(per):
            packet = packets_ref[group * per + i].astype(jnp.float32)
            owned.append(packet[0:rows, :] + packet[rows : 2 * rows, :])
        points = jnp.concatenate(
            [
                jnp.concatenate(
                    [inputs[:, start : start + run_count] for inputs in owned],
                    axis=1,
                )
                for start in range(0, terms, run_count)
            ],
            axis=0,
        )
        columns = hermite_columns(points)
        columns = jnp.concatenate(
            [
                columns,
                jnp.zeros((half - columns.shape[0], LANES), jnp.float32),
            ],
            axis=0,
        ).T
        high = columns.astype(jnp.bfloat16)
        low = (columns - high.astype(jnp.float32)).astype(jnp.bfloat16)
        block = slice(group * LANES, (group + 1) * LANES)
        exact[block, :] = columns
        table[block, 0:half] = high
        table[block, half : 2 * half] = low

    for start in range(0, table.shape[0], LANES):
        block = slice(start, start + LANES)
        values = exact[block, :]
        for first in range(0, design_ref.shape[1], tile):
            lanes = slice(first, first + tile)
            product = None
            for slot in range(chosen_ref.shape[0]):
                factor = jnp.dot(
                    table[block, :],
                    chosen_ref[slot, :, lanes],
                    preferred_element_type=jnp.float32,
                )
                product = factor if product is None else product * factor
            for part in range(0, tile, half):
                factor = product[:, part : part + half]
                lanes = slice(first + part, first + part + half)
                for slot in range(spots_ref.shape[0]):
                    spot = jnp.broadcast_to(
                        spots_ref[slot : slot + 1, lanes], values.shape
                    )
                    factor = factor * jnp.take_along_axis(values, spot, axis=1)
                design_ref[block, lanes] = factor.astype(jnp.bfloat16)


def shrink_factor(squares, limits):
    return jnp.maximum(0.0, 1.0 - limits / jnp.sqrt(squares + EPSILON))


def rows_and_weights(row, first, packets_ref, levels_ref):
    squares, levels = [], []
    for k in range(packets_ref.shape[0]):
        packet = packets_ref[k].astype(jnp.float32)
        squares.append(packet[row : row + 1, :] + packet[row + 1 : row + 2, :])
        device = first ^ (CORES * partner(k, packets_ref.shape[0]))
        levels.append(levels_ref[:, rows_of(device, packets_ref.shape[2])])
    weights = jnp.exp2(jnp.concatenate(levels, axis=1).astype(jnp.float32))
    return jnp.concatenate(squares, axis=1), weights


def fit_kernel(row, me_ref, levels_ref, own_ref, other_ref, *refs):
    *refs, fitted_ref, scale_ref, first_ref = refs
    block_refs, design_refs = refs[:-CORES], refs[-CORES:]
    count = fitted_ref.shape[0]
    term_count = own_ref.shape[2]
    me = me_ref[0]
    squares, weights = rows_and_weights(row, me, own_ref, levels_ref)
    others, other_weights = rows_and_weights(row, me ^ 1, other_ref, levels_ref)
    ratio = jnp.maximum(
        jnp.max(jnp.sqrt(squares) / weights, axis=1, keepdims=True),
        jnp.max(jnp.sqrt(others) / other_weights, axis=1, keepdims=True),
    )
    limits = STEP * (LAMBDA_FRACTION * ratio) * weights
    factor = shrink_factor(STEP * STEP * squares, limits)
    scale_ref[0:1, :] = factor[:, 0:term_count]
    scale_ref[1:2, :] = limits[:, 0:term_count]
    for k, block_ref in enumerate(block_refs):
        terms = slice(k * term_count, (k + 1) * term_count)
        first = STEP * block_ref[0:count, :].astype(jnp.float32) * factor[:, terms]
        first_ref[:, terms] = first.astype(jnp.bfloat16)
    runs = design_refs[0].shape[0]
    for i, design_ref in enumerate(design_refs):
        fitted_ref[:, i * runs : (i + 1) * runs] = lax.dot_general(
            first_ref[...],
            design_ref[...],
            (((1,), (1,)), ((), ())),
            preferred_element_type=jnp.float32,
        )


def sum_kernel(total_runs, chips, own_ref, other_ref, *refs):
    design_refs = refs[:CORES]
    summed_refs = refs[len(refs) - chips :]
    runs = design_refs[0].shape[0]
    near = own_ref[:, 0:runs] + other_ref[:, runs : 2 * runs]
    far = own_ref[:, runs : 2 * runs] + other_ref[:, 0:runs]
    near, far = near.astype(jnp.bfloat16), far.astype(jnp.bfloat16)
    term_count = summed_refs[0].shape[1]
    for k, summed_ref in enumerate(summed_refs):
        terms = slice(k * term_count, (k + 1) * term_count)
        summed = jnp.dot(
            near, design_refs[0][:, terms], preferred_element_type=jnp.float32
        ) + jnp.dot(far, design_refs[1][:, terms], preferred_element_type=jnp.float32)
        summed_ref[...] = (summed / total_runs).astype(jnp.bfloat16)


def reorder_kernel(map_ref, slab_ref, *refs):
    modes_ref = refs[-1]
    cells, block = slab_ref.shape[0], modes_ref.shape[0]
    row = lax.broadcasted_iota(jnp.int32, (cells, block), 0)
    chosen = jnp.where(row == map_ref[...], 1.0, 0.0).astype(jnp.bfloat16)
    modes_ref[...] = lax.dot_general(
        chosen,
        slab_ref[...],
        (((0,), (0,)), ((), ())),
        preferred_element_type=jnp.float32,
    ).astype(jnp.bfloat16)


def finish_kernel(pieces, me_ref, corr_ref, scale_ref, *refs):
    modes_refs, refs = refs[:pieces], refs[pieces:]
    *summed_refs, out_ref, lifted_ref, moved, values, half, lifted, out_sem, sems = refs
    modes, terms = corr_ref.shape
    count = summed_refs[0].shape[0]
    squares = jnp.zeros((1, terms), jnp.float32)
    for k, summed_ref in enumerate(summed_refs):
        rows = rows_of((me_ref[0] // CORES) ^ partner(k, len(summed_refs)), count)
        corr = corr_ref[rows, :].astype(jnp.float32)
        first = STEP * corr * scale_ref[0:1, :]
        gradient = summed_ref[...].astype(jnp.float32) - corr
        step = first - STEP * gradient
        moved[rows, :] = step
        squares = squares + jnp.sum(step * step, axis=0, keepdims=True)
    factor = shrink_factor(squares, scale_ref[1:2, :])
    for start in range(0, modes, LANES):
        block = slice(start, start + LANES)
        turned = (moved[block, :] * factor).T
        values[:, block] = turned
        half[:, block] = turned.astype(jnp.bfloat16)
    copies = [pltpu.make_async_copy(values, out_ref, out_sem)]
    copies[0].start()
    width = lifted.shape[2]
    for i, modes_ref in enumerate(modes_refs):
        block = slice(i * width, (i + 1) * width)
        lifted[i] = lax.dot_general(
            half[...],
            modes_ref[...],
            (((1,), (1,)), ((), ())),
            preferred_element_type=jnp.float32,
        ).astype(jnp.bfloat16)
        copies.append(
            pltpu.make_async_copy(lifted.at[i], lifted_ref.at[:, block], sems.at[i])
        )
        copies[-1].start()
    for copy in copies:
        copy.wait()


def in_hbm(array):
    return pltpu.with_memory_space_constraint(array, pltpu.HBM)


def params(limit):
    return pltpu.CompilerParams(vmem_limit_bytes=limit * MIB)


def cost(flops, moved):
    return pl.CostEstimate(flops=flops, bytes_accessed=moved, transcendentals=0)


def to_device(array, bits):
    devices = lax.axis_size("runs")
    return lax.ppermute(array, "runs", [(i, i ^ bits) for i in range(devices)])


def to_chips(arrays):
    chips = len(arrays)
    return [arrays[0]] + [
        to_device(arrays[k], CORES * partner(k, chips)) for k in range(1, chips)
    ]


def split_by_modes(
    run_inputs, term_codes, weight_levels, correlations, slab_modes, cell_map
):
    run_count, dim = run_inputs.shape
    term_count, modes = correlations.shape
    terms, slots = term_codes.shape
    cells = slab_modes.shape[0]
    slab_cells = cell_map.shape[0]
    chips = lax.axis_size("runs") // CORES
    total_runs = run_count * CORES * chips
    core_terms = terms // CORES
    own_modes = modes // chips
    rows = dim * run_count // term_count
    packet_rows = round_up(2 * rows + 2, 16)
    me = lax.axis_index("runs").astype(jnp.int32).reshape(1)
    smem = pl.BlockSpec(memory_space=pltpu.SMEM)
    vmem = pl.BlockSpec(memory_space=pltpu.VMEM)
    anywhere = pl.BlockSpec(memory_space=pl.ANY)

    block_type = jax.ShapeDtypeStruct((own_modes + packet_rows, term_count), jnp.bfloat16)
    turned, *sent = pl.pallas_call(
        functools.partial(prepare_kernel, chips),
        in_specs=[smem, vmem, vmem],
        out_specs=[vmem] * (1 + chips),
        out_shape=[jax.ShapeDtypeStruct((modes, term_count), jnp.bfloat16)]
        + [block_type] * chips,
        scratch_shapes=[pltpu.VMEM((packet_rows, term_count), jnp.bfloat16)],
        compiler_params=params(16),
        name="prepare",
    )(me, in_hbm(correlations), in_hbm(run_inputs.T))

    block = math.gcd(512, slab_cells)

    def reorder(start, *after):
        return pl.pallas_call(
            reorder_kernel,
            in_specs=[vmem, vmem] + [anywhere] * len(after),
            out_specs=vmem,
            out_shape=jax.ShapeDtypeStruct((block, modes), jnp.bfloat16),
            compiler_params=params(16),
            cost_estimate=cost(2 * cells * block * modes, 2 * cells * modes),
            name="reorder",
        )(cell_map[None, start : start + block], slab_modes, *after)

    starts = range(0, slab_cells, block)
    quarters = [starts[i * len(starts) // 4 : (i + 1) * len(starts) // 4] for i in range(4)]
    blocks = to_chips(sent)
    half = round_up(DEGREES * dim, LANES)
    gathers = slots // 4
    chosen, spots = pl.pallas_call(
        functools.partial(choose_kernel, dim, chips),
        in_specs=[smem, vmem] + [anywhere] * len(blocks[1:3]),
        out_specs=[vmem, vmem],
        out_shape=[
            jax.ShapeDtypeStruct((slots - gathers, 2 * half, core_terms), jnp.bfloat16),
            jax.ShapeDtypeStruct((gathers, core_terms), jnp.int32),
        ],
        compiler_params=params(8),
        cost_estimate=cost(0, 2 * slots * half * core_terms),
        name="choose",
    )(me, in_hbm(term_codes.T), *blocks[1:3])
    ordered = [
        reorder(start, *blocks[1:3]) for start in quarters[0]
    ]
    packets = pl.pallas_call(
        functools.partial(collect_kernel, chips),
        in_specs=[vmem] * chips + [anywhere] * (1 + len(ordered)),
        out_specs=vmem,
        out_shape=jax.ShapeDtypeStruct((chips, packet_rows, term_count), jnp.bfloat16),
        compiler_params=params(8),
        name="collect",
    )(*blocks, spots, *ordered)
    others = to_device(packets, 1)

    core_runs = run_count * chips

    def design_of(packets):
        return pl.pallas_call(
            functools.partial(design_kernel, dim, run_count),
            in_specs=[vmem] * 3,
            out_specs=vmem,
            out_shape=jax.ShapeDtypeStruct((core_runs, core_terms), jnp.bfloat16),
            scratch_shapes=[
                pltpu.VMEM((core_runs, half), jnp.float32),
                pltpu.VMEM((core_runs, 2 * half), jnp.bfloat16),
            ],
            compiler_params=params(16),
            cost_estimate=cost(
                4 * core_runs * core_terms * slots * half, 2 * core_runs * core_terms
            ),
            name="design",
        )(packets, chosen, spots)

    designs = [design_of(packets), design_of(others)]

    fit_cost = cost(
        2 * total_runs * core_terms * own_modes, 2 * total_runs * core_terms
    )
    fitted, scale = pl.pallas_call(
        functools.partial(fit_kernel, 2 * rows),
        in_specs=[smem] + [vmem] * (3 + chips + CORES),
        out_specs=[vmem, vmem],
        out_shape=[
            jax.ShapeDtypeStruct((own_modes, total_runs), jnp.float32),
            jax.ShapeDtypeStruct((8, term_count), jnp.float32),
        ],
        scratch_shapes=[pltpu.VMEM((own_modes, core_terms), jnp.bfloat16)],
        compiler_params=params(16),
        cost_estimate=fit_cost,
        name="fit",
    )(me, weight_levels[None, :], packets, others, *blocks, *designs)
    beside = [reorder(start, fitted) for start in quarters[1]]
    summed = pl.pallas_call(
        functools.partial(sum_kernel, float(total_runs), chips),
        in_specs=[vmem] * (2 + CORES) + [anywhere] * len(beside),
        out_specs=[vmem] * chips,
        out_shape=[jax.ShapeDtypeStruct((own_modes, term_count), jnp.bfloat16)] * chips,
        compiler_params=params(16),
        cost_estimate=fit_cost,
        name="sum",
    )(fitted, to_device(fitted, 1), *designs, *beside)
    returned = to_chips(summed)
    ordered += beside
    ordered += [
        reorder(start, *returned[1:3]) for start in [*quarters[2], *quarters[3]]
    ]

    return pl.pallas_call(
        functools.partial(finish_kernel, len(ordered)),
        in_specs=[smem] + [vmem] * (2 + len(ordered) + chips),
        out_specs=(anywhere, anywhere),
        out_shape=(
            jax.ShapeDtypeStruct((term_count, modes), jnp.float32),
            jax.ShapeDtypeStruct((term_count, slab_cells), jnp.bfloat16),
        ),
        scratch_shapes=[
            pltpu.VMEM((modes, term_count), jnp.float32),
            pltpu.VMEM((term_count, modes), jnp.float32),
            pltpu.VMEM((term_count, modes), jnp.bfloat16),
            pltpu.VMEM((len(ordered), term_count, block), jnp.bfloat16),
            pltpu.SemaphoreType.DMA,
            pltpu.SemaphoreType.DMA((len(ordered),)),
        ],
        compiler_params=params(20),
        name="finish",
    )(me, turned, scale, *ordered, *returned)


def hermite_table(points):
    squared = points * points
    columns = [
        jnp.ones_like(points),
        points,
        (squared - 1.0) / ROOT_TWO,
        points * (squared - 3.0) / ROOT_SIX,
        (squared * squared - 6.0 * squared + 3.0) / ROOT_TWENTYFOUR,
    ]
    return jnp.stack(columns, axis=-1).reshape(points.shape[0], -1)


def basis(points, codes):
    hermite = hermite_table(points)
    product = jnp.take(hermite, codes[:, 0], axis=1)
    for column in range(1, codes.shape[1]):
        product = product * jnp.take(hermite, codes[:, column], axis=1)
    return product.astype(jnp.bfloat16)


def shrink(values, limits):
    length = jnp.sqrt(jnp.sum(values * values, axis=1, keepdims=True) + EPSILON)
    return values * jnp.maximum(0.0, 1.0 - limits[:, None] / length)


def transposed_product(left, right):
    return lax.dot_general(
        left, right, (((0,), (0,)), ((), ())), preferred_element_type=jnp.float32
    )


def split_by_runs(
    run_inputs, term_codes, weight_levels, correlations, slab_modes, cell_map
):
    run_count = run_inputs.shape[0]
    term_count = correlations.shape[0]
    devices = lax.axis_size("runs")
    offset = lax.axis_index("runs") * term_count
    total_runs = run_count * devices
    weights_all = jnp.exp2(weight_levels.astype(jnp.float32))
    own_weights = lax.dynamic_slice_in_dim(weights_all, offset, term_count)
    own_corr = correlations.astype(jnp.float32)
    ratio = jnp.max(jnp.sqrt(jnp.sum(own_corr * own_corr, axis=1)) / own_weights)
    penalty = LAMBDA_FRACTION * lax.pmax(ratio, "runs")
    first = shrink(STEP * own_corr, STEP * penalty * own_weights)
    design = basis(run_inputs, term_codes)
    fitted = jnp.dot(
        design,
        lax.all_gather(first.astype(jnp.bfloat16), "runs", axis=0, tiled=True),
        preferred_element_type=jnp.float32,
    )
    fitted_half = fitted.astype(jnp.bfloat16)
    all_points = lax.all_gather(run_inputs, "runs", axis=0, tiled=True)
    own_codes = lax.dynamic_slice_in_dim(term_codes, offset, term_count, 0)
    owned_design = basis(all_points, own_codes)
    summed = transposed_product(
        owned_design, lax.all_gather(fitted_half, "runs", axis=0, tiled=True)
    )
    gradient = summed / total_runs - own_corr
    coefficients = shrink(first - STEP * gradient, STEP * penalty * own_weights)
    modes = jnp.take(slab_modes, cell_map, axis=0)
    lifted = lax.dot_general(
        coefficients.astype(jnp.bfloat16),
        modes,
        (((1,), (1,)), ((), ())),
        preferred_element_type=jnp.float32,
    ).astype(jnp.bfloat16)
    return (coefficients, lifted)


def on_device(
    run_inputs, term_codes, weight_levels, correlations, slab_modes, cell_map
):
    devices = lax.axis_size("runs")
    run_count = run_inputs.shape[0]
    term_count, modes = correlations.shape
    chips = max(1, devices // CORES)
    whole_tiles = (
        devices >= CORES
        and devices & (devices - 1) == 0
        and modes % (LANES * chips) == 0
        and term_count % LANES == 0
        and DEGREES * run_inputs.shape[1] <= LANES
        and LANES % run_count == 0
        and chips % (LANES // run_count) == 0
        and term_count % run_count == 0
        and run_inputs.shape[1] % (term_count // run_count) == 0
        and slab_modes.shape[0] % LANES == 0
        and cell_map.shape[0] % LANES == 0
    )
    plan = split_by_modes if whole_tiles else split_by_runs
    return plan(
        run_inputs, term_codes, weight_levels, correlations, slab_modes, cell_map
    )


def solution(mesh):
    return jax.shard_map(
        on_device,
        mesh=mesh,
        in_specs=(
            P(("cases", "runs"), None),
            P(),
            P(),
            P(("cases", "runs"), None),
            P("cases", None),
            P(),
        ),
        out_specs=(P(("cases", "runs"), None), P(("cases", "runs"), None)),
        check_vma=False,
    )
```
